32 devices in a mesh: grp: 2 (over y), blk: 4 (over z), head: 4 (over x, core).
Axes of the slice: x: 2, y: 2, z: 4, core: 2. Of those that a mesh axis runs over, the one named last changes fastest.
Arguments:
- query: bfloat16 [2048, 512], P(('grp', 'blk', 'head')), parts along dimension 0, may hold values from -128 to 128
- keys: bfloat16 [2048, 512], P(('grp', 'blk', 'head')), parts along dimension 0, may hold values from -8 to 8
- values: bfloat16 [2048, 512], P(('grp', 'blk', 'head')), parts along dimension 0, may hold values from -6 to 6
- grad_out: bfloat16 [2048, 512], P(('grp', 'blk', 'head')), parts along dimension 0, may hold values from -6 to 6
- valid: int32 [64], P('grp'), parts along dimension 0, may hold values from 16 to 32, as said below
- views: int32 [64], P('grp'), parts along dimension 0, may hold values from 0 to 1
- cross_bias: float32 [8], replicated, may hold values from -2 to 2
Outputs:
- grad_query: float32 [2048, 512], P(('grp', 'blk', 'head')), parts along dimension 0
- grad_keys: float32 [2048, 512], P(('grp', 'blk', 'head')), parts along dimension 0
- grad_values: float32 [2048, 512], P(('grp', 'blk', 'head')), parts along dimension 0
The draws below stay inside these ranges and needn't reach their ends.
There are 2 independent parts, one for each index of `grp`. The reference program is written for one: setup_inputs(seed, part) draws one part's arguments, and reference() takes and returns one part's arrays. A program takes and returns all parts, laid end to end along the dimension named above; an argument that names none is the same for every part. Nothing has to cross between parts.
Inputs may be any that keep to these rules, and one draw needn't show every extreme that they name: `valid`: every frame has at least half of its slots live, and some frame has all 32 live.
All inputs are finite; a program needn't handle non-finite values.
Results may differ from the reference program's by a relative error of at most 0.025.
Values may be sent and summed in bfloat16 or wider, within the bound.
No kernel may reach another device: no remote copies, remote signals or barrier semaphores. Data moves between devices by JAX's collectives and lax.ppermute only.
A program may use at most 64 MiB of HBM per device.

```python
import jax
import jax.numpy as jnp
from jax import lax

HEADS = 8
HD = 64
FRAME = 32
TOK_DEV = 64
FRAMES = 32
TOKENS = 1024
N_HEAD = 4


def paired_fields(key):
    shape = (TOKENS, HEADS * HD)
    key_scale = 128.0 / HD
    key_base = jnp.clip(jax.random.normal(jax.random.fold_in(key, 11), shape, jnp.float32), -4.0, 4.0)
    key_part = key_base * key_scale
    query_part = jnp.clip(jax.random.normal(jax.random.fold_in(key, 12), shape, jnp.float32), -4.0, 4.0)
    return (query_part, key_part)


def draw_query(key, part):
    return paired_fields(key)[0].astype(jnp.bfloat16)


def draw_keys(key, part):
    return paired_fields(key)[1].astype(jnp.bfloat16)


def draw_valid(key, part):
    counts = jax.random.randint(jax.random.fold_in(key, 13), (FRAMES,), FRAME // 2, FRAME + 1, dtype=jnp.int32)
    return jnp.where(jnp.arange(FRAMES) == 0, FRAME, counts).astype(jnp.int32)


def with_ends(drawn, own_key, least, high):
    longest = drawn.shape.index(max(drawn.shape))
    spots = []
    for shift in (0, 1):
        where = [jax.random.randint(jax.random.fold_in(own_key, axis), (), 0, length) for axis, length in enumerate(drawn.shape)]
        where[longest] = (where[longest] + shift) % drawn.shape[longest]
        spots.append(tuple(where))
    return drawn.at[spots[0]].set(least).at[spots[1]].set(high)


def shard_levels(rng, dims, cuts, low, high):
    gain, own = 1.0, jax.random.fold_in(rng, 6)
    for dim, shards_of in cuts:
        steps = jnp.exp(jax.random.uniform(jax.random.fold_in(own, dim), (shards_of,), jnp.float32, low / len(cuts), high / len(cuts)))
        gain = gain * jnp.repeat(steps, dims[dim] // shards_of).reshape([-1 if axis == dim else 1 for axis in range(len(dims))])
    return gain


def scatter_about(stream_key, shape, deviation, limit, shards=(), kind=jnp.bfloat16):
    loudness = shard_levels(stream_key, shape, shards, -0.22, 0.18) if shards else 1.0
    values = jax.random.normal(stream_key, shape, jnp.float32) * deviation * loudness
    return jnp.minimum(jnp.maximum(values, -limit), limit).astype(kind)


def setup_inputs(seed: int = 0, part: int = 0) -> dict:
    key_of = jax.random.split(jax.random.key(seed), 8)
    part_keys = jax.random.split(jax.random.fold_in(key_of[7], part), 8)
    query = draw_query(jax.random.fold_in(jax.random.fold_in(key_of[7], part), 71), part)
    keys = draw_keys(jax.random.fold_in(jax.random.fold_in(key_of[7], part), 71), part)
    values = scatter_about(part_keys[2], (TOKENS, HEADS * HD), 1.0, 6.0, ((0, 16),))
    grad_out = scatter_about(part_keys[3], (TOKENS, HEADS * HD), 1.0, 6.0, ((0, 16),))
    valid = draw_valid(jax.random.fold_in(jax.random.fold_in(key_of[7], part), 71), part)
    views = with_ends(jax.random.randint(part_keys[5], (FRAMES,), 0, 2), jax.random.fold_in(part_keys[5], 1), 0, 1).astype(jnp.int32)
    cross_bias = jnp.clip(jax.random.uniform(key_of[6], (HEADS,), jnp.float32, -2.0, 2.0), -2.0, 2.0)
    return dict(query=query, keys=keys, values=values, grad_out=grad_out, valid=valid, views=views, cross_bias=cross_bias)


neg_large = -1.0e30


def reference(query, keys, values, grad_out, valid, views, cross_bias):
    tokens = jnp.arange(TOKENS, dtype=jnp.int32)
    frames = tokens // FRAME
    live = (tokens % FRAME) < valid[frames]
    labels = views[frames]
    block_len = N_HEAD * TOK_DEV
    count = TOKENS // block_len

    def per_head(head):
        q_head = lax.dynamic_slice_in_dim(query, head * HD, HD, 1)
        k_head = lax.dynamic_slice_in_dim(keys, head * HD, HD, 1)
        v_head = lax.dynamic_slice_in_dim(values, head * HD, HD, 1)
        g_head = lax.dynamic_slice_in_dim(grad_out, head * HD, HD, 1)
        bias = cross_bias[head]

        def one(carry, index):
            dk_acc, dv_acc = carry
            start = (index * block_len).astype(jnp.int32)
            q_part = lax.dynamic_slice_in_dim(q_head, start, block_len, 0)
            g_part = lax.dynamic_slice_in_dim(g_head, start, block_len, 0)
            q_label = lax.dynamic_slice_in_dim(labels, start, block_len, 0)
            cross = (q_label[:, None] != labels[None, :]).astype(jnp.float32)
            logits = jnp.dot(q_part, k_head.T, preferred_element_type=jnp.float32) * 0.125 + bias * cross
            logits = jnp.where(live[None, :], logits, neg_large)
            top = jnp.max(logits, axis=1, keepdims=True)
            total = jnp.sum(jnp.where(live[None, :], jnp.exp(logits - top), 0.0), axis=1, keepdims=True)
            log_norm = top + jnp.log(total)
            weights = jnp.where(live[None, :], jnp.exp(logits - log_norm), 0.0)
            weights_low = weights.astype(jnp.bfloat16)
            outputs = jnp.dot(weights_low, v_head, preferred_element_type=jnp.float32)
            row_delta = jnp.sum(g_part.astype(jnp.float32) * outputs, axis=1, keepdims=True)
            grad_weights = jnp.dot(g_part, v_head.T, preferred_element_type=jnp.float32)
            grad_logits = (0.125 * weights * (grad_weights - row_delta)).astype(jnp.bfloat16)
            dq_part = jnp.dot(grad_logits, k_head, preferred_element_type=jnp.float32)
            dk_acc = dk_acc + jnp.dot(grad_logits.T, q_part, preferred_element_type=jnp.float32)
            dv_acc = dv_acc + jnp.dot(weights_low.T, g_part, preferred_element_type=jnp.float32)
            return (dk_acc, dv_acc), dq_part

        zeros = jnp.zeros((TOKENS, HD), jnp.float32)
        (dk_all, dv_all), dq_all = lax.scan(one, (zeros, zeros), jnp.arange(count, dtype=jnp.int32))
        return dq_all.reshape(TOKENS, HD), dk_all, dv_all

    dq, dk, dv = lax.map(per_head, jnp.arange(HEADS, dtype=jnp.int32))

    def arrange(grads):
        return jnp.transpose(grads, (1, 0, 2)).reshape(TOKENS, HEADS * HD).astype(jnp.float32)

    return (arrange(dq), arrange(dk), arrange(dv))
```

```python
import functools
import math

import jax
import jax.numpy as jnp
from jax import lax
from jax.experimental import pallas as pl
from jax.experimental.pallas import tpu as pltpu
from jax.sharding import PartitionSpec as P

HD = 64
FRAME = 32
PAIR = 2 * HD
TILE = 128
CHUNK = 1024
ROWS16 = 16

SCALE = 0.125
DEAD = -1e30
LOG2E = math.log2(math.e)
LIMIT = 48 * 1024 * 1024

VMEM = pl.BlockSpec(memory_space=pltpu.VMEM)
SMEM = pl.BlockSpec(memory_space=pltpu.SMEM)


def repeat(count, body, written=4):
    if count <= written:
        for index in range(count):
            body(index)
    else:
        pl.loop(0, count)(body)


def side_by_side(left, right, head):
    columns = slice(head * HD, (head + 1) * HD)
    return jnp.concatenate([left[:, columns], right[:, columns]], axis=1)


def pack_kernel(split, q_ref, k_ref, v_ref, g_ref, out_ref):
    rows, width = q_ref.shape
    part = rows // split
    q, k, v, g = q_ref[...], k_ref[...], v_ref[...], g_ref[...]
    for head in range(width // HD):
        kv = side_by_side(k, v, head)
        qg = side_by_side(q, g, head)
        for share in range(split):
            out_ref[head * split + share, :rows] = kv
            out_ref[head * split + share, rows:] = qg[share * part : (share + 1) * part]


def pack(query, keys, values, grad_out, split):
    rows, width = query.shape
    heads, part = width // HD, rows // split
    shape = (heads * split, rows + part, PAIR)
    if part % ROWS16 == 0:
        return pl.pallas_call(
            functools.partial(pack_kernel, split),
            out_shape=jax.ShapeDtypeStruct(shape, query.dtype),
            in_specs=[VMEM] * 4,
            out_specs=VMEM,
            name="pack_heads",
        )(query, keys, values, grad_out)
    joined = [
        jnp.concatenate([a.reshape(rows, heads, HD), b.reshape(rows, heads, HD)], axis=2)
        for a, b in ((keys, values), (query, grad_out))
    ]
    kv, qg = (jnp.swapaxes(x, 0, 1) for x in joined)
    kv = jnp.broadcast_to(kv[:, None], (heads, split, rows, PAIR)).reshape(-1, rows, PAIR)
    return jnp.concatenate([kv, qg.reshape(heads * split, part, PAIR)], axis=1)


def attend_kernel(rows, part, joined, *refs):
    if joined:
        taken, label_ref, valid_ref, views_ref, bias_ref, out_ref = refs[:6]
        kv_from, qg_from, skip = taken, taken, rows
    else:
        kv_from, qg_from, label_ref, valid_ref, views_ref, bias_ref, out_ref, dq_ref = refs[:8]
        skip = 0
    base_ref, turn_ref, both_ref, sum_ref, kv_ref, flip_ref = refs[-6:]
    tokens, tiles = kv_ref.shape[0], label_ref.shape[0]
    chunk = min(CHUNK, tokens)
    chunks = tokens // chunk
    homes = chunk // rows
    bias = bias_ref[0] * LOG2E
    slot = lax.broadcasted_iota(jnp.int32, (FRAME, TILE), 0)

    def frame_terms(frame):
        exo = views_ref[frame] != 0
        live = slot < valid_ref[frame]
        here = pl.ds(frame * FRAME, FRAME)
        base_ref[here, :] = jnp.where(live, jnp.where(exo, bias, 0.0), DEAD)
        turn_ref[here, :] = jnp.where(live, jnp.where(exo, 0.0, bias), DEAD)

    def gather_keys(c):
        at = pl.ds(c * chunk, chunk)
        kv = kv_from[pl.ds(c * homes, homes), :rows, :].reshape(chunk, PAIR)
        kv_ref[at, :] = kv
        flip_ref[:, at] = kv.astype(jnp.float32).T.astype(jnp.bfloat16)

    repeat(tokens // FRAME, frame_terms, 32)
    repeat(chunks, gather_keys)

    low = lax.broadcasted_iota(jnp.int32, (TILE, PAIR), 1) < HD
    contract_last = (((1,), (1,)), ((), ()))
    blocks = TILE // (qg_from.shape[1] - skip)

    def tile(index):
        qg = qg_from[pl.ds(index * blocks, blocks), skip:, :].reshape(TILE, PAIR)
        qg = qg.astype(jnp.float32)
        weights = jnp.concatenate(
            [jnp.where(low, qg, 0.0), jnp.where(low, 0.0, qg)], axis=0
        ).astype(jnp.bfloat16)
        exo = label_ref[pl.ds(index, 1), :] != 0

        def scores(c):
            at = pl.ds(c * chunk, chunk)
            both = lax.dot_general(
                kv_ref[at, :], weights, contract_last, preferred_element_type=jnp.float32
            )
            logits = both[:, :TILE] * (SCALE * LOG2E) + jnp.where(
                exo, turn_ref[at, :], base_ref[at, :]
            )
            both_ref[at, :TILE] = logits
            both_ref[at, TILE:] = both[:, TILE:]
            return jnp.max(logits, axis=0, keepdims=True)

        def sums(c, top):
            at = pl.ds(c * chunk, chunk)
            expo = jnp.exp2(both_ref[at, :TILE] - top)
            both_ref[at, :TILE] = expo
            return (
                jnp.sum(expo, axis=0, keepdims=True),
                jnp.sum(expo * both_ref[at, TILE:], axis=0, keepdims=True),
            )

        def grads(c, inverse, delta):
            at = pl.ds(c * chunk, chunk)
            expo = both_ref[at, :TILE]
            low_weights = (expo * inverse).astype(jnp.bfloat16)
            grad_logits = (
                (expo * (inverse * SCALE)) * (both_ref[at, TILE:] - delta)
            ).astype(jnp.bfloat16)
            added = jnp.dot(
                jnp.concatenate([grad_logits, low_weights], axis=1),
                weights,
                preferred_element_type=jnp.float32,
            )
            if isinstance(index, int) and index == 0:
                sum_ref[at, :] = added
            else:
                sum_ref[at, :] += added
            return jnp.dot(flip_ref[:, at], grad_logits, preferred_element_type=jnp.float32)

        zero = jnp.zeros((1, TILE), jnp.float32)
        if chunks == 1:
            total, mixed = sums(0, scores(0))
            inverse = 1.0 / total
            turned = grads(0, inverse, mixed * inverse)
        else:
            top = lax.fori_loop(0, chunks, lambda c, m: jnp.maximum(m, scores(c)), zero + DEAD)
            total, mixed = lax.fori_loop(
                0, chunks, lambda c, m: jax.tree.map(jnp.add, m, sums(c, top)), (zero, zero)
            )
            inverse = 1.0 / total
            turned = lax.fori_loop(
                0,
                chunks,
                lambda c, m: m + grads(c, inverse, mixed * inverse),
                jnp.zeros((PAIR, TILE), jnp.float32),
            )
        dq = turned.T[:, :HD].astype(jnp.bfloat16)
        if joined:
            for block in range(blocks):
                ours = dq[block * part : (block + 1) * part]
                out_ref[index * blocks + block, rows:, :] = jnp.concatenate(
                    [ours[: part // 2], ours[part // 2 :]], axis=1
                )
        else:
            dq_ref[pl.ds(index * TILE, TILE), :] = dq

    if tiles > 4:
        sum_ref[...] = jnp.zeros_like(sum_ref)
    repeat(tiles, tile)

    def leave(c):
        at = pl.ds(c * chunk, chunk)
        done = sum_ref[at, :].astype(jnp.bfloat16).reshape(homes, rows, PAIR)
        out_ref[pl.ds(c * homes, homes), :rows, :] = done

    repeat(chunks, leave)


def attend(taken, rows, labels, valid, views, bias):
    homes, part = taken.shape[0], taken.shape[1] - rows
    tokens, queries = homes * rows, homes * part
    tiles = queries // TILE
    joined = part % (2 * ROWS16) == 0
    whole = jax.ShapeDtypeStruct((homes, rows + part // 2, PAIR), jnp.bfloat16)
    split = (
        jax.ShapeDtypeStruct((homes, rows, PAIR), jnp.bfloat16),
        jax.ShapeDtypeStruct((queries, HD), jnp.bfloat16),
    )
    sources = (
        (taken,) if joined else (taken[:, :rows], taken[:, rows:].reshape(tiles, TILE, PAIR))
    )
    given = pl.pallas_call(
        functools.partial(attend_kernel, rows, part, joined),
        out_shape=whole if joined else split,
        in_specs=[VMEM] * (len(sources) + 1) + [SMEM] * 3,
        out_specs=VMEM if joined else (VMEM, VMEM),
        scratch_shapes=[
            pltpu.VMEM((tokens, TILE), jnp.float32),
            pltpu.VMEM((tokens, TILE), jnp.float32),
            pltpu.VMEM((tokens, 2 * TILE), jnp.float32),
            pltpu.VMEM((tokens, PAIR), jnp.float32),
            pltpu.VMEM((tokens, PAIR), jnp.bfloat16),
            pltpu.VMEM((PAIR, tokens), jnp.bfloat16),
        ],
        compiler_params=pltpu.CompilerParams(vmem_limit_bytes=LIMIT),
        name="attend_backward",
    )(*sources, labels, valid, views, bias)
    if joined:
        return given
    dkv, dq = given
    dq = dq.reshape(homes, 2, part // 2, HD)
    return jnp.concatenate([dkv, jnp.concatenate([dq[:, 0], dq[:, 1]], axis=2)], axis=1)


def unpack_kernel(split, rows, in_ref, dq_ref, dk_ref, dv_ref):
    part = rows // split
    heads = in_ref.shape[0] // split
    half = part // 2

    def joined(head):
        kv = in_ref[head * split, :rows].astype(jnp.float32)
        for share in range(1, split):
            kv = kv + in_ref[head * split + share, :rows].astype(jnp.float32)
        return kv

    for head in range(0, heads, 2):
        columns = slice(head * HD, (head + 2) * HD)
        one, two = joined(head), joined(head + 1)
        dk_ref[:, columns] = jnp.concatenate([one[:, :HD], two[:, :HD]], axis=1)
        dv_ref[:, columns] = jnp.concatenate([one[:, HD:], two[:, HD:]], axis=1)
        for share in range(split):
            one, two = (
                in_ref[(head + which) * split + share, rows:].astype(jnp.float32)
                for which in (0, 1)
            )
            first = share * part
            dq_ref[first : first + half, columns] = jnp.concatenate(
                [one[:, :HD], two[:, :HD]], axis=1
            )
            dq_ref[first + half : first + part, columns] = jnp.concatenate(
                [one[:, HD:], two[:, HD:]], axis=1
            )


def unpack(given, rows, split):
    heads, part = given.shape[0] // split, rows // split
    shape = jax.ShapeDtypeStruct((rows, heads * HD), jnp.float32)
    if part % (2 * ROWS16) == 0:
        return pl.pallas_call(
            functools.partial(unpack_kernel, split, rows),
            out_shape=(shape,) * 3,
            in_specs=[VMEM],
            out_specs=(VMEM,) * 3,
            name="unpack_heads",
        )(given)
    wide = given.astype(jnp.float32).reshape(heads, split, -1, PAIR)
    kv = jnp.sum(wide[:, :, :rows], axis=1)
    dq = wide[:, :, rows:].reshape(heads, split, part // 2, 2, HD)
    dq = jnp.transpose(dq, (1, 3, 2, 0, 4)).reshape(rows, heads * HD)
    dk, dv = (
        jnp.swapaxes(x, 0, 1).reshape(rows, heads * HD) for x in (kv[..., :HD], kv[..., HD:])
    )
    return dq, dk, dv


def local(query, keys, values, grad_out, valid, views, cross_bias):
    rows, width = query.shape
    axes = ("blk", "head")
    devices = lax.axis_size("blk") * lax.axis_size("head")
    split = devices // (width // HD)
    part = rows // split
    mine = lax.axis_index("blk") * lax.axis_size("head") + lax.axis_index("head")
    head, share = mine // split, mine % split

    packed = pack(query, keys, values, grad_out, split)
    taken = lax.all_to_all(packed, axes, split_axis=0, concat_axis=0, tiled=True)
    first = jnp.arange(devices, dtype=jnp.int32) * rows + share * part
    tokens = first[:, None] + jnp.arange(part, dtype=jnp.int32)[None, :]
    labels = views[tokens // FRAME].reshape(-1, TILE)
    bias = lax.dynamic_slice_in_dim(cross_bias, head, 1)
    given = attend(taken, rows, labels, valid, views, bias)
    back = lax.all_to_all(given, axes, split_axis=0, concat_axis=0, tiled=True)
    return unpack(back, rows, split)


def solution(mesh):
    tokens = P(("grp", "blk", "head"), None)
    return jax.shard_map(
        local,
        mesh=mesh,
        in_specs=(tokens,) * 4 + (P("grp"), P("grp"), P()),
        out_specs=(tokens,) * 3,
        check_vma=False,
    )
```

```python
import functools
import math

import jax
import jax.numpy as jnp
from jax import lax
from jax.experimental import pallas as pl
from jax.experimental.pallas import tpu as pltpu
from jax.sharding import Mesh, PartitionSpec as P

HD = 64
FRAME = 32
PAIR = 2 * HD
TILE = 128
CHUNK = 128

SCALE = 0.125
DEAD = -1e30
LOG2E = math.log2(math.e)
LIMIT = 48 * 1024 * 1024

VMEM = pl.BlockSpec(memory_space=pltpu.VMEM)
SMEM = pl.BlockSpec(memory_space=pltpu.SMEM)


def side_by_side(left, right):
    return jnp.concatenate([left, right], axis=1)


def pack_kernel(q_ref, k_ref, v_ref, g_ref, out_ref):
    rows, width = q_ref.shape
    q, k, v, g = q_ref[...], k_ref[...], v_ref[...], g_ref[...]
    for head in range(width // HD):
        at = slice(head * HD, (head + 1) * HD)
        out_ref[head, :rows] = side_by_side(k[:, at], v[:, at])
        out_ref[head, rows:] = side_by_side(q[:, at], g[:, at])


def pack(query, keys, values, grad_out):
    rows, width = query.shape
    return pl.pallas_call(
        pack_kernel,
        out_shape=jax.ShapeDtypeStruct((width // HD, 2 * rows, PAIR), query.dtype),
        in_specs=[VMEM] * 4,
        out_specs=VMEM,
        name="pack_heads",
    )(query, keys, values, grad_out)


def attend_kernel(shares, *refs):
    blocks = refs[:shares]
    valid_ref, views_ref, bias_ref, out_ref = refs[shares : shares + 4]
    base_ref, turn_ref, kv_ref, flip_ref, expo_ref, gw_ref, sum_ref = refs[shares + 4 :]
    homes, rows = blocks[0].shape[0], blocks[0].shape[1] // 2
    own = homes * rows
    tokens = own * shares
    per_home, per_tile = rows // FRAME, TILE // rows
    tiles, chunks, own_chunks = own // TILE, tokens // CHUNK, own // CHUNK
    mine = lax.axis_index("share")
    bias = bias_ref[lax.axis_index("heads")] * LOG2E
    slot = lax.broadcasted_iota(jnp.int32, (FRAME, TILE), 0)
    lane = lax.broadcasted_iota(jnp.int32, (1, TILE), 1)

    def frame_of(block, home, which):
        share = lax.rem(mine + block, shares)
        return (home * shares + share) * per_home + which

    for block in range(shares):
        kv = blocks[block][:, :rows, :].reshape(own, PAIR)
        here = slice(block * own, (block + 1) * own)
        kv_ref[here, :] = kv
        flip_ref[:, here] = kv.astype(jnp.float32).T.astype(jnp.bfloat16)
        for home in range(homes):
            for which in range(per_home):
                frame = frame_of(block, home, which)
                exo = views_ref[frame] != 0
                live = slot < valid_ref[frame]
                start = block * own + home * rows + which * FRAME
                base_ref[start : start + FRAME, :] = jnp.where(
                    live, jnp.where(exo, bias, 0.0), DEAD
                )
                turn_ref[start : start + FRAME, :] = jnp.where(
                    live, jnp.where(exo, 0.0, bias), DEAD
                )

    sum_ref[...] = jnp.zeros_like(sum_ref)
    low = lax.broadcasted_iota(jnp.int32, (TILE, PAIR), 1) < HD
    contract_last = (((1,), (1,)), ((), ()))

    def tile(block, index):
        qg = blocks[block][pl.ds(index * per_tile, per_tile), rows:, :].reshape(TILE, PAIR)
        qg = qg.astype(jnp.float32)
        weights = jnp.concatenate(
            [jnp.where(low, qg, 0.0), jnp.where(low, 0.0, qg)], axis=0
        ).astype(jnp.bfloat16)
        label = jnp.zeros((1, TILE), jnp.int32)
        for part in range(TILE // FRAME):
            view = views_ref[
                frame_of(block, index * per_tile + part // per_home, part % per_home)
            ]
            label = jnp.where(lane // FRAME == part, view, label)
        exo = label != 0

        both = lax.dot_general(
            kv_ref[...], weights, contract_last, preferred_element_type=jnp.float32
        )
        tops, totals, mixes = [], [], []
        for c in range(chunks):
            at = slice(c * CHUNK, (c + 1) * CHUNK)
            logits = both[at, :TILE] * (SCALE * LOG2E) + jnp.where(
                exo, turn_ref[at, :], base_ref[at, :]
            )
            gw = both[at, TILE:]
            top = jnp.max(logits, axis=0, keepdims=True)
            expo = jnp.exp2(logits - top)
            expo_ref[at, :] = expo
            gw_ref[at, :] = gw
            tops.append(top)
            totals.append(jnp.sum(expo, axis=0, keepdims=True))
            mixes.append(jnp.sum(expo * gw, axis=0, keepdims=True))
        highest = functools.reduce(jnp.maximum, tops)
        factors = [jnp.exp2(top - highest) for top in tops]
        inverse = 1.0 / sum(f * t for f, t in zip(factors, totals))
        delta = sum(f * m for f, m in zip(factors, mixes)) * inverse

        lows, grads = [], []
        for c in range(chunks if block == 0 else own_chunks):
            at = slice(c * CHUNK, (c + 1) * CHUNK)
            factor = factors[c] * inverse
            expo = expo_ref[at, :]
            grads.append(
                ((expo * (factor * SCALE)) * (gw_ref[at, :] - delta)).astype(jnp.bfloat16)
            )
            if c < own_chunks:
                lows.append((expo * factor).astype(jnp.bfloat16))
        sum_ref[...] += jnp.dot(
            side_by_side(
                jnp.concatenate(grads[:own_chunks], axis=0), jnp.concatenate(lows, axis=0)
            ),
            weights,
            preferred_element_type=jnp.float32,
        )
        if block == 0:
            turned = jnp.dot(
                flip_ref[...],
                jnp.concatenate(grads, axis=0),
                preferred_element_type=jnp.float32,
            )
            dq = turned.T[:, :HD].astype(jnp.bfloat16)
            for home in range(per_tile):
                ours = dq[home * rows : (home + 1) * rows]
                out_ref[index * per_tile + home, rows:, :] = side_by_side(
                    ours[: rows // 2], ours[rows // 2 :]
                )

    for block in range(shares):
        pl.loop(0, tiles)(functools.partial(tile, block))
    out_ref[:, :rows, :] = sum_ref[...].astype(jnp.bfloat16).reshape(homes, rows, PAIR)


def attend(blocks, valid, views, cross_bias):
    homes, both, _ = blocks[0].shape
    rows = both // 2
    own = homes * rows
    tokens = own * len(blocks)
    return pl.pallas_call(
        functools.partial(attend_kernel, len(blocks)),
        out_shape=jax.ShapeDtypeStruct((homes, rows + rows // 2, PAIR), jnp.bfloat16),
        in_specs=[VMEM] * len(blocks) + [SMEM] * 3,
        out_specs=VMEM,
        scratch_shapes=[
            pltpu.VMEM((tokens, TILE), jnp.float32),
            pltpu.VMEM((tokens, TILE), jnp.float32),
            pltpu.VMEM((tokens, PAIR), jnp.bfloat16),
            pltpu.VMEM((PAIR, tokens), jnp.bfloat16),
            pltpu.VMEM((tokens, TILE), jnp.float32),
            pltpu.VMEM((tokens, TILE), jnp.float32),
            pltpu.VMEM((own, PAIR), jnp.float32),
        ],
        compiler_params=pltpu.CompilerParams(vmem_limit_bytes=LIMIT),
        name="attend_backward",
    )(*blocks, valid, views, cross_bias)


def unpack_kernel(in_ref, dq_ref, dk_ref, dv_ref):
    rows = dq_ref.shape[0]
    half = rows // 2
    for head in range(0, in_ref.shape[0], 2):
        columns = slice(head * HD, (head + 2) * HD)
        one, two = (in_ref[head + which].astype(jnp.float32) for which in (0, 1))
        left = side_by_side(one[:, :HD], two[:, :HD])
        right = side_by_side(one[:, HD:], two[:, HD:])
        dk_ref[:, columns] = left[:rows]
        dv_ref[:, columns] = right[:rows]
        dq_ref[:half, columns] = left[rows:]
        dq_ref[half:, columns] = right[rows:]


def unpack(given, rows):
    shape = jax.ShapeDtypeStruct((rows, given.shape[0] * HD), jnp.float32)
    return pl.pallas_call(
        unpack_kernel,
        out_shape=(shape,) * 3,
        in_specs=[VMEM],
        out_specs=(VMEM,) * 3,
        name="unpack_heads",
    )(given)


def local(query, keys, values, grad_out, valid, views, cross_bias):
    swap = functools.partial(
        lax.all_to_all, axis_name="heads", split_axis=0, concat_axis=0, tiled=True
    )
    shares = lax.axis_size("share")
    mine = swap(pack(query, keys, values, grad_out))
    blocks = [mine] + [
        lax.ppermute(mine, "share", [((i + k) % shares, i) for i in range(shares)])
        for k in range(1, shares)
    ]
    return unpack(swap(attend(blocks, valid, views, cross_bias)), query.shape[0])


def solution(mesh):
    groups = mesh.shape["grp"]
    members = mesh.shape["blk"] * mesh.shape["head"]

    def run(query, keys, values, grad_out, valid, views, cross_bias):
        heads = query.shape[1] // HD
        layout = Mesh(
            mesh.devices.reshape(groups, heads, members // heads), ("grp", "heads", "share")
        )
        tokens = P(("grp", "heads", "share"), None)
        return jax.shard_map(
            local,
            mesh=layout,
            in_specs=(tokens,) * 4 + (P("grp"), P("grp"), P()),
            out_specs=(tokens,) * 3,
            check_vma=False,
        )(query, keys, values, grad_out, valid, views, cross_bias)

    return run
```

```python
import functools
import math

import jax
import jax.numpy as jnp
from jax import lax
from jax.experimental import pallas as pl
from jax.experimental.pallas import tpu as pltpu
from jax.sharding import Mesh, PartitionSpec as P

HD = 64
FRAME = 32
PAIR = 2 * HD
TILE = 128
CHUNK = 128

SCALE = 0.125
DEAD = -1e30
LOG2E = math.log2(math.e)
LIMIT = 48 * 1024 * 1024

VMEM = pl.BlockSpec(memory_space=pltpu.VMEM)
SMEM = pl.BlockSpec(memory_space=pltpu.SMEM)


def side_by_side(left, right):
    return jnp.concatenate([left, right], axis=1)


def pack_kernel(q_ref, k_ref, v_ref, g_ref, *out_refs):
    rows = q_ref.shape[0]
    me = lax.axis_index("heads")
    odd = lax.rem(me, 2) == 1
    for pair in range(len(out_refs) // 2):
        first = lax.bitwise_xor(lax.div(me, 2), pair) * PAIR
        at = pl.ds(pl.multiple_of(first, PAIR), PAIR)
        for into, (left, right) in (
            (slice(0, rows), (k_ref[:, at], v_ref[:, at])),
            (slice(rows, 2 * rows), (q_ref[:, at], g_ref[:, at])),
        ):
            even_one = side_by_side(left[:, :HD], right[:, :HD])
            odd_one = side_by_side(left[:, HD:], right[:, HD:])
            out_refs[2 * pair][into, :] = jnp.where(odd, odd_one, even_one)
            out_refs[2 * pair + 1][into, :] = jnp.where(odd, even_one, odd_one)


def pack(query, keys, values, grad_out):
    rows, width = query.shape
    heads = width // HD
    return pl.pallas_call(
        pack_kernel,
        out_shape=(jax.ShapeDtypeStruct((2 * rows, PAIR), query.dtype),) * heads,
        in_specs=[VMEM] * 4,
        out_specs=(VMEM,) * heads,
        name="pack_heads",
    )(query, keys, values, grad_out)


def attend_kernel(homes, shares, *refs):
    own_refs, other_refs = refs[:homes], refs[homes : homes + shares - 1]
    refs = refs[homes + shares - 1 :]
    valid_ref, views_ref, bias_ref = refs[:3]
    out_refs = refs[3 : 3 + homes]
    base_ref, turn_ref, kv_ref, qg_ref, flip_ref, sum_ref, dq_ref = refs[3 + homes :]
    rows = own_refs[0].shape[0] // 2
    own = homes * rows
    tokens = own * shares
    per_home, per_tile = rows // FRAME, TILE // rows
    tiles, chunks, own_chunks = own // TILE, tokens // CHUNK, own // CHUNK
    me, mine = lax.axis_index("heads"), lax.axis_index("share")
    bias = bias_ref[me] * LOG2E
    slot = lax.broadcasted_iota(jnp.int32, (FRAME, TILE), 0)
    lane = lax.broadcasted_iota(jnp.int32, (1, TILE), 1)

    def frame_of(block, home, which):
        share = lax.rem(mine + block, shares)
        return (lax.bitwise_xor(me, home) * shares + share) * per_home + which

    for block in range(shares):
        start = block * own
        for home in range(homes):
            if block:
                both = other_refs[block - 1][home]
            else:
                both = own_refs[home][...]
            here = slice(start + home * rows, start + (home + 1) * rows)
            kv_ref[here, :] = both[:rows]
            qg_ref[here, :] = both[rows:]
            for which in range(per_home):
                frame = frame_of(block, home, which)
                exo = views_ref[frame] != 0
                live = slot < valid_ref[frame]
                here = slice(
                    start + home * rows + which * FRAME,
                    start + home * rows + (which + 1) * FRAME,
                )
                base_ref[here, :] = jnp.where(live, jnp.where(exo, bias, 0.0), DEAD)
                turn_ref[here, :] = jnp.where(live, jnp.where(exo, 0.0, bias), DEAD)
        here = slice(start, start + own)
        flip_ref[:, here] = kv_ref[here, :].astype(jnp.float32).T.astype(jnp.bfloat16)

    sum_ref[...] = jnp.zeros_like(sum_ref)
    low = lax.broadcasted_iota(jnp.int32, (TILE, PAIR), 1) < HD
    contract_last = (((1,), (1,)), ((), ()))

    def tile(ours, index):
        here = pl.ds(pl.multiple_of(index * TILE, TILE), TILE)
        qg = qg_ref[here, :].astype(jnp.float32)
        weights = jnp.concatenate(
            [jnp.where(low, qg, 0.0), jnp.where(low, 0.0, qg)], axis=0
        ).astype(jnp.bfloat16)
        block, first = lax.div(index, tiles), lax.rem(index, tiles) * per_tile
        label = jnp.zeros((1, TILE), jnp.int32)
        for part in range(TILE // FRAME):
            view = views_ref[frame_of(block, first + part // per_home, part % per_home)]
            label = jnp.where(lane // FRAME == part, view, label)
        exo = label != 0

        both = lax.dot_general(
            kv_ref[...], weights, contract_last, preferred_element_type=jnp.float32
        )
        tops, totals, mixes, expos = [], [], [], []
        for c in range(chunks):
            at = slice(c * CHUNK, (c + 1) * CHUNK)
            logits = both[at, :TILE] * (SCALE * LOG2E) + jnp.where(
                exo, turn_ref[at, :], base_ref[at, :]
            )
            top = jnp.max(logits, axis=0, keepdims=True)
            expo = jnp.exp2(logits - top)
            expos.append(expo)
            tops.append(top)
            totals.append(jnp.sum(expo, axis=0, keepdims=True))
            mixes.append(jnp.sum(expo * both[at, TILE:], axis=0, keepdims=True))
        highest = functools.reduce(jnp.maximum, tops)
        factors = [jnp.exp2(top - highest) for top in tops]
        inverse = 1.0 / sum(f * t for f, t in zip(factors, totals))
        delta = sum(f * m for f, m in zip(factors, mixes)) * inverse

        lows, grads = [], []
        for c in range(chunks if ours else own_chunks):
            at = slice(c * CHUNK, (c + 1) * CHUNK)
            weight = expos[c] * (factors[c] * inverse)
            grads.append(
                ((weight * SCALE) * (both[at, TILE:] - delta)).astype(jnp.bfloat16)
            )
            if c < own_chunks:
                lows.append(weight.astype(jnp.bfloat16))
        sum_ref[...] += jnp.dot(
            side_by_side(
                jnp.concatenate(grads[:own_chunks], axis=0), jnp.concatenate(lows, axis=0)
            ),
            weights,
            preferred_element_type=jnp.float32,
        )
        if ours:
            turned = jnp.dot(
                flip_ref[...],
                jnp.concatenate(grads, axis=0),
                preferred_element_type=jnp.float32,
            )
            dq_ref[here, :] = turned.T

    pl.loop(0, tiles, unroll=2)(functools.partial(tile, True))
    pl.loop(tiles, tiles * shares, unroll=2)(functools.partial(tile, False))
    for home, out_ref in enumerate(out_refs):
        start, half = home * rows, rows // 2
        out_ref[:rows, :] = sum_ref[start : start + rows, :].astype(jnp.bfloat16)
        out_ref[rows:, :] = side_by_side(
            dq_ref[start : start + half, :HD], dq_ref[start + half : start + rows, :HD]
        ).astype(jnp.bfloat16)


def attend(own_blocks, other_blocks, valid, views, cross_bias):
    homes, shares = len(own_blocks), len(other_blocks) + 1
    rows = own_blocks[0].shape[0] // 2
    own = homes * rows
    tokens = own * shares
    return pl.pallas_call(
        functools.partial(attend_kernel, homes, shares),
        out_shape=(jax.ShapeDtypeStruct((rows + rows // 2, PAIR), jnp.bfloat16),) * homes,
        in_specs=[VMEM] * (homes + shares - 1) + [SMEM] * 3,
        out_specs=(VMEM,) * homes,
        scratch_shapes=[
            pltpu.VMEM((tokens, TILE), jnp.float32),
            pltpu.VMEM((tokens, TILE), jnp.float32),
            pltpu.VMEM((tokens, PAIR), jnp.bfloat16),
            pltpu.VMEM((tokens, PAIR), jnp.bfloat16),
            pltpu.VMEM((PAIR, tokens), jnp.bfloat16),
            pltpu.VMEM((own, PAIR), jnp.float32),
            pltpu.VMEM((own, PAIR), jnp.float32),
        ],
        compiler_params=pltpu.CompilerParams(vmem_limit_bytes=LIMIT),
        name="attend_backward",
    )(*own_blocks, *other_blocks, valid, views, cross_bias)


def unpack_kernel(heads, *refs):
    in_refs, (dq_ref, dk_ref, dv_ref) = refs[:heads], refs[heads:]
    rows = dq_ref.shape[0]
    half = rows // 2
    me = lax.axis_index("heads")
    odd = lax.rem(me, 2) == 1
    for pair in range(heads // 2):
        first = lax.bitwise_xor(lax.div(me, 2), pair) * PAIR
        at = pl.ds(pl.multiple_of(first, PAIR), PAIR)
        near, far = (in_refs[2 * pair + which][...].astype(jnp.float32) for which in (0, 1))
        one, two = jnp.where(odd, far, near), jnp.where(odd, near, far)
        left = side_by_side(one[:, :HD], two[:, :HD])
        right = side_by_side(one[:, HD:], two[:, HD:])
        dk_ref[:, at] = left[:rows]
        dv_ref[:, at] = right[:rows]
        dq_ref[:half, at] = left[rows:]
        dq_ref[half:, at] = right[rows:]


def unpack(given, rows):
    shape = jax.ShapeDtypeStruct((rows, len(given) * HD), jnp.float32)
    return pl.pallas_call(
        functools.partial(unpack_kernel, len(given)),
        out_shape=(shape,) * 3,
        in_specs=[VMEM] * len(given),
        out_specs=(VMEM,) * 3,
        name="unpack_heads",
    )(*given)


def trade(arrays):
    heads = len(arrays)
    return [arrays[0]] + [
        lax.ppermute(arrays[k], "heads", [(i, i ^ k) for i in range(heads)])
        for k in range(1, heads)
    ]


def local(query, keys, values, grad_out, valid, views, cross_bias):
    shares = lax.axis_size("share")
    mine = trade(pack(query, keys, values, grad_out))
    stacked = jnp.stack(mine)
    others = [
        lax.ppermute(stacked, "share", [((i + k) % shares, i) for i in range(shares)])
        for k in range(1, shares)
    ]
    return unpack(trade(attend(mine, others, valid, views, cross_bias)), query.shape[0])


def solution(mesh):
    groups = mesh.shape["grp"]
    members = mesh.shape["blk"] * mesh.shape["head"]

    def run(query, keys, values, grad_out, valid, views, cross_bias):
        heads = query.shape[1] // HD
        layout = Mesh(
            mesh.devices.reshape(groups, heads, members // heads), ("grp", "heads", "share")
        )
        tokens = P(("grp", "heads", "share"), None)
        return jax.shard_map(
            local,
            mesh=layout,
            in_specs=(tokens,) * 4 + (P("grp"), P("grp"), P()),
            out_specs=(tokens,) * 3,
            check_vma=False,
        )(query, keys, values, grad_out, valid, views, cross_bias)

    return run
```

```python
import functools
import math

import jax
import jax.numpy as jnp
from jax import lax
from jax.experimental import pallas as pl
from jax.experimental.pallas import tpu as pltpu
from jax.sharding import Mesh, PartitionSpec as P

HD = 64
FRAME = 32
PAIR = 2 * HD
TILE = 128
CHUNK = 128
UNROLL = 2

SCALE = 0.125
DEAD = -1e30
LOG2E = math.log2(math.e)
LIMIT = 48 * 1024 * 1024

VMEM = pl.BlockSpec(memory_space=pltpu.VMEM)
SMEM = pl.BlockSpec(memory_space=pltpu.SMEM)


def side_by_side(left, right):
    return jnp.concatenate([left, right], axis=1)


def pack_kernel(q_ref, k_ref, v_ref, g_ref, out_ref):
    rows, width = q_ref.shape
    q, k, v, g = q_ref[...], k_ref[...], v_ref[...], g_ref[...]
    for head in range(width // HD):
        at = slice(head * HD, (head + 1) * HD)
        out_ref[head, :rows] = side_by_side(k[:, at], v[:, at])
        out_ref[head, rows:] = side_by_side(q[:, at], g[:, at])


def pack(query, keys, values, grad_out):
    rows, width = query.shape
    return pl.pallas_call(
        pack_kernel,
        out_shape=pltpu.VMEM((width // HD, 2 * rows, PAIR), query.dtype),
        in_specs=[VMEM] * 4,
        out_specs=VMEM,
        name="pack_heads",
    )(query, keys, values, grad_out)


def attend_kernel(shares, *refs):
    blocks = refs[:shares]
    valid_ref, views_ref, bias_ref, out_ref = refs[shares : shares + 4]
    base_ref, turn_ref, kv_ref, qg_ref, flip_ref, sum_ref, dq_ref = refs[shares + 4 :]
    homes, rows = blocks[0].shape[0], blocks[0].shape[1] // 2
    own = homes * rows
    tokens = own * shares
    per_home, per_tile = rows // FRAME, TILE // rows
    tiles, chunks, own_chunks = own // TILE, tokens // CHUNK, own // CHUNK
    mine = lax.axis_index("share")
    bias = bias_ref[lax.axis_index("heads")] * LOG2E
    slot = lax.broadcasted_iota(jnp.int32, (FRAME, TILE), 0)
    lane = lax.broadcasted_iota(jnp.int32, (1, TILE), 1)

    def frame_of(block, home, which):
        share = lax.rem(mine + block, shares)
        return (home * shares + share) * per_home + which

    for block in range(shares):
        start = block * own
        for home in range(homes):
            here = slice(start + home * rows, start + (home + 1) * rows)
            kv_ref[here, :] = blocks[block][home, :rows]
            qg_ref[here, :] = blocks[block][home, rows:]
            for which in range(per_home):
                frame = frame_of(block, home, which)
                exo = views_ref[frame] != 0
                live = slot < valid_ref[frame]
                here = slice(
                    start + home * rows + which * FRAME,
                    start + home * rows + (which + 1) * FRAME,
                )
                base_ref[here, :] = jnp.where(live, jnp.where(exo, bias, 0.0), DEAD)
                turn_ref[here, :] = jnp.where(live, jnp.where(exo, 0.0, bias), DEAD)
        here = slice(start, start + own)
        flip_ref[:, here] = kv_ref[here, :].astype(jnp.float32).T.astype(jnp.bfloat16)

    sum_ref[...] = jnp.zeros_like(sum_ref)
    low = lax.broadcasted_iota(jnp.int32, (TILE, PAIR), 1) < HD
    contract_last = (((1,), (1,)), ((), ()))

    def tile(ours, index):
        here = pl.ds(pl.multiple_of(index * TILE, TILE), TILE)
        qg = qg_ref[here, :].astype(jnp.float32)
        weights = jnp.concatenate(
            [jnp.where(low, qg, 0.0), jnp.where(low, 0.0, qg)], axis=0
        ).astype(jnp.bfloat16)
        block, first = lax.div(index, tiles), lax.rem(index, tiles) * per_tile
        label = jnp.zeros((1, TILE), jnp.int32)
        for part in range(TILE // FRAME):
            view = views_ref[frame_of(block, first + part // per_home, part % per_home)]
            label = jnp.where(lane // FRAME == part, view, label)
        exo = label != 0

        both = lax.dot_general(
            kv_ref[...], weights, contract_last, preferred_element_type=jnp.float32
        )
        tops, totals, mixes, expos = [], [], [], []
        for c in range(chunks):
            at = slice(c * CHUNK, (c + 1) * CHUNK)
            logits = both[at, :TILE] * (SCALE * LOG2E) + jnp.where(
                exo, turn_ref[at, :], base_ref[at, :]
            )
            top = jnp.max(logits, axis=0, keepdims=True)
            expo = jnp.exp2(logits - top)
            expos.append(expo)
            tops.append(top)
            totals.append(jnp.sum(expo, axis=0, keepdims=True))
            mixes.append(jnp.sum(expo * both[at, TILE:], axis=0, keepdims=True))
        highest = functools.reduce(jnp.maximum, tops)
        factors = [jnp.exp2(top - highest) for top in tops]
        inverse = 1.0 / sum(f * t for f, t in zip(factors, totals))
        delta = sum(f * m for f, m in zip(factors, mixes)) * inverse

        lows, grads = [], []
        for c in range(chunks if ours else own_chunks):
            at = slice(c * CHUNK, (c + 1) * CHUNK)
            weight = expos[c] * (factors[c] * inverse)
            grads.append(
                ((weight * SCALE) * (both[at, TILE:] - delta)).astype(jnp.bfloat16)
            )
            if c < own_chunks:
                lows.append(weight.astype(jnp.bfloat16))
        sum_ref[...] += jnp.dot(
            side_by_side(
                jnp.concatenate(grads[:own_chunks], axis=0), jnp.concatenate(lows, axis=0)
            ),
            weights,
            preferred_element_type=jnp.float32,
        )
        if ours:
            turned = jnp.dot(
                flip_ref[...],
                jnp.concatenate(grads, axis=0),
                preferred_element_type=jnp.float32,
            )
            dq_ref[here, :] = turned.T

    pl.loop(0, tiles, unroll=UNROLL)(functools.partial(tile, True))
    pl.loop(tiles, tiles * shares, unroll=UNROLL)(functools.partial(tile, False))
    out_ref[:, :rows, :] = sum_ref[...].astype(jnp.bfloat16).reshape(homes, rows, PAIR)
    for home in range(homes):
        start, half = home * rows, rows // 2
        out_ref[home, rows:, :] = side_by_side(
            dq_ref[start : start + half, :HD], dq_ref[start + half : start + rows, :HD]
        ).astype(jnp.bfloat16)


def attend(blocks, valid, views, cross_bias):
    homes, both, _ = blocks[0].shape
    rows = both // 2
    own = homes * rows
    tokens = own * len(blocks)
    return pl.pallas_call(
        functools.partial(attend_kernel, len(blocks)),
        out_shape=jax.ShapeDtypeStruct((homes, rows + rows // 2, PAIR), jnp.bfloat16),
        in_specs=[VMEM] * len(blocks) + [SMEM] * 3,
        out_specs=VMEM,
        scratch_shapes=[
            pltpu.VMEM((tokens, TILE), jnp.float32),
            pltpu.VMEM((tokens, TILE), jnp.float32),
            pltpu.VMEM((tokens, PAIR), jnp.bfloat16),
            pltpu.VMEM((tokens, PAIR), jnp.bfloat16),
            pltpu.VMEM((PAIR, tokens), jnp.bfloat16),
            pltpu.VMEM((own, PAIR), jnp.float32),
            pltpu.VMEM((own, PAIR), jnp.float32),
        ],
        compiler_params=pltpu.CompilerParams(vmem_limit_bytes=LIMIT),
        name="attend_backward",
    )(*blocks, valid, views, cross_bias)


def unpack_kernel(in_ref, dq_ref, dk_ref, dv_ref):
    rows = dq_ref.shape[0]
    half = rows // 2
    for head in range(0, in_ref.shape[0], 2):
        columns = slice(head * HD, (head + 2) * HD)
        one, two = (in_ref[head + which].astype(jnp.float32) for which in (0, 1))
        left = side_by_side(one[:, :HD], two[:, :HD])
        right = side_by_side(one[:, HD:], two[:, HD:])
        dk_ref[:, columns] = left[:rows]
        dv_ref[:, columns] = right[:rows]
        dq_ref[:half, columns] = left[rows:]
        dq_ref[half:, columns] = right[rows:]


def unpack(given, rows):
    shape = jax.ShapeDtypeStruct((rows, given.shape[0] * HD), jnp.float32)
    return pl.pallas_call(
        unpack_kernel,
        out_shape=(shape,) * 3,
        in_specs=[VMEM],
        out_specs=(VMEM,) * 3,
        name="unpack_heads",
    )(pltpu.with_memory_space_constraint(given, pltpu.VMEM))


def local(query, keys, values, grad_out, valid, views, cross_bias):
    swap = functools.partial(
        lax.all_to_all, axis_name="heads", split_axis=0, concat_axis=0, tiled=True
    )
    shares = lax.axis_size("share")
    mine = swap(pack(query, keys, values, grad_out))
    blocks = [mine] + [
        lax.ppermute(mine, "share", [((i + k) % shares, i) for i in range(shares)])
        for k in range(1, shares)
    ]
    return unpack(swap(attend(blocks, valid, views, cross_bias)), query.shape[0])


def solution(mesh):
    groups = mesh.shape["grp"]
    members = mesh.shape["blk"] * mesh.shape["head"]

    def run(query, keys, values, grad_out, valid, views, cross_bias):
        heads = query.shape[1] // HD
        layout = Mesh(
            mesh.devices.reshape(groups, heads, members // heads), ("grp", "heads", "share")
        )
        tokens = P(("grp", "heads", "share"), None)
        return jax.shard_map(
            local,
            mesh=layout,
            in_specs=(tokens,) * 4 + (P("grp"), P("grp"), P()),
            out_specs=(tokens,) * 3,
            check_vma=False,
        )(query, keys, values, grad_out, valid, views, cross_bias)

    return run
```

```python
import functools
import math

import jax
import jax.numpy as jnp
from jax import lax
from jax.experimental import pallas as pl
from jax.experimental.pallas import tpu as pltpu
from jax.sharding import Mesh, PartitionSpec as P

HD = 64
FRAME = 32
PAIR = 2 * HD
TILE = 128
CHUNK = 128
UNROLL = 4

SCALE = 0.125
DEAD = -1e30
LOG2E = math.log2(math.e)
LIMIT = 48 * 1024 * 1024

VMEM = pl.BlockSpec(memory_space=pltpu.VMEM)
SMEM = pl.BlockSpec(memory_space=pltpu.SMEM)


def side_by_side(left, right):
    return jnp.concatenate([left, right], axis=1)


def pack_kernel(q_ref, k_ref, v_ref, g_ref, out_ref):
    rows, width = q_ref.shape
    q, k, v, g = q_ref[...], k_ref[...], v_ref[...], g_ref[...]
    for head in range(width // HD):
        at = slice(head * HD, (head + 1) * HD)
        out_ref[head, :rows] = side_by_side(k[:, at], v[:, at])
        out_ref[head, rows:] = side_by_side(q[:, at], g[:, at])


def pack(query, keys, values, grad_out):
    rows, width = query.shape
    return pl.pallas_call(
        pack_kernel,
        out_shape=pltpu.VMEM((width // HD, 2 * rows, PAIR), query.dtype),
        in_specs=[VMEM] * 4,
        out_specs=VMEM,
        name="pack_heads",
    )(query, keys, values, grad_out)


def attend_kernel(shares, *refs):
    blocks = refs[:shares]
    valid_ref, views_ref, bias_ref, out_ref = refs[shares : shares + 4]
    base_ref, turn_ref, kv_ref, qg_ref, flip_ref, sum_ref, dq_ref = refs[shares + 4 :]
    homes, rows = blocks[0].shape[0], blocks[0].shape[1] // 2
    own = homes * rows
    tokens = own * shares
    per_home, per_tile = rows // FRAME, TILE // rows
    tiles, chunks, own_chunks = own // TILE, tokens // CHUNK, own // CHUNK
    mine = lax.axis_index("share")
    bias = bias_ref[lax.axis_index("heads")] * LOG2E
    slot = lax.broadcasted_iota(jnp.int32, (FRAME, TILE), 0)
    lane = lax.broadcasted_iota(jnp.int32, (1, TILE), 1)

    def frame_of(block, home, which):
        share = lax.rem(mine + block, shares)
        return (home * shares + share) * per_home + which

    for block in range(shares):
        start = block * own
        for home in range(homes):
            here = slice(start + home * rows, start + (home + 1) * rows)
            kv_ref[here, :] = blocks[block][home, :rows]
            qg_ref[here, :] = blocks[block][home, rows:]
            for which in range(per_home):
                frame = frame_of(block, home, which)
                exo = views_ref[frame] != 0
                live = slot < valid_ref[frame]
                here = slice(
                    start + home * rows + which * FRAME,
                    start + home * rows + (which + 1) * FRAME,
                )
                base_ref[here, :] = jnp.where(live, jnp.where(exo, bias, 0.0), DEAD)
                turn_ref[here, :] = jnp.where(live, jnp.where(exo, 0.0, bias), DEAD)
        here = slice(start, start + own)
        flip_ref[:, here] = kv_ref[here, :].astype(jnp.float32).T.astype(jnp.bfloat16)

    sum_ref[...] = jnp.zeros_like(sum_ref)
    low = lax.broadcasted_iota(jnp.int32, (TILE, PAIR), 1) < HD
    contract_last = (((1,), (1,)), ((), ()))

    def tile(ours, index):
        here = pl.ds(pl.multiple_of(index * TILE, TILE), TILE)
        qg = qg_ref[here, :].astype(jnp.float32)
        weights = jnp.concatenate(
            [jnp.where(low, qg, 0.0), jnp.where(low, 0.0, qg)], axis=0
        ).astype(jnp.bfloat16)
        block, first = lax.div(index, tiles), lax.rem(index, tiles) * per_tile
        label = jnp.zeros((1, TILE), jnp.int32)
        for part in range(TILE // FRAME):
            view = views_ref[frame_of(block, first + part // per_home, part % per_home)]
            label = jnp.where(lane // FRAME == part, view, label)
        exo = label != 0

        both = lax.dot_general(
            kv_ref[...], weights, contract_last, preferred_element_type=jnp.float32
        )
        tops, totals, mixes, expos = [], [], [], []
        for c in range(chunks):
            at = slice(c * CHUNK, (c + 1) * CHUNK)
            logits = both[at, :TILE] * (SCALE * LOG2E) + jnp.where(
                exo, turn_ref[at, :], base_ref[at, :]
            )
            top = jnp.max(logits, axis=0, keepdims=True)
            expo = jnp.exp2(logits - top)
            expos.append(expo)
            tops.append(top)
            totals.append(jnp.sum(expo, axis=0, keepdims=True))
            mixes.append(jnp.sum(expo * both[at, TILE:], axis=0, keepdims=True))
        highest = functools.reduce(jnp.maximum, tops)
        factors = [jnp.exp2(top - highest) for top in tops]
        inverse = 1.0 / sum(f * t for f, t in zip(factors, totals))
        delta = sum(f * m for f, m in zip(factors, mixes)) * inverse

        lows, grads = [], []
        for c in range(chunks if ours else own_chunks):
            at = slice(c * CHUNK, (c + 1) * CHUNK)
            weight = expos[c] * (factors[c] * inverse)
            grads.append(
                ((weight * SCALE) * (both[at, TILE:] - delta)).astype(jnp.bfloat16)
            )
            if c < own_chunks:
                lows.append(weight.astype(jnp.bfloat16))
        sum_ref[...] += jnp.dot(
            side_by_side(
                jnp.concatenate(grads[:own_chunks], axis=0), jnp.concatenate(lows, axis=0)
            ),
            weights,
            preferred_element_type=jnp.float32,
        )
        if ours:
            turned = jnp.dot(
                flip_ref[...],
                jnp.concatenate(grads, axis=0),
                preferred_element_type=jnp.float32,
            )
            dq_ref[here, :] = turned.T

    pl.loop(0, tiles, unroll=UNROLL)(functools.partial(tile, True))
    pl.loop(tiles, tiles * shares, unroll=UNROLL)(functools.partial(tile, False))
    out_ref[:, :rows, :] = sum_ref[...].astype(jnp.bfloat16).reshape(homes, rows, PAIR)
    for home in range(homes):
        start, half = home * rows, rows // 2
        out_ref[home, rows:, :] = side_by_side(
            dq_ref[start : start + half, :HD], dq_ref[start + half : start + rows, :HD]
        ).astype(jnp.bfloat16)


def attend(blocks, valid, views, cross_bias):
    homes, both, _ = blocks[0].shape
    rows = both // 2
    own = homes * rows
    tokens = own * len(blocks)
    return pl.pallas_call(
        functools.partial(attend_kernel, len(blocks)),
        out_shape=jax.ShapeDtypeStruct((homes, rows + rows // 2, PAIR), jnp.bfloat16),
        in_specs=[VMEM] * len(blocks) + [SMEM] * 3,
        out_specs=VMEM,
        scratch_shapes=[
            pltpu.VMEM((tokens, TILE), jnp.float32),
            pltpu.VMEM((tokens, TILE), jnp.float32),
            pltpu.VMEM((tokens, PAIR), jnp.bfloat16),
            pltpu.VMEM((tokens, PAIR), jnp.bfloat16),
            pltpu.VMEM((PAIR, tokens), jnp.bfloat16),
            pltpu.VMEM((own, PAIR), jnp.float32),
            pltpu.VMEM((own, PAIR), jnp.float32),
        ],
        compiler_params=pltpu.CompilerParams(vmem_limit_bytes=LIMIT),
        name="attend_backward",
    )(*blocks, valid, views, cross_bias)


def unpack_kernel(in_ref, dq_ref, dk_ref, dv_ref):
    rows = dq_ref.shape[0]
    half = rows // 2
    for head in range(0, in_ref.shape[0], 2):
        columns = slice(head * HD, (head + 2) * HD)
        one, two = (in_ref[head + which].astype(jnp.float32) for which in (0, 1))
        left = side_by_side(one[:, :HD], two[:, :HD])
        right = side_by_side(one[:, HD:], two[:, HD:])
        dk_ref[:, columns] = left[:rows]
        dv_ref[:, columns] = right[:rows]
        dq_ref[:half, columns] = left[rows:]
        dq_ref[half:, columns] = right[rows:]


def unpack(given, rows):
    shape = jax.ShapeDtypeStruct((rows, given.shape[0] * HD), jnp.float32)
    return pl.pallas_call(
        unpack_kernel,
        out_shape=(shape,) * 3,
        in_specs=[VMEM],
        out_specs=(VMEM,) * 3,
        name="unpack_heads",
    )(pltpu.with_memory_space_constraint(given, pltpu.VMEM))


def local(query, keys, values, grad_out, valid, views, cross_bias):
    swap = functools.partial(
        lax.all_to_all, axis_name="heads", split_axis=0, concat_axis=0, tiled=True
    )
    shares = lax.axis_size("share")
    mine = swap(pack(query, keys, values, grad_out))
    blocks = [mine] + [
        lax.ppermute(mine, "share", [((i + k) % shares, i) for i in range(shares)])
        for k in range(1, shares)
    ]
    return unpack(swap(attend(blocks, valid, views, cross_bias)), query.shape[0])


def solution(mesh):
    groups = mesh.shape["grp"]
    members = mesh.shape["blk"] * mesh.shape["head"]

    def run(query, keys, values, grad_out, valid, views, cross_bias):
        heads = query.shape[1] // HD
        layout = Mesh(
            mesh.devices.reshape(groups, heads, members // heads), ("grp", "heads", "share")
        )
        tokens = P(("grp", "heads", "share"), None)
        return jax.shard_map(
            local,
            mesh=layout,
            in_specs=(tokens,) * 4 + (P("grp"), P("grp"), P()),
            out_specs=(tokens,) * 3,
            check_vma=False,
        )(query, keys, values, grad_out, valid, views, cross_bias)

    return run
```

```python
import functools
import math

import jax
import jax.numpy as jnp
from jax import lax
from jax.experimental import pallas as pl
from jax.experimental.pallas import tpu as pltpu
from jax.sharding import Mesh, PartitionSpec as P

HD = 64
FRAME = 32
PAIR = 2 * HD
TILE = 128
CHUNK = 128
UNROLL = 4

SCALE = 0.125
DEAD = -1e30
LOG2E = math.log2(math.e)
LIMIT = 48 * 1024 * 1024

VMEM = pl.BlockSpec(memory_space=pltpu.VMEM)
SMEM = pl.BlockSpec(memory_space=pltpu.SMEM)


def side_by_side(left, right):
    return jnp.concatenate([left, right], axis=1)


def pack_kernel(q_ref, k_ref, v_ref, g_ref, out_ref):
    rows, width = q_ref.shape
    q, k, v, g = q_ref[...], k_ref[...], v_ref[...], g_ref[...]
    for head in range(width // HD):
        at = slice(head * HD, (head + 1) * HD)
        out_ref[head, :rows] = side_by_side(k[:, at], v[:, at])
        out_ref[head, rows:] = side_by_side(q[:, at], g[:, at])


def pack(query, keys, values, grad_out):
    rows, width = query.shape
    return pl.pallas_call(
        pack_kernel,
        out_shape=pltpu.VMEM((width // HD, 2 * rows, PAIR), query.dtype),
        in_specs=[VMEM] * 4,
        out_specs=VMEM,
        name="pack_heads",
    )(query, keys, values, grad_out)


def attend_kernel(shares, *refs):
    blocks = refs[:shares]
    valid_ref, views_ref, bias_ref, out_ref = refs[shares : shares + 4]
    kv_ref, qg_ref, flip_ref, sum_ref, dq_ref = refs[shares + 4 :]
    homes, rows = blocks[0].shape[0], blocks[0].shape[1] // 2
    own = homes * rows
    tokens = own * shares
    per_home, per_tile = rows // FRAME, TILE // rows
    tiles, chunks, own_chunks = own // TILE, tokens // CHUNK, own // CHUNK
    mine = lax.axis_index("share")
    unroll = UNROLL if shares <= 2 else 1
    slot = lax.broadcasted_iota(jnp.int32, (FRAME, PAIR), 0)
    lane = lax.broadcasted_iota(jnp.int32, (1, PAIR), 1)

    bias = jnp.full((1, PAIR), bias_ref[lax.axis_index("heads")] / SCALE, jnp.float32)
    high = bias.astype(jnp.bfloat16).astype(jnp.float32)
    middle = (bias - high).astype(jnp.bfloat16).astype(jnp.float32)
    part = lax.rem(lane, 3)
    parts = jnp.where(part == 0, high, jnp.where(part == 1, middle, bias - high - middle))
    dead = jnp.where(lane == 6, DEAD / SCALE, 0.0)
    of_exo_query = jnp.where(lane < 3, parts, dead)
    of_ego_query = jnp.where((lane >= 3) & (lane < 6), parts, dead)

    def frame_of(block, home, which):
        share = lax.rem(mine + block, shares)
        return (home * shares + share) * per_home + which

    for block in range(shares):
        start = block * own
        for home in range(homes):
            here = slice(start + home * rows, start + (home + 1) * rows)
            kv_ref[here, :PAIR] = blocks[block][home, :rows]
            qg_ref[here, :] = blocks[block][home, rows:]
            for which in range(per_home):
                frame = frame_of(block, home, which)
                first = jnp.where(views_ref[frame] != 0, 3, 0)
                marks = jnp.where((lane >= first) & (lane < first + 3), 1.0, 0.0)
                gone = jnp.where(slot < valid_ref[frame], 0.0, 1.0)
                here = slice(
                    start + home * rows + which * FRAME,
                    start + home * rows + (which + 1) * FRAME,
                )
                kv_ref[here, PAIR:] = jnp.where(lane == 6, gone, marks).astype(jnp.bfloat16)
        here = slice(start, start + own)
        flip_ref[:, here] = kv_ref[here, :PAIR].astype(jnp.float32).T.astype(jnp.bfloat16)

    sum_ref[...] = jnp.zeros_like(sum_ref)
    low = lax.broadcasted_iota(jnp.int32, (TILE, PAIR), 1) < HD
    contract_last = (((1,), (1,)), ((), ()))

    def tile(ours, index):
        here = pl.ds(pl.multiple_of(index * TILE, TILE), TILE)
        qg = qg_ref[here, :].astype(jnp.float32)
        weights = jnp.concatenate(
            [jnp.where(low, qg, 0.0), jnp.where(low, 0.0, qg)], axis=0
        ).astype(jnp.bfloat16)
        block, first = lax.div(index, tiles), lax.rem(index, tiles) * per_tile
        marks = []
        for part in range(TILE // FRAME):
            view = views_ref[frame_of(block, first + part // per_home, part % per_home)]
            row = jnp.where(view != 0, of_exo_query, of_ego_query)
            marks.append(jnp.broadcast_to(row, (FRAME, PAIR)))
        marks.append(jnp.zeros((TILE, PAIR), jnp.float32))
        marks = jnp.concatenate(marks, axis=0).astype(jnp.bfloat16)

        both = lax.dot_general(
            kv_ref[...],
            side_by_side(weights, marks),
            contract_last,
            preferred_element_type=jnp.float32,
        )
        tops, totals, mixes, expos = [], [], [], []
        for c in range(chunks):
            at = slice(c * CHUNK, (c + 1) * CHUNK)
            top = jnp.max(both[at, :TILE], axis=0, keepdims=True)
            expo = jnp.exp2((both[at, :TILE] - top) * (SCALE * LOG2E))
            expos.append(expo)
            tops.append(top)
            totals.append(jnp.sum(expo, axis=0, keepdims=True))
            mixes.append(jnp.sum(expo * both[at, TILE:], axis=0, keepdims=True))
        highest = functools.reduce(jnp.maximum, tops)
        factors = [jnp.exp2((top - highest) * (SCALE * LOG2E)) for top in tops]
        inverse = 1.0 / sum(f * t for f, t in zip(factors, totals))
        delta = sum(f * m for f, m in zip(factors, mixes)) * inverse

        lows, grads = [], []
        for c in range(chunks if ours else own_chunks):
            at = slice(c * CHUNK, (c + 1) * CHUNK)
            weight = expos[c] * (factors[c] * inverse)
            grads.append(
                ((weight * SCALE) * (both[at, TILE:] - delta)).astype(jnp.bfloat16)
            )
            if c < own_chunks:
                lows.append(weight.astype(jnp.bfloat16))
        sum_ref[...] += jnp.dot(
            side_by_side(
                jnp.concatenate(grads[:own_chunks], axis=0), jnp.concatenate(lows, axis=0)
            ),
            weights,
            preferred_element_type=jnp.float32,
        )
        if ours:
            turned = jnp.dot(
                flip_ref[...],
                jnp.concatenate(grads, axis=0),
                preferred_element_type=jnp.float32,
            )
            dq_ref[here, :] = turned.T

    pl.loop(0, tiles, unroll=unroll)(functools.partial(tile, True))
    pl.loop(tiles, tiles * shares, unroll=unroll)(functools.partial(tile, False))
    out_ref[:, :rows, :] = sum_ref[...].astype(jnp.bfloat16).reshape(homes, rows, PAIR)
    for home in range(homes):
        start, half = home * rows, rows // 2
        out_ref[home, rows:, :] = side_by_side(
            dq_ref[start : start + half, :HD], dq_ref[start + half : start + rows, :HD]
        ).astype(jnp.bfloat16)


def attend(blocks, valid, views, cross_bias):
    homes, both, _ = blocks[0].shape
    rows = both // 2
    own = homes * rows
    tokens = own * len(blocks)
    return pl.pallas_call(
        functools.partial(attend_kernel, len(blocks)),
        out_shape=jax.ShapeDtypeStruct((homes, rows + rows // 2, PAIR), jnp.bfloat16),
        in_specs=[VMEM] * len(blocks) + [SMEM] * 3,
        out_specs=VMEM,
        scratch_shapes=[
            pltpu.VMEM((tokens, 2 * PAIR), jnp.bfloat16),
            pltpu.VMEM((tokens, PAIR), jnp.bfloat16),
            pltpu.VMEM((PAIR, tokens), jnp.bfloat16),
            pltpu.VMEM((own, PAIR), jnp.float32),
            pltpu.VMEM((own, PAIR), jnp.float32),
        ],
        compiler_params=pltpu.CompilerParams(vmem_limit_bytes=LIMIT),
        name="attend_backward",
    )(*blocks, valid, views, cross_bias)


def unpack_kernel(in_ref, dq_ref, dk_ref, dv_ref):
    rows = dq_ref.shape[0]
    half = rows // 2
    for head in range(0, in_ref.shape[0], 2):
        columns = slice(head * HD, (head + 2) * HD)
        one, two = (in_ref[head + which].astype(jnp.float32) for which in (0, 1))
        left = side_by_side(one[:, :HD], two[:, :HD])
        right = side_by_side(one[:, HD:], two[:, HD:])
        dk_ref[:, columns] = left[:rows]
        dv_ref[:, columns] = right[:rows]
        dq_ref[:half, columns] = left[rows:]
        dq_ref[half:, columns] = right[rows:]


def unpack(given, rows):
    shape = jax.ShapeDtypeStruct((rows, given.shape[0] * HD), jnp.float32)
    return pl.pallas_call(
        unpack_kernel,
        out_shape=(shape,) * 3,
        in_specs=[VMEM],
        out_specs=(VMEM,) * 3,
        name="unpack_heads",
    )(pltpu.with_memory_space_constraint(given, pltpu.VMEM))


def local(query, keys, values, grad_out, valid, views, cross_bias):
    swap = functools.partial(
        lax.all_to_all, axis_name="heads", split_axis=0, concat_axis=0, tiled=True
    )
    shares = lax.axis_size("share")
    mine = swap(pack(query, keys, values, grad_out))
    blocks = [mine] + [
        lax.ppermute(mine, "share", [((i + k) % shares, i) for i in range(shares)])
        for k in range(1, shares)
    ]
    return unpack(swap(attend(blocks, valid, views, cross_bias)), query.shape[0])


def solution(mesh):
    groups = mesh.shape["grp"]
    members = mesh.shape["blk"] * mesh.shape["head"]

    def run(query, keys, values, grad_out, valid, views, cross_bias):
        heads = query.shape[1] // HD
        layout = Mesh(
            mesh.devices.reshape(groups, heads, members // heads), ("grp", "heads", "share")
        )
        tokens = P(("grp", "heads", "share"), None)
        return jax.shard_map(
            local,
            mesh=layout,
            in_specs=(tokens,) * 4 + (P("grp"), P("grp"), P()),
            out_specs=(tokens,) * 3,
            check_vma=False,
        )(query, keys, values, grad_out, valid, views, cross_bias)

    return run
```

```python
import functools
import math

import jax
import jax.numpy as jnp
from jax import lax
from jax.experimental import pallas as pl
from jax.experimental.pallas import tpu as pltpu
from jax.sharding import Mesh, PartitionSpec as P

HD = 64
FRAME = 32
PAIR = 2 * HD
TILE = 128
CHUNK = 128
UNROLL = 4

SCALE = 0.125
DEAD = -1e30
LOG2E = math.log2(math.e)
LIMIT = 48 * 1024 * 1024

VMEM = pl.BlockSpec(memory_space=pltpu.VMEM)
SMEM = pl.BlockSpec(memory_space=pltpu.SMEM)


def side_by_side(left, right):
    return jnp.concatenate([left, right], axis=1)


def pack_kernel(q_ref, k_ref, v_ref, g_ref, out_ref):
    rows, width = q_ref.shape
    q, k, v, g = q_ref[...], k_ref[...], v_ref[...], g_ref[...]
    for head in range(width // HD):
        at = slice(head * HD, (head + 1) * HD)
        out_ref[head, :rows] = side_by_side(k[:, at], v[:, at])
        out_ref[head, rows:] = side_by_side(q[:, at], g[:, at])


def pack(query, keys, values, grad_out):
    rows, width = query.shape
    return pl.pallas_call(
        pack_kernel,
        out_shape=pltpu.VMEM((width // HD, 2 * rows, PAIR), query.dtype),
        in_specs=[VMEM] * 4,
        out_specs=VMEM,
        name="pack_heads",
    )(query, keys, values, grad_out)


def frame_of(homes, shares, per_home, block, home, which):
    share = lax.rem(lax.axis_index("share") + block, shares)
    return (home * shares + share) * per_home + which


def query_weights(qg):
    qg = qg.astype(jnp.float32)
    low = lax.broadcasted_iota(jnp.int32, qg.shape, 1) < HD
    return jnp.concatenate(
        [jnp.where(low, qg, 0.0), jnp.where(low, 0.0, qg)], axis=0
    ).astype(jnp.bfloat16)


def products(keys, weights):
    return lax.dot_general(
        keys, weights, (((1,), (1,)), ((), ())), preferred_element_type=jnp.float32
    )


def exponentials(raw, gw):
    top = jnp.max(raw, axis=0, keepdims=True)
    expo = jnp.exp2((raw - top) * (SCALE * LOG2E))
    total = jnp.sum(expo, axis=0, keepdims=True)
    return expo, (top, total, jnp.sum(expo * gw, axis=0, keepdims=True))


def chunk_of(c):
    return slice(c * CHUNK, (c + 1) * CHUNK)


def begin_kernel(shares, mine_ref, valid_ref, views_ref, bias_ref, key_mark_ref,
                 query_mark_ref, weights_ref, flip_ref, expo_ref, gw_ref, stat_ref, keys_ref):
    homes, rows = mine_ref.shape[0], mine_ref.shape[1] // 2
    own = homes * rows
    per_home, per_tile, tiles = rows // FRAME, TILE // rows, own // TILE
    unroll = UNROLL if shares <= 2 else 1
    slot = lax.broadcasted_iota(jnp.int32, (FRAME, PAIR), 0)
    lane = lax.broadcasted_iota(jnp.int32, (1, PAIR), 1)

    bias = jnp.full((1, PAIR), bias_ref[lax.axis_index("heads")] / SCALE, jnp.float32)
    high = bias.astype(jnp.bfloat16).astype(jnp.float32)
    middle = (bias - high).astype(jnp.bfloat16).astype(jnp.float32)
    part = lax.rem(lane, 3)
    parts = jnp.where(part == 0, high, jnp.where(part == 1, middle, bias - high - middle))
    dead = jnp.where(lane == 6, DEAD / SCALE, 0.0)
    of_exo_query = jnp.where(lane < 3, parts, dead)
    of_ego_query = jnp.where((lane >= 3) & (lane < 6), parts, dead)

    for block in range(shares):
        for home in range(homes):
            for which in range(per_home):
                frame = frame_of(homes, shares, per_home, block, home, which)
                start = block * own + home * rows + which * FRAME
                here = slice(start, start + FRAME)
                exo = views_ref[frame] != 0
                first = jnp.where(exo, 3, 0)
                marks = jnp.where((lane >= first) & (lane < first + 3), 1.0, 0.0)
                gone = jnp.where(slot < valid_ref[frame], 0.0, 1.0)
                key_mark_ref[here, :] = jnp.where(lane == 6, gone, marks).astype(jnp.bfloat16)
                query_mark_ref[here, :] = jnp.broadcast_to(
                    jnp.where(exo, of_exo_query, of_ego_query), (FRAME, PAIR)
                ).astype(jnp.bfloat16)

    kv = mine_ref[:, :rows, :].reshape(own, PAIR)
    flip_ref[...] = kv.astype(jnp.float32).T.astype(jnp.bfloat16)
    keys_ref[:, :PAIR] = kv
    keys_ref[:, PAIR:] = key_mark_ref[:own, :]

    def tile(index):
        qg = mine_ref[pl.ds(index * per_tile, per_tile), rows:, :].reshape(TILE, PAIR)
        here = pl.ds(pl.multiple_of(index * TILE, TILE), TILE)
        marks = query_mark_ref[here, :]
        weights = side_by_side(
            query_weights(qg), jnp.concatenate([marks, jnp.zeros_like(marks)], axis=0)
        )
        weights_ref[index] = weights
        both = products(keys_ref[...], weights)
        gw_ref[index] = both[:, TILE:]
        for c in range(own // CHUNK):
            at = chunk_of(c)
            expo, stats = exponentials(both[at, :TILE], both[at, TILE:])
            expo_ref[index, at, :] = expo
            for which, stat in enumerate(stats):
                stat_ref[index, which, c : c + 1, :] = stat

    pl.loop(0, tiles, unroll=unroll)(tile)


def finish_kernel(shares, *refs):
    blocks, refs = refs[:shares], refs[shares:]
    key_mark_ref, query_mark_ref, weights_ref, own_flip_ref = refs[:4]
    expo_ref, gw_ref, stat_ref, out_ref, keys_ref, qg_ref, flip_ref, sum_ref, dq_ref = refs[4:]
    homes, rows = blocks[0].shape[0], blocks[0].shape[1] // 2
    own = homes * rows
    tokens = own * shares
    tiles, chunks, own_chunks = own // TILE, tokens // CHUNK, own // CHUNK
    unroll = UNROLL if shares <= 2 else 1

    keys_ref[:, PAIR:] = key_mark_ref[...]
    for block in range(shares):
        here = slice(block * own, (block + 1) * own)
        kv = blocks[block][:, :rows, :].reshape(own, PAIR)
        keys_ref[here, :PAIR] = kv
        if block:
            there = slice((block - 1) * own, block * own)
            flip_ref[:, there] = kv.astype(jnp.float32).T.astype(jnp.bfloat16)
            qg_ref[there, :] = blocks[block][:, rows:, :].reshape(own, PAIR)
    sum_ref[...] = jnp.zeros_like(sum_ref)

    def tile(ours, index):
        here = pl.ds(pl.multiple_of(index * TILE, TILE), TILE)
        if ours:
            weights = weights_ref[index]
            given = own_chunks
            if chunks > own_chunks:
                both = products(keys_ref[own:, :], weights)
        else:
            marks = query_mark_ref[pl.ds(pl.multiple_of(own + index * TILE, TILE), TILE), :]
            weights = side_by_side(
                query_weights(qg_ref[here, :]),
                jnp.concatenate([marks, jnp.zeros_like(marks)], axis=0),
            )
            given = 0
            both = products(keys_ref[...], weights)
        expos, gws, stats = [], [], []
        for c in range(chunks):
            if c < given:
                expos.append(expo_ref[index, chunk_of(c), :])
                gws.append(gw_ref[index, chunk_of(c), :])
                stats.append([stat_ref[index, which, c : c + 1, :] for which in range(3)])
            else:
                at = chunk_of(c - given)
                gws.append(both[at, TILE:])
                expo, stat = exponentials(both[at, :TILE], gws[-1])
                expos.append(expo)
                stats.append(stat)
        highest = functools.reduce(jnp.maximum, [top for top, _, _ in stats])
        factors = [jnp.exp2((top - highest) * (SCALE * LOG2E)) for top, _, _ in stats]
        inverse = 1.0 / sum(f * total for f, (_, total, _) in zip(factors, stats))
        delta = sum(f * mix for f, (_, _, mix) in zip(factors, stats)) * inverse

        lows, grads = [], []
        for c in range(chunks if ours else own_chunks):
            weight = expos[c] * (factors[c] * inverse)
            grads.append(((weight * SCALE) * (gws[c] - delta)).astype(jnp.bfloat16))
            if c < own_chunks:
                lows.append(weight.astype(jnp.bfloat16))
        own_grads = jnp.concatenate(grads[:own_chunks], axis=0)
        sum_ref[...] += jnp.dot(
            side_by_side(own_grads, jnp.concatenate(lows, axis=0)),
            weights[:, :PAIR],
            preferred_element_type=jnp.float32,
        )
        if ours:
            turned = jnp.dot(own_flip_ref[...], own_grads, preferred_element_type=jnp.float32)
            if chunks > own_chunks:
                turned += jnp.dot(
                    flip_ref[...],
                    jnp.concatenate(grads[own_chunks:], axis=0),
                    preferred_element_type=jnp.float32,
                )
            dq_ref[here, :] = turned.T

    pl.loop(0, tiles, unroll=unroll)(functools.partial(tile, True))
    pl.loop(0, tiles * (shares - 1), unroll=unroll)(functools.partial(tile, False))
    out_ref[:, :rows, :] = sum_ref[...].astype(jnp.bfloat16).reshape(homes, rows, PAIR)
    for home in range(homes):
        start, half = home * rows, rows // 2
        out_ref[home, rows:, :] = side_by_side(
            dq_ref[start : start + half, :HD], dq_ref[start + half : start + rows, :HD]
        ).astype(jnp.bfloat16)


def attend(mine, others, valid, views, cross_bias):
    shares = len(others) + 1
    homes, both, _ = mine.shape
    rows = both // 2
    own = homes * rows
    tokens, tiles = own * shares, own // TILE
    begun = pl.pallas_call(
        functools.partial(begin_kernel, shares),
        out_shape=(
            pltpu.VMEM((tokens, PAIR), jnp.bfloat16),
            pltpu.VMEM((tokens, PAIR), jnp.bfloat16),
            pltpu.VMEM((tiles, 2 * TILE, 2 * PAIR), jnp.bfloat16),
            pltpu.VMEM((PAIR, own), jnp.bfloat16),
            pltpu.VMEM((tiles, own, TILE), jnp.float32),
            pltpu.VMEM((tiles, own, TILE), jnp.float32),
            pltpu.VMEM((tiles, 3, own // CHUNK, TILE), jnp.float32),
        ),
        in_specs=[VMEM] + [SMEM] * 3,
        out_specs=(VMEM,) * 7,
        scratch_shapes=[pltpu.VMEM((own, 2 * PAIR), jnp.bfloat16)],
        compiler_params=pltpu.CompilerParams(vmem_limit_bytes=LIMIT),
        cost_estimate=pl.CostEstimate(
            flops=8 * own * own * PAIR, bytes_accessed=8 * own * own, transcendentals=own * own
        ),
        name="attend_begin",
    )(mine, valid, views, cross_bias)
    return pl.pallas_call(
        functools.partial(finish_kernel, shares),
        out_shape=pltpu.VMEM((homes, rows + rows // 2, PAIR), jnp.bfloat16),
        in_specs=[VMEM] * (shares + 7),
        out_specs=VMEM,
        scratch_shapes=[
            pltpu.VMEM((tokens, 2 * PAIR), jnp.bfloat16),
            pltpu.VMEM((max(tokens - own, TILE), PAIR), jnp.bfloat16),
            pltpu.VMEM((PAIR, max(tokens - own, TILE)), jnp.bfloat16),
            pltpu.VMEM((own, PAIR), jnp.float32),
            pltpu.VMEM((own, PAIR), jnp.float32),
        ],
        compiler_params=pltpu.CompilerParams(vmem_limit_bytes=LIMIT),
        name="attend_finish",
    )(mine, *others, *begun)


def unpack_kernel(in_ref, dq_ref, dk_ref, dv_ref):
    rows = dq_ref.shape[0]
    half = rows // 2
    for head in range(0, in_ref.shape[0], 2):
        columns = slice(head * HD, (head + 2) * HD)
        one, two = (in_ref[head + which].astype(jnp.float32) for which in (0, 1))
        left = side_by_side(one[:, :HD], two[:, :HD])
        right = side_by_side(one[:, HD:], two[:, HD:])
        dk_ref[:, columns] = left[:rows]
        dv_ref[:, columns] = right[:rows]
        dq_ref[:half, columns] = left[rows:]
        dq_ref[half:, columns] = right[rows:]


def unpack(given, rows):
    shape = jax.ShapeDtypeStruct((rows, given.shape[0] * HD), jnp.float32)
    return pl.pallas_call(
        unpack_kernel,
        out_shape=(shape,) * 3,
        in_specs=[VMEM],
        out_specs=(VMEM,) * 3,
        name="unpack_heads",
    )(pltpu.with_memory_space_constraint(given, pltpu.VMEM))


def local(query, keys, values, grad_out, valid, views, cross_bias):
    swap = functools.partial(
        lax.all_to_all, axis_name="heads", split_axis=0, concat_axis=0, tiled=True
    )
    shares = lax.axis_size("share")
    mine = swap(pack(query, keys, values, grad_out))
    others = [
        lax.ppermute(mine, "share", [((i + k) % shares, i) for i in range(shares)])
        for k in range(1, shares)
    ]
    given = attend(mine, others, valid, views, cross_bias)
    return unpack(swap(given), query.shape[0])


def solution(mesh):
    groups = mesh.shape["grp"]
    members = mesh.shape["blk"] * mesh.shape["head"]

    def run(query, keys, values, grad_out, valid, views, cross_bias):
        heads = query.shape[1] // HD
        layout = Mesh(
            mesh.devices.reshape(groups, heads, members // heads), ("grp", "heads", "share")
        )
        tokens = P(("grp", "heads", "share"), None)
        return jax.shard_map(
            local,
            mesh=layout,
            in_specs=(tokens,) * 4 + (P("grp"), P("grp"), P()),
            out_specs=(tokens,) * 3,
            check_vma=False,
        )(query, keys, values, grad_out, valid, views, cross_bias)

    return run
```

```python
import functools
import math

import jax
import jax.numpy as jnp
from jax import lax
from jax.experimental import pallas as pl
from jax.experimental.pallas import tpu as pltpu
from jax.sharding import Mesh, PartitionSpec as P

HD = 64
FRAME = 32
PAIR = 2 * HD
TILE = 256
CHUNK = 64
UNROLL = 2

SCALE = 0.125
DEAD = -1e30
LOG2E = math.log2(math.e)
LIMIT = 48 * 1024 * 1024

VMEM = pl.BlockSpec(memory_space=pltpu.VMEM)
SMEM = pl.BlockSpec(memory_space=pltpu.SMEM)


def side_by_side(left, right):
    return jnp.concatenate([left, right], axis=1)


def pack_kernel(q_ref, k_ref, v_ref, g_ref, out_ref):
    rows, width = q_ref.shape
    q, k, v, g = q_ref[...], k_ref[...], v_ref[...], g_ref[...]
    for head in range(width // HD):
        at = slice(head * HD, (head + 1) * HD)
        out_ref[head, :rows] = side_by_side(k[:, at], v[:, at])
        out_ref[head, rows:] = side_by_side(q[:, at], g[:, at])


def pack(query, keys, values, grad_out):
    rows, width = query.shape
    return pl.pallas_call(
        pack_kernel,
        out_shape=pltpu.VMEM((width // HD, 2 * rows, PAIR), query.dtype),
        in_specs=[VMEM] * 4,
        out_specs=VMEM,
        name="pack_heads",
    )(query, keys, values, grad_out)


def attend_kernel(shares, *refs):
    blocks = refs[:shares]
    valid_ref, views_ref, bias_ref, out_ref = refs[shares : shares + 4]
    kv_ref, qg_ref, flip_ref, sum_ref, dq_ref = refs[shares + 4 :]
    homes, rows = blocks[0].shape[0], blocks[0].shape[1] // 2
    own = homes * rows
    tokens = own * shares
    per_home, per_tile = rows // FRAME, TILE // rows
    tiles, chunks, own_chunks = own // TILE, tokens // CHUNK, own // CHUNK
    mine = lax.axis_index("share")
    unroll = UNROLL if shares <= 2 else 1
    slot = lax.broadcasted_iota(jnp.int32, (FRAME, PAIR), 0)
    lane = lax.broadcasted_iota(jnp.int32, (1, PAIR), 1)

    bias = jnp.full((1, PAIR), bias_ref[lax.axis_index("heads")] / SCALE, jnp.float32)
    high = bias.astype(jnp.bfloat16).astype(jnp.float32)
    middle = (bias - high).astype(jnp.bfloat16).astype(jnp.float32)
    part = lax.rem(lane, 3)
    parts = jnp.where(part == 0, high, jnp.where(part == 1, middle, bias - high - middle))
    dead = jnp.where(lane == 6, DEAD / SCALE, 0.0)
    of_exo_query = jnp.where(lane < 3, parts, dead)
    of_ego_query = jnp.where((lane >= 3) & (lane < 6), parts, dead)

    def frame_of(block, home, which):
        share = lax.rem(mine + block, shares)
        return (home * shares + share) * per_home + which

    for block in range(shares):
        start = block * own
        for home in range(homes):
            here = slice(start + home * rows, start + (home + 1) * rows)
            kv_ref[here, :PAIR] = blocks[block][home, :rows]
            qg_ref[here, :] = blocks[block][home, rows:]
            for which in range(per_home):
                frame = frame_of(block, home, which)
                first = jnp.where(views_ref[frame] != 0, 3, 0)
                marks = jnp.where((lane >= first) & (lane < first + 3), 1.0, 0.0)
                gone = jnp.where(slot < valid_ref[frame], 0.0, 1.0)
                here = slice(
                    start + home * rows + which * FRAME,
                    start + home * rows + (which + 1) * FRAME,
                )
                kv_ref[here, PAIR:] = jnp.where(lane == 6, gone, marks).astype(jnp.bfloat16)
        here = slice(start, start + own)
        flip_ref[:, here] = kv_ref[here, :PAIR].astype(jnp.float32).T.astype(jnp.bfloat16)

    sum_ref[...] = jnp.zeros_like(sum_ref)
    low = lax.broadcasted_iota(jnp.int32, (TILE, PAIR), 1) < HD
    contract_last = (((1,), (1,)), ((), ()))

    def tile(ours, index):
        here = pl.ds(pl.multiple_of(index * TILE, TILE), TILE)
        qg = qg_ref[here, :].astype(jnp.float32)
        weights = jnp.concatenate(
            [jnp.where(low, qg, 0.0), jnp.where(low, 0.0, qg)], axis=0
        ).astype(jnp.bfloat16)
        block, first = lax.div(index, tiles), lax.rem(index, tiles) * per_tile
        marks = []
        for part in range(TILE // FRAME):
            view = views_ref[frame_of(block, first + part // per_home, part % per_home)]
            row = jnp.where(view != 0, of_exo_query, of_ego_query)
            marks.append(jnp.broadcast_to(row, (FRAME, PAIR)))
        marks.append(jnp.zeros((TILE, PAIR), jnp.float32))
        marks = jnp.concatenate(marks, axis=0).astype(jnp.bfloat16)

        both = lax.dot_general(
            kv_ref[...],
            side_by_side(weights, marks),
            contract_last,
            preferred_element_type=jnp.float32,
        )
        tops, totals, mixes, expos = [], [], [], []
        for c in range(chunks):
            at = slice(c * CHUNK, (c + 1) * CHUNK)
            top = jnp.max(both[at, :TILE], axis=0, keepdims=True)
            expo = jnp.exp2((both[at, :TILE] - top) * (SCALE * LOG2E))
            expos.append(expo)
            tops.append(top)
            totals.append(jnp.sum(expo, axis=0, keepdims=True))
            mixes.append(jnp.sum(expo * both[at, TILE:], axis=0, keepdims=True))
        highest = functools.reduce(jnp.maximum, tops)
        factors = [jnp.exp2((top - highest) * (SCALE * LOG2E)) for top in tops]
        inverse = 1.0 / sum(f * t for f, t in zip(factors, totals))
        delta = sum(f * m for f, m in zip(factors, mixes)) * inverse

        lows, grads = [], []
        for c in range(chunks if ours else own_chunks):
            at = slice(c * CHUNK, (c + 1) * CHUNK)
            weight = expos[c] * (factors[c] * inverse)
            grads.append(
                ((weight * SCALE) * (both[at, TILE:] - delta)).astype(jnp.bfloat16)
            )
            if c < own_chunks:
                lows.append(weight.astype(jnp.bfloat16))
        sum_ref[...] += jnp.dot(
            side_by_side(
                jnp.concatenate(grads[:own_chunks], axis=0), jnp.concatenate(lows, axis=0)
            ),
            weights,
            preferred_element_type=jnp.float32,
        )
        if ours:
            turned = jnp.dot(
                flip_ref[...],
                jnp.concatenate(grads, axis=0),
                preferred_element_type=jnp.float32,
            )
            dq_ref[here, :] = turned.T

    pl.loop(0, tiles, unroll=unroll)(functools.partial(tile, True))
    pl.loop(tiles, tiles * shares, unroll=unroll)(functools.partial(tile, False))
    out_ref[:, :rows, :] = sum_ref[...].astype(jnp.bfloat16).reshape(homes, rows, PAIR)
    for home in range(homes):
        start, half = home * rows, rows // 2
        out_ref[home, rows:, :] = side_by_side(
            dq_ref[start : start + half, :HD], dq_ref[start + half : start + rows, :HD]
        ).astype(jnp.bfloat16)


def attend(blocks, valid, views, cross_bias):
    homes, both, _ = blocks[0].shape
    rows = both // 2
    own = homes * rows
    tokens = own * len(blocks)
    return pl.pallas_call(
        functools.partial(attend_kernel, len(blocks)),
        out_shape=jax.ShapeDtypeStruct((homes, rows + rows // 2, PAIR), jnp.bfloat16),
        in_specs=[VMEM] * len(blocks) + [SMEM] * 3,
        out_specs=VMEM,
        scratch_shapes=[
            pltpu.VMEM((tokens, 2 * PAIR), jnp.bfloat16),
            pltpu.VMEM((tokens, PAIR), jnp.bfloat16),
            pltpu.VMEM((PAIR, tokens), jnp.bfloat16),
            pltpu.VMEM((own, PAIR), jnp.float32),
            pltpu.VMEM((own, PAIR), jnp.float32),
        ],
        compiler_params=pltpu.CompilerParams(vmem_limit_bytes=LIMIT),
        name="attend_backward",
    )(*blocks, valid, views, cross_bias)


def unpack_kernel(in_ref, dq_ref, dk_ref, dv_ref):
    rows = dq_ref.shape[0]
    half = rows // 2
    for head in range(0, in_ref.shape[0], 2):
        columns = slice(head * HD, (head + 2) * HD)
        one, two = (in_ref[head + which].astype(jnp.float32) for which in (0, 1))
        left = side_by_side(one[:, :HD], two[:, :HD])
        right = side_by_side(one[:, HD:], two[:, HD:])
        dk_ref[:, columns] = left[:rows]
        dv_ref[:, columns] = right[:rows]
        dq_ref[:half, columns] = left[rows:]
        dq_ref[half:, columns] = right[rows:]


def unpack(given, rows):
    shape = jax.ShapeDtypeStruct((rows, given.shape[0] * HD), jnp.float32)
    return pl.pallas_call(
        unpack_kernel,
        out_shape=(shape,) * 3,
        in_specs=[VMEM],
        out_specs=(VMEM,) * 3,
        name="unpack_heads",
    )(pltpu.with_memory_space_constraint(given, pltpu.VMEM))


def local(query, keys, values, grad_out, valid, views, cross_bias):
    swap = functools.partial(
        lax.all_to_all, axis_name="heads", split_axis=0, concat_axis=0, tiled=True
    )
    shares = lax.axis_size("share")
    mine = swap(pack(query, keys, values, grad_out))
    blocks = [mine] + [
        lax.ppermute(mine, "share", [((i + k) % shares, i) for i in range(shares)])
        for k in range(1, shares)
    ]
    return unpack(swap(attend(blocks, valid, views, cross_bias)), query.shape[0])


def solution(mesh):
    groups = mesh.shape["grp"]
    members = mesh.shape["blk"] * mesh.shape["head"]

    def run(query, keys, values, grad_out, valid, views, cross_bias):
        heads = query.shape[1] // HD
        layout = Mesh(
            mesh.devices.reshape(groups, heads, members // heads), ("grp", "heads", "share")
        )
        tokens = P(("grp", "heads", "share"), None)
        return jax.shard_map(
            local,
            mesh=layout,
            in_specs=(tokens,) * 4 + (P("grp"), P("grp"), P()),
            out_specs=(tokens,) * 3,
            check_vma=False,
        )(query, keys, values, grad_out, valid, views, cross_bias)

    return run
```

```python
import functools
import math

import jax
import jax.numpy as jnp
from jax import lax
from jax.experimental import pallas as pl
from jax.experimental.pallas import tpu as pltpu
from jax.sharding import Mesh, PartitionSpec as P

HD = 64
FRAME = 32
PAIR = 2 * HD
TILE = 128
CHUNK = 128
SUBLANES = 8
UNROLL = 2

SCALE = 0.125
DEAD = -1e30
LOG2E = math.log2(math.e)
LIMIT = 48 * 1024 * 1024

VMEM = pl.BlockSpec(memory_space=pltpu.VMEM)
SMEM = pl.BlockSpec(memory_space=pltpu.SMEM)


def side_by_side(left, right):
    return jnp.concatenate([left, right], axis=1)


def pack_kernel(q_ref, k_ref, v_ref, g_ref, out_ref):
    rows, width = q_ref.shape
    q, k, v, g = q_ref[...], k_ref[...], v_ref[...], g_ref[...]
    for head in range(width // HD):
        at = slice(head * HD, (head + 1) * HD)
        out_ref[head, :rows] = side_by_side(k[:, at], v[:, at])
        out_ref[head, rows:] = side_by_side(q[:, at], g[:, at])


def pack(query, keys, values, grad_out):
    rows, width = query.shape
    return pl.pallas_call(
        pack_kernel,
        out_shape=pltpu.VMEM((width // HD, 2 * rows, PAIR), query.dtype),
        in_specs=[VMEM] * 4,
        out_specs=VMEM,
        name="pack_heads",
    )(query, keys, values, grad_out)


def attend_kernel(shares, *refs):
    blocks = refs[:shares]
    valid_ref, views_ref, bias_ref, out_ref = refs[shares : shares + 4]
    kv_ref, qg_ref, flip_ref, sum_ref, dq_ref = refs[shares + 4 :]
    homes, rows = blocks[0].shape[0], blocks[0].shape[1] // 2
    own = homes * rows
    tokens = own * shares
    per_home, per_tile = rows // FRAME, TILE // rows
    tiles, chunks, own_chunks = own // TILE, tokens // CHUNK, own // CHUNK
    mine = lax.axis_index("share")
    unroll = UNROLL if shares <= 2 else 1
    slot = lax.broadcasted_iota(jnp.int32, (FRAME, PAIR), 0)
    lane = lax.broadcasted_iota(jnp.int32, (1, PAIR), 1)

    bias = jnp.full((1, PAIR), bias_ref[lax.axis_index("heads")] / SCALE, jnp.float32)
    high = bias.astype(jnp.bfloat16).astype(jnp.float32)
    middle = (bias - high).astype(jnp.bfloat16).astype(jnp.float32)
    part = lax.rem(lane, 3)
    parts = jnp.where(part == 0, high, jnp.where(part == 1, middle, bias - high - middle))
    dead = jnp.where(lane == 6, DEAD / SCALE, 0.0)
    of_exo_query = jnp.where(lane < 3, parts, dead)
    of_ego_query = jnp.where((lane >= 3) & (lane < 6), parts, dead)

    def frame_of(block, home, which):
        share = lax.rem(mine + block, shares)
        return (home * shares + share) * per_home + which

    for block in range(shares):
        start = block * own
        for home in range(homes):
            here = slice(start + home * rows, start + (home + 1) * rows)
            kv_ref[here, :PAIR] = blocks[block][home, :rows]
            qg_ref[here, :] = blocks[block][home, rows:]
            for which in range(per_home):
                frame = frame_of(block, home, which)
                first = jnp.where(views_ref[frame] != 0, 3, 0)
                marks = jnp.where((lane >= first) & (lane < first + 3), 1.0, 0.0)
                gone = jnp.where(slot < valid_ref[frame], 0.0, 1.0)
                here = slice(
                    start + home * rows + which * FRAME,
                    start + home * rows + (which + 1) * FRAME,
                )
                kv_ref[here, PAIR:] = jnp.where(lane == 6, gone, marks).astype(jnp.bfloat16)
        here = slice(start, start + own)
        flip = kv_ref[here, :PAIR].astype(jnp.float32).T
        flip_ref[:, here] = flip[:HD].astype(jnp.bfloat16)

    sum_ref[...] = jnp.zeros_like(sum_ref)
    low = lax.broadcasted_iota(jnp.int32, (TILE, PAIR), 1) < HD
    contract_last = (((1,), (1,)), ((), ()))

    def tile(ours, index):
        here = pl.ds(pl.multiple_of(index * TILE, TILE), TILE)
        qg = qg_ref[here, :].astype(jnp.float32)
        weights = jnp.concatenate(
            [jnp.where(low, qg, 0.0), jnp.where(low, 0.0, qg)], axis=0
        ).astype(jnp.bfloat16)
        block, first = lax.div(index, tiles), lax.rem(index, tiles) * per_tile
        marks = []
        for part in range(TILE // FRAME):
            view = views_ref[frame_of(block, first + part // per_home, part % per_home)]
            row = jnp.where(view != 0, of_exo_query, of_ego_query)
            marks.append(jnp.broadcast_to(row, (FRAME, PAIR)))
        marks.append(jnp.zeros((TILE, PAIR), jnp.float32))
        marks = jnp.concatenate(marks, axis=0).astype(jnp.bfloat16)

        both = lax.dot_general(
            kv_ref[...],
            side_by_side(weights, marks),
            contract_last,
            preferred_element_type=jnp.float32,
        )
        tops, totals, mixes, expos, gws = [], [], [], [], []
        for c in range(chunks):
            at = slice(c * CHUNK, (c + 1) * CHUNK)
            raw = both[at, :TILE].reshape(-1, SUBLANES, TILE)
            gw = both[at, TILE:].reshape(-1, SUBLANES, TILE)
            top = jnp.max(raw, axis=0)
            expo = jnp.exp2((raw - top) * (SCALE * LOG2E))
            expos.append(expo)
            gws.append(gw)
            tops.append(top)
            totals.append(jnp.sum(expo, axis=0))
            mixes.append(jnp.sum(expo * gw, axis=0))
        highest = jnp.max(functools.reduce(jnp.maximum, tops), axis=0, keepdims=True)
        factors = [jnp.exp2((top - highest) * (SCALE * LOG2E)) for top in tops]
        total = jnp.sum(sum(f * t for f, t in zip(factors, totals)), axis=0, keepdims=True)
        mixed = jnp.sum(sum(f * m for f, m in zip(factors, mixes)), axis=0, keepdims=True)
        inverse = 1.0 / total
        delta = mixed * inverse

        lows, grads = [], []
        for c in range(chunks if ours else own_chunks):
            weight = expos[c] * (factors[c] * inverse)
            grad = (weight * SCALE) * (gws[c] - delta)
            grads.append(grad.reshape(CHUNK, TILE).astype(jnp.bfloat16))
            if c < own_chunks:
                lows.append(weight.reshape(CHUNK, TILE).astype(jnp.bfloat16))
        return weights, jnp.concatenate(grads, axis=0), jnp.concatenate(lows, axis=0)

    def two_tiles(ours, pair):
        weights, grads, lows = zip(*(tile(ours, 2 * pair + which) for which in range(2)))
        factors = [x for both in zip(grads, lows) for x in (both[0][:own], both[1])]
        sum_ref[...] += jnp.dot(
            jnp.concatenate(factors, axis=1),
            jnp.concatenate(weights, axis=0),
            preferred_element_type=jnp.float32,
        )
        if ours:
            turned = jnp.dot(
                flip_ref[...], side_by_side(*grads), preferred_element_type=jnp.float32
            )
            here = pl.ds(pl.multiple_of(pair * (2 * TILE), 2 * TILE), 2 * TILE)
            dq_ref[here, :] = jnp.concatenate([turned, turned], axis=0).T

    pairs = tiles // 2
    pl.loop(0, pairs, unroll=unroll)(functools.partial(two_tiles, True))
    pl.loop(pairs, pairs * shares, unroll=unroll)(functools.partial(two_tiles, False))
    out_ref[:, :rows, :] = sum_ref[...].astype(jnp.bfloat16).reshape(homes, rows, PAIR)
    for home in range(homes):
        start, half = home * rows, rows // 2
        out_ref[home, rows:, :] = side_by_side(
            dq_ref[start : start + half, :HD], dq_ref[start + half : start + rows, :HD]
        ).astype(jnp.bfloat16)


def attend(blocks, valid, views, cross_bias):
    homes, both, _ = blocks[0].shape
    rows = both // 2
    own = homes * rows
    tokens = own * len(blocks)
    return pl.pallas_call(
        functools.partial(attend_kernel, len(blocks)),
        out_shape=jax.ShapeDtypeStruct((homes, rows + rows // 2, PAIR), jnp.bfloat16),
        in_specs=[VMEM] * len(blocks) + [SMEM] * 3,
        out_specs=VMEM,
        scratch_shapes=[
            pltpu.VMEM((tokens, 2 * PAIR), jnp.bfloat16),
            pltpu.VMEM((tokens, PAIR), jnp.bfloat16),
            pltpu.VMEM((HD, tokens), jnp.bfloat16),
            pltpu.VMEM((own, PAIR), jnp.float32),
            pltpu.VMEM((own, PAIR), jnp.float32),
        ],
        compiler_params=pltpu.CompilerParams(vmem_limit_bytes=LIMIT),
        name="attend_backward",
    )(*blocks, valid, views, cross_bias)


def unpack_kernel(in_ref, dq_ref, dk_ref, dv_ref):
    rows = dq_ref.shape[0]
    half = rows // 2
    for head in range(0, in_ref.shape[0], 2):
        columns = slice(head * HD, (head + 2) * HD)
        one, two = (in_ref[head + which].astype(jnp.float32) for which in (0, 1))
        left = side_by_side(one[:, :HD], two[:, :HD])
        right = side_by_side(one[:, HD:], two[:, HD:])
        dk_ref[:, columns] = left[:rows]
        dv_ref[:, columns] = right[:rows]
        dq_ref[:half, columns] = left[rows:]
        dq_ref[half:, columns] = right[rows:]


def unpack(given, rows):
    shape = jax.ShapeDtypeStruct((rows, given.shape[0] * HD), jnp.float32)
    return pl.pallas_call(
        unpack_kernel,
        out_shape=(shape,) * 3,
        in_specs=[VMEM],
        out_specs=(VMEM,) * 3,
        name="unpack_heads",
    )(pltpu.with_memory_space_constraint(given, pltpu.VMEM))


def local(query, keys, values, grad_out, valid, views, cross_bias):
    swap = functools.partial(
        lax.all_to_all, axis_name="heads", split_axis=0, concat_axis=0, tiled=True
    )
    shares = lax.axis_size("share")
    mine = swap(pack(query, keys, values, grad_out))
    blocks = [mine] + [
        lax.ppermute(mine, "share", [((i + k) % shares, i) for i in range(shares)])
        for k in range(1, shares)
    ]
    return unpack(swap(attend(blocks, valid, views, cross_bias)), query.shape[0])


def solution(mesh):
    groups = mesh.shape["grp"]
    members = mesh.shape["blk"] * mesh.shape["head"]

    def run(query, keys, values, grad_out, valid, views, cross_bias):
        heads = query.shape[1] // HD
        layout = Mesh(
            mesh.devices.reshape(groups, heads, members // heads), ("grp", "heads", "share")
        )
        tokens = P(("grp", "heads", "share"), None)
        return jax.shard_map(
            local,
            mesh=layout,
            in_specs=(tokens,) * 4 + (P("grp"), P("grp"), P()),
            out_specs=(tokens,) * 3,
            check_vma=False,
        )(query, keys, values, grad_out, valid, views, cross_bias)

    return run
```

```python
import functools
import math

import jax
import jax.numpy as jnp
from jax import lax
from jax.experimental import pallas as pl
from jax.experimental.pallas import tpu as pltpu
from jax.sharding import Mesh, PartitionSpec as P

HD = 64
FRAME = 32
PAIR = 2 * HD
TILE = 128
CHUNK = 128
SUBLANES = 8

SCALE = 0.125
DEAD = -1e30
LOG2E = math.log2(math.e)
LIMIT = 48 * 1024 * 1024

VMEM = pl.BlockSpec(memory_space=pltpu.VMEM)
SMEM = pl.BlockSpec(memory_space=pltpu.SMEM)


def side_by_side(left, right):
    return jnp.concatenate([left, right], axis=1)


def pack_kernel(q_ref, k_ref, v_ref, g_ref, out_ref):
    rows, width = q_ref.shape
    q, k, v, g = q_ref[...], k_ref[...], v_ref[...], g_ref[...]
    for head in range(width // HD):
        at = slice(head * HD, (head + 1) * HD)
        out_ref[head, :rows] = side_by_side(k[:, at], v[:, at])
        out_ref[head, rows:] = side_by_side(q[:, at], g[:, at])


def pack(query, keys, values, grad_out):
    rows, width = query.shape
    return pl.pallas_call(
        pack_kernel,
        out_shape=pltpu.VMEM((width // HD, 2 * rows, PAIR), query.dtype),
        in_specs=[VMEM] * 4,
        out_specs=VMEM,
        name="pack_heads",
    )(query, keys, values, grad_out)


def attend_kernel(shares, *refs):
    blocks = refs[:shares]
    valid_ref, views_ref, bias_ref, out_ref = refs[shares : shares + 4]
    kv_ref, qg_ref, flip_ref, sum_ref, dq_ref = refs[shares + 4 :]
    homes, rows = blocks[0].shape[0], blocks[0].shape[1] // 2
    own = homes * rows
    tokens = own * shares
    per_home, per_tile = rows // FRAME, TILE // rows
    tiles, chunks, own_chunks = own // TILE, tokens // CHUNK, own // CHUNK
    mine = lax.axis_index("share")
    slot = lax.broadcasted_iota(jnp.int32, (FRAME, PAIR), 0)
    lane = lax.broadcasted_iota(jnp.int32, (1, PAIR), 1)

    bias = jnp.full((1, PAIR), bias_ref[lax.axis_index("heads")] / SCALE, jnp.float32)
    high = bias.astype(jnp.bfloat16).astype(jnp.float32)
    middle = (bias - high).astype(jnp.bfloat16).astype(jnp.float32)
    part = lax.rem(lane, 3)
    parts = jnp.where(part == 0, high, jnp.where(part == 1, middle, bias - high - middle))
    dead = jnp.where(lane == 6, DEAD / SCALE, 0.0)
    of_exo_query = jnp.where(lane < 3, parts, dead)
    of_ego_query = jnp.where((lane >= 3) & (lane < 6), parts, dead)

    def frame_of(block, home, which):
        share = lax.rem(mine + block, shares)
        return (home * shares + share) * per_home + which

    for block in range(shares):
        start = block * own
        for home in range(homes):
            here = slice(start + home * rows, start + (home + 1) * rows)
            kv_ref[here, :PAIR] = blocks[block][home, :rows]
            qg_ref[here, :] = blocks[block][home, rows:]
            for which in range(per_home):
                frame = frame_of(block, home, which)
                first = jnp.where(views_ref[frame] != 0, 3, 0)
                marks = jnp.where((lane >= first) & (lane < first + 3), 1.0, 0.0)
                gone = jnp.where(slot < valid_ref[frame], 0.0, 1.0)
                here = slice(
                    start + home * rows + which * FRAME,
                    start + home * rows + (which + 1) * FRAME,
                )
                kv_ref[here, PAIR:] = jnp.where(lane == 6, gone, marks).astype(jnp.bfloat16)
        here = slice(start, start + own)
        flip = kv_ref[here, :PAIR].astype(jnp.float32).T
        flip_ref[:, here] = flip[:HD].astype(jnp.bfloat16)

    sum_ref[...] = jnp.zeros_like(sum_ref)
    low = lax.broadcasted_iota(jnp.int32, (TILE, PAIR), 1) < HD
    contract_last = (((1,), (1,)), ((), ()))

    def score(index):
        here = pl.ds(pl.multiple_of(index * TILE, TILE), TILE)
        qg = qg_ref[here, :].astype(jnp.float32)
        weights = jnp.concatenate(
            [jnp.where(low, qg, 0.0), jnp.where(low, 0.0, qg)], axis=0
        ).astype(jnp.bfloat16)
        block, first = lax.div(index, tiles), lax.rem(index, tiles) * per_tile
        marks = []
        for part in range(TILE // FRAME):
            view = views_ref[frame_of(block, first + part // per_home, part % per_home)]
            row = jnp.where(view != 0, of_exo_query, of_ego_query)
            marks.append(jnp.broadcast_to(row, (FRAME, PAIR)))
        marks.append(jnp.zeros((TILE, PAIR), jnp.float32))
        marks = jnp.concatenate(marks, axis=0).astype(jnp.bfloat16)
        return weights, lax.dot_general(
            kv_ref[...],
            side_by_side(weights, marks),
            contract_last,
            preferred_element_type=jnp.float32,
        )

    def exponentials(both):
        parts = []
        for c in range(chunks):
            at = slice(c * CHUNK, (c + 1) * CHUNK)
            raw = both[at, :TILE].reshape(-1, SUBLANES, TILE)
            gw = both[at, TILE:].reshape(-1, SUBLANES, TILE)
            top = jnp.max(raw, axis=0)
            expo = jnp.exp2((raw - top) * (SCALE * LOG2E))
            parts.append((expo, gw, top, jnp.sum(expo, axis=0), jnp.sum(expo * gw, axis=0)))
        return parts

    def gradients(ours, parts):
        expos, gws, tops, totals, mixes = zip(*parts)
        highest = jnp.max(functools.reduce(jnp.maximum, tops), axis=0, keepdims=True)
        factors = [jnp.exp2((top - highest) * (SCALE * LOG2E)) for top in tops]
        total = jnp.sum(sum(f * t for f, t in zip(factors, totals)), axis=0, keepdims=True)
        mixed = jnp.sum(sum(f * m for f, m in zip(factors, mixes)), axis=0, keepdims=True)
        inverse = 1.0 / total
        delta = mixed * inverse
        lows, grads = [], []
        for c in range(chunks if ours else own_chunks):
            weight = expos[c] * (factors[c] * inverse)
            grad = (weight * SCALE) * (gws[c] - delta)
            grads.append(grad.reshape(CHUNK, TILE).astype(jnp.bfloat16))
            if c < own_chunks:
                lows.append(weight.reshape(CHUNK, TILE).astype(jnp.bfloat16))
        return jnp.concatenate(grads, axis=0), jnp.concatenate(lows, axis=0)

    def leave(ours, first, pair):
        weights, grads, lows = zip(*pair)
        factors = [x for both in zip(grads, lows) for x in (both[0][:own], both[1])]
        sum_ref[...] += jnp.dot(
            jnp.concatenate(factors, axis=1),
            jnp.concatenate(weights, axis=0),
            preferred_element_type=jnp.float32,
        )
        if ours:
            turned = jnp.dot(
                flip_ref[...], side_by_side(*grads), preferred_element_type=jnp.float32
            )
            here = pl.ds(pl.multiple_of(first * TILE, 2 * TILE), 2 * TILE)
            dq_ref[here, :] = jnp.concatenate([turned, turned], axis=0).T

    def pipeline(work):
        scored, expos, done = {}, {}, {}
        for step in range(len(work) + 2):
            if step < len(work):
                scored[step] = score(work[step][1])
            if 0 <= step - 1 < len(work):
                weights, both = scored.pop(step - 1)
                expos[step - 1] = weights, exponentials(both)
            if 0 <= step - 2:
                ours, index = work[step - 2]
                weights, parts = expos.pop(step - 2)
                done[step - 2] = (weights, *gradients(ours, parts))
                if step % 2:
                    leave(ours, work[step - 3][1], (done.pop(step - 3), done.pop(step - 2)))

    if shares <= 2:
        pipeline([(index < tiles, index) for index in range(tiles * shares)])
    else:
        pl.loop(0, tiles, step=2)(lambda i: pipeline([(True, i), (True, i + 1)]))
        pl.loop(tiles, tiles * shares, step=2)(
            lambda i: pipeline([(False, i), (False, i + 1)])
        )
    out_ref[:, :rows, :] = sum_ref[...].astype(jnp.bfloat16).reshape(homes, rows, PAIR)
    for home in range(homes):
        start, half = home * rows, rows // 2
        out_ref[home, rows:, :] = side_by_side(
            dq_ref[start : start + half, :HD], dq_ref[start + half : start + rows, :HD]
        ).astype(jnp.bfloat16)


def attend(blocks, valid, views, cross_bias):
    homes, both, _ = blocks[0].shape
    rows = both // 2
    own = homes * rows
    tokens = own * len(blocks)
    return pl.pallas_call(
        functools.partial(attend_kernel, len(blocks)),
        out_shape=jax.ShapeDtypeStruct((homes, rows + rows // 2, PAIR), jnp.bfloat16),
        in_specs=[VMEM] * len(blocks) + [SMEM] * 3,
        out_specs=VMEM,
        scratch_shapes=[
            pltpu.VMEM((tokens, 2 * PAIR), jnp.bfloat16),
            pltpu.VMEM((tokens, PAIR), jnp.bfloat16),
            pltpu.VMEM((HD, tokens), jnp.bfloat16),
            pltpu.VMEM((own, PAIR), jnp.float32),
            pltpu.VMEM((own, PAIR), jnp.float32),
        ],
        compiler_params=pltpu.CompilerParams(vmem_limit_bytes=LIMIT),
        name="attend_backward",
    )(*blocks, valid, views, cross_bias)


def unpack_kernel(in_ref, dq_ref, dk_ref, dv_ref):
    rows = dq_ref.shape[0]
    half = rows // 2
    for head in range(0, in_ref.shape[0], 2):
        columns = slice(head * HD, (head + 2) * HD)
        one, two = (in_ref[head + which].astype(jnp.float32) for which in (0, 1))
        left = side_by_side(one[:, :HD], two[:, :HD])
        right = side_by_side(one[:, HD:], two[:, HD:])
        dk_ref[:, columns] = left[:rows]
        dv_ref[:, columns] = right[:rows]
        dq_ref[:half, columns] = left[rows:]
        dq_ref[half:, columns] = right[rows:]


def unpack(given, rows):
    shape = jax.ShapeDtypeStruct((rows, given.shape[0] * HD), jnp.float32)
    return pl.pallas_call(
        unpack_kernel,
        out_shape=(shape,) * 3,
        in_specs=[VMEM],
        out_specs=(VMEM,) * 3,
        name="unpack_heads",
    )(pltpu.with_memory_space_constraint(given, pltpu.VMEM))


def local(query, keys, values, grad_out, valid, views, cross_bias):
    swap = functools.partial(
        lax.all_to_all, axis_name="heads", split_axis=0, concat_axis=0, tiled=True
    )
    shares = lax.axis_size("share")
    mine = swap(pack(query, keys, values, grad_out))
    blocks = [mine] + [
        lax.ppermute(mine, "share", [((i + k) % shares, i) for i in range(shares)])
        for k in range(1, shares)
    ]
    return unpack(swap(attend(blocks, valid, views, cross_bias)), query.shape[0])


def solution(mesh):
    groups = mesh.shape["grp"]
    members = mesh.shape["blk"] * mesh.shape["head"]

    def run(query, keys, values, grad_out, valid, views, cross_bias):
        heads = query.shape[1] // HD
        layout = Mesh(
            mesh.devices.reshape(groups, heads, members // heads), ("grp", "heads", "share")
        )
        tokens = P(("grp", "heads", "share"), None)
        return jax.shard_map(
            local,
            mesh=layout,
            in_specs=(tokens,) * 4 + (P("grp"), P("grp"), P()),
            out_specs=(tokens,) * 3,
            check_vma=False,
        )(query, keys, values, grad_out, valid, views, cross_bias)

    return run
```

```python
import functools
import math

import jax
import jax.numpy as jnp
from jax import lax
from jax.experimental import pallas as pl
from jax.experimental.pallas import tpu as pltpu
from jax.sharding import Mesh, PartitionSpec as P

HD = 64
FRAME = 32
PAIR = 2 * HD
TILE = 128
CHUNK = 128
SUBLANES = 8

SCALE = 0.125
DEAD = -1e30
LOG2E = math.log2(math.e)
LIMIT = 48 * 1024 * 1024

VMEM = pl.BlockSpec(memory_space=pltpu.VMEM)
SMEM = pl.BlockSpec(memory_space=pltpu.SMEM)


def side_by_side(left, right):
    return jnp.concatenate([left, right], axis=1)


def pack_kernel(q_ref, k_ref, v_ref, g_ref, out_ref):
    rows, width = q_ref.shape
    q, k, v, g = q_ref[...], k_ref[...], v_ref[...], g_ref[...]
    for head in range(width // HD):
        at = slice(head * HD, (head + 1) * HD)
        out_ref[head, :rows] = side_by_side(k[:, at], v[:, at])
        out_ref[head, rows:] = side_by_side(q[:, at], g[:, at])


def pack(query, keys, values, grad_out):
    rows, width = query.shape
    return pl.pallas_call(
        pack_kernel,
        out_shape=pltpu.VMEM((width // HD, 2 * rows, PAIR), query.dtype),
        in_specs=[VMEM] * 4,
        out_specs=VMEM,
        name="pack_heads",
    )(query, keys, values, grad_out)


def frame_of(homes, shares, per_home, block, home, which):
    share = lax.rem(lax.axis_index("share") + block, shares)
    return (home * shares + share) * per_home + which


def query_weights(qg):
    qg = qg.astype(jnp.float32)
    low = lax.broadcasted_iota(jnp.int32, qg.shape, 1) < HD
    return jnp.concatenate(
        [jnp.where(low, qg, 0.0), jnp.where(low, 0.0, qg)], axis=0
    ).astype(jnp.bfloat16)


def products(keys, weights):
    return lax.dot_general(
        keys, weights, (((1,), (1,)), ((), ())), preferred_element_type=jnp.float32
    )


def exponentials(raw, gw):
    raw, gw = (x.reshape(-1, SUBLANES, TILE) for x in (raw, gw))
    top = jnp.max(raw, axis=0)
    expo = jnp.exp2((raw - top) * (SCALE * LOG2E))
    return expo, (top, jnp.sum(expo, axis=0), jnp.sum(expo * gw, axis=0))


def chunk_of(c):
    return slice(c * CHUNK, (c + 1) * CHUNK)


def begin_kernel(shares, mine_ref, valid_ref, views_ref, bias_ref, key_mark_ref,
                 query_mark_ref, weights_ref, flip_ref, expo_ref, gw_ref, stat_ref, keys_ref):
    homes, rows = mine_ref.shape[0], mine_ref.shape[1] // 2
    own = homes * rows
    per_home, per_tile, tiles = rows // FRAME, TILE // rows, own // TILE
    slot = lax.broadcasted_iota(jnp.int32, (FRAME, PAIR), 0)
    lane = lax.broadcasted_iota(jnp.int32, (1, PAIR), 1)

    bias = jnp.full((1, PAIR), bias_ref[lax.axis_index("heads")] / SCALE, jnp.float32)
    high = bias.astype(jnp.bfloat16).astype(jnp.float32)
    middle = (bias - high).astype(jnp.bfloat16).astype(jnp.float32)
    part = lax.rem(lane, 3)
    parts = jnp.where(part == 0, high, jnp.where(part == 1, middle, bias - high - middle))
    dead = jnp.where(lane == 6, DEAD / SCALE, 0.0)
    of_exo_query = jnp.where(lane < 3, parts, dead)
    of_ego_query = jnp.where((lane >= 3) & (lane < 6), parts, dead)

    for block in range(shares):
        for home in range(homes):
            for which in range(per_home):
                frame = frame_of(homes, shares, per_home, block, home, which)
                start = block * own + home * rows + which * FRAME
                here = slice(start, start + FRAME)
                exo = views_ref[frame] != 0
                first = jnp.where(exo, 3, 0)
                marks = jnp.where((lane >= first) & (lane < first + 3), 1.0, 0.0)
                gone = jnp.where(slot < valid_ref[frame], 0.0, 1.0)
                key_mark_ref[here, :] = jnp.where(lane == 6, gone, marks).astype(jnp.bfloat16)
                query_mark_ref[here, :] = jnp.broadcast_to(
                    jnp.where(exo, of_exo_query, of_ego_query), (FRAME, PAIR)
                ).astype(jnp.bfloat16)

    kv = mine_ref[:, :rows, :].reshape(own, PAIR)
    flip_ref[...] = kv.astype(jnp.float32).T[:HD].astype(jnp.bfloat16)
    keys_ref[:, :PAIR] = kv
    keys_ref[:, PAIR:] = key_mark_ref[:own, :]

    def score(index):
        qg = mine_ref[index * per_tile : (index + 1) * per_tile, rows:, :].reshape(TILE, PAIR)
        marks = query_mark_ref[index * TILE : (index + 1) * TILE, :]
        weights = side_by_side(
            query_weights(qg), jnp.concatenate([marks, jnp.zeros_like(marks)], axis=0)
        )
        weights_ref[index] = weights
        return products(keys_ref[...], weights)

    def leave(index, both):
        gw_ref[index] = both[:, TILE:]
        for c in range(own // CHUNK):
            at = chunk_of(c)
            expo, stats = exponentials(both[at, :TILE], both[at, TILE:])
            expo_ref[index, at, :] = expo.reshape(CHUNK, TILE)
            for which, stat in enumerate(stats):
                stat_ref[index, which, c] = stat

    scored = None
    for step in range(tiles + 1):
        last, scored = scored, score(step) if step < tiles else None
        if step:
            leave(step - 1, last)


def finish_kernel(shares, *refs):
    blocks, refs = refs[:shares], refs[shares:]
    key_mark_ref, query_mark_ref, weights_ref, own_flip_ref = refs[:4]
    expo_ref, gw_ref, stat_ref, out_ref, keys_ref, qg_ref, flip_ref, sum_ref, dq_ref = refs[4:]
    homes, rows = blocks[0].shape[0], blocks[0].shape[1] // 2
    own = homes * rows
    tokens = own * shares
    tiles, chunks, own_chunks = own // TILE, tokens // CHUNK, own // CHUNK

    keys_ref[:, PAIR:] = key_mark_ref[...]
    flip_ref[:, :own] = own_flip_ref[...]
    for block in range(shares):
        here = slice(block * own, (block + 1) * own)
        kv = blocks[block][:, :rows, :].reshape(own, PAIR)
        keys_ref[here, :PAIR] = kv
        if block:
            there = slice((block - 1) * own, block * own)
            flip_ref[:, here] = kv.astype(jnp.float32).T[:HD].astype(jnp.bfloat16)
            qg_ref[there, :] = blocks[block][:, rows:, :].reshape(own, PAIR)
    sum_ref[...] = jnp.zeros_like(sum_ref)

    def score(ours, index):
        if ours:
            weights = weights_ref[index]
            if chunks == own_chunks:
                return weights, None
            return weights, products(keys_ref[own:, :], weights)
        here = pl.ds(pl.multiple_of(index * TILE, TILE), TILE)
        there = pl.ds(pl.multiple_of(own + index * TILE, TILE), TILE)
        marks = query_mark_ref[there, :]
        weights = side_by_side(
            query_weights(qg_ref[here, :]),
            jnp.concatenate([marks, jnp.zeros_like(marks)], axis=0),
        )
        return weights, products(keys_ref[...], weights)

    def all_exponentials(ours, index, both):
        parts = []
        given = own_chunks if ours else 0
        for c in range(given):
            parts.append((None, None, *(stat_ref[index, which, c] for which in range(3))))
        for c in range(chunks - given):
            gw = both[chunk_of(c), TILE:]
            expo, stats = exponentials(both[chunk_of(c), :TILE], gw)
            parts.append((expo, gw.reshape(-1, SUBLANES, TILE), *stats))
        return parts

    def gradients(ours, index, parts):
        expos, gws, tops, totals, mixes = zip(*parts)
        highest = jnp.max(functools.reduce(jnp.maximum, tops), axis=0, keepdims=True)
        factors = [jnp.exp2((top - highest) * (SCALE * LOG2E)) for top in tops]
        total = jnp.sum(sum(f * t for f, t in zip(factors, totals)), axis=0, keepdims=True)
        mixed = jnp.sum(sum(f * m for f, m in zip(factors, mixes)), axis=0, keepdims=True)
        inverse = 1.0 / total
        delta = mixed * inverse
        lows, grads = [], []
        for c in range(chunks if ours else own_chunks):
            expo, gw = expos[c], gws[c]
            if expo is None:
                expo, gw = (
                    ref[index, chunk_of(c), :].reshape(-1, SUBLANES, TILE)
                    for ref in (expo_ref, gw_ref)
                )
            weight = expo * (factors[c] * inverse)
            grad = (weight * SCALE) * (gw - delta)
            grads.append(grad.reshape(CHUNK, TILE).astype(jnp.bfloat16))
            if c < own_chunks:
                lows.append(weight.reshape(CHUNK, TILE).astype(jnp.bfloat16))
        return jnp.concatenate(grads, axis=0), jnp.concatenate(lows, axis=0)

    def leave(ours, first, pair):
        weights, grads, lows = zip(*pair)
        factors = [x for both in zip(grads, lows) for x in (both[0][:own], both[1])]
        sum_ref[...] += jnp.dot(
            jnp.concatenate(factors, axis=1),
            jnp.concatenate([each[:, :PAIR] for each in weights], axis=0),
            preferred_element_type=jnp.float32,
        )
        if ours:
            turned = jnp.dot(
                flip_ref[...], side_by_side(*grads), preferred_element_type=jnp.float32
            )
            here = pl.ds(pl.multiple_of(first * TILE, 2 * TILE), 2 * TILE)
            dq_ref[here, :] = jnp.concatenate([turned, turned], axis=0).T

    def pipeline(work):
        scored, expos, done = {}, {}, {}
        for step in range(len(work) + 2):
            if step < len(work):
                scored[step] = score(*work[step])
            if 0 <= step - 1 < len(work):
                weights, both = scored.pop(step - 1)
                expos[step - 1] = weights, all_exponentials(*work[step - 1], both)
            if 0 <= step - 2:
                weights, parts = expos.pop(step - 2)
                done[step - 2] = (weights, *gradients(*work[step - 2], parts))
                if step % 2:
                    leave(*work[step - 3], (done.pop(step - 3), done.pop(step - 2)))

    others = tiles * (shares - 1)
    if shares <= 2:
        pipeline([(True, i) for i in range(tiles)] + [(False, i) for i in range(others)])
    else:
        pl.loop(0, tiles, step=2)(lambda i: pipeline([(True, i), (True, i + 1)]))
        pl.loop(0, others, step=2)(lambda i: pipeline([(False, i), (False, i + 1)]))
    out_ref[:, :rows, :] = sum_ref[...].astype(jnp.bfloat16).reshape(homes, rows, PAIR)
    for home in range(homes):
        start, half = home * rows, rows // 2
        out_ref[home, rows:, :] = side_by_side(
            dq_ref[start : start + half, :HD], dq_ref[start + half : start + rows, :HD]
        ).astype(jnp.bfloat16)


def attend(mine, others, valid, views, cross_bias):
    shares = len(others) + 1
    homes, both, _ = mine.shape
    rows = both // 2
    own = homes * rows
    tokens, tiles = own * shares, own // TILE
    begun = pl.pallas_call(
        functools.partial(begin_kernel, shares),
        out_shape=(
            pltpu.VMEM((tokens, PAIR), jnp.bfloat16),
            pltpu.VMEM((tokens, PAIR), jnp.bfloat16),
            pltpu.VMEM((tiles, 2 * TILE, 2 * PAIR), jnp.bfloat16),
            pltpu.VMEM((HD, own), jnp.bfloat16),
            pltpu.VMEM((tiles, own, TILE), jnp.float32),
            pltpu.VMEM((tiles, own, TILE), jnp.float32),
            pltpu.VMEM((tiles, 3, own // CHUNK, SUBLANES, TILE), jnp.float32),
        ),
        in_specs=[VMEM] + [SMEM] * 3,
        out_specs=(VMEM,) * 7,
        scratch_shapes=[pltpu.VMEM((own, 2 * PAIR), jnp.bfloat16)],
        compiler_params=pltpu.CompilerParams(vmem_limit_bytes=LIMIT),
        cost_estimate=pl.CostEstimate(
            flops=8 * own * own * PAIR, bytes_accessed=8 * own * own, transcendentals=own * own
        ),
        name="attend_begin",
    )(mine, valid, views, cross_bias)
    return pl.pallas_call(
        functools.partial(finish_kernel, shares),
        out_shape=pltpu.VMEM((homes, rows + rows // 2, PAIR), jnp.bfloat16),
        in_specs=[VMEM] * (shares + 7),
        out_specs=VMEM,
        scratch_shapes=[
            pltpu.VMEM((tokens, 2 * PAIR), jnp.bfloat16),
            pltpu.VMEM((max(tokens - own, TILE), PAIR), jnp.bfloat16),
            pltpu.VMEM((HD, tokens), jnp.bfloat16),
            pltpu.VMEM((own, PAIR), jnp.float32),
            pltpu.VMEM((own, PAIR), jnp.float32),
        ],
        compiler_params=pltpu.CompilerParams(vmem_limit_bytes=LIMIT),
        name="attend_finish",
    )(mine, *others, *begun)


def unpack_kernel(in_ref, dq_ref, dk_ref, dv_ref):
    rows = dq_ref.shape[0]
    half = rows // 2
    for head in range(0, in_ref.shape[0], 2):
        columns = slice(head * HD, (head + 2) * HD)
        one, two = (in_ref[head + which].astype(jnp.float32) for which in (0, 1))
        left = side_by_side(one[:, :HD], two[:, :HD])
        right = side_by_side(one[:, HD:], two[:, HD:])
        dk_ref[:, columns] = left[:rows]
        dv_ref[:, columns] = right[:rows]
        dq_ref[:half, columns] = left[rows:]
        dq_ref[half:, columns] = right[rows:]


def unpack(given, rows):
    shape = jax.ShapeDtypeStruct((rows, given.shape[0] * HD), jnp.float32)
    return pl.pallas_call(
        unpack_kernel,
        out_shape=(shape,) * 3,
        in_specs=[VMEM],
        out_specs=(VMEM,) * 3,
        name="unpack_heads",
    )(pltpu.with_memory_space_constraint(given, pltpu.VMEM))


def local(query, keys, values, grad_out, valid, views, cross_bias):
    swap = functools.partial(
        lax.all_to_all, axis_name="heads", split_axis=0, concat_axis=0, tiled=True
    )
    shares = lax.axis_size("share")
    mine = swap(pack(query, keys, values, grad_out))
    others = [
        lax.ppermute(mine, "share", [((i + k) % shares, i) for i in range(shares)])
        for k in range(1, shares)
    ]
    given = attend(mine, others, valid, views, cross_bias)
    return unpack(swap(given), query.shape[0])


def solution(mesh):
    groups = mesh.shape["grp"]
    members = mesh.shape["blk"] * mesh.shape["head"]

    def run(query, keys, values, grad_out, valid, views, cross_bias):
        heads = query.shape[1] // HD
        layout = Mesh(
            mesh.devices.reshape(groups, heads, members // heads), ("grp", "heads", "share")
        )
        tokens = P(("grp", "heads", "share"), None)
        return jax.shard_map(
            local,
            mesh=layout,
            in_specs=(tokens,) * 4 + (P("grp"), P("grp"), P()),
            out_specs=(tokens,) * 3,
            check_vma=False,
        )(query, keys, values, grad_out, valid, views, cross_bias)

    return run
```

```python
import functools
import math

import jax
import jax.numpy as jnp
from jax import lax
from jax.experimental import pallas as pl
from jax.experimental.pallas import tpu as pltpu
from jax.sharding import Mesh, PartitionSpec as P

HD = 64
FRAME = 32
PAIR = 2 * HD
TILE = 128
CHUNK = 128
SUBLANES = 8

SCALE = 0.125
DEAD = -1e30
LOG2E = math.log2(math.e)
LIMIT = 48 * 1024 * 1024

VMEM = pl.BlockSpec(memory_space=pltpu.VMEM)
SMEM = pl.BlockSpec(memory_space=pltpu.SMEM)


def side_by_side(left, right):
    return jnp.concatenate([left, right], axis=1)


def pack_kernel(q_ref, k_ref, v_ref, g_ref, out_ref):
    rows, width = q_ref.shape
    q, k, v, g = q_ref[...], k_ref[...], v_ref[...], g_ref[...]
    for head in range(width // HD):
        at = slice(head * HD, (head + 1) * HD)
        out_ref[head, :rows] = side_by_side(k[:, at], v[:, at])
        out_ref[head, rows:] = side_by_side(q[:, at], g[:, at])


def pack(query, keys, values, grad_out):
    rows, width = query.shape
    return pl.pallas_call(
        pack_kernel,
        out_shape=pltpu.VMEM((width // HD, 2 * rows, PAIR), query.dtype),
        in_specs=[VMEM] * 4,
        out_specs=VMEM,
        name="pack_heads",
    )(query, keys, values, grad_out)


def owners(heads):
    half = heads // 2
    return [which * half + i for i in range(half) for which in range(2)]


def frame_of(homes, shares, per_home, block, home, which):
    share = lax.rem(lax.axis_index("share") + block, shares)
    return (owners(homes)[home] * shares + share) * per_home + which


def query_weights(qg):
    qg = qg.astype(jnp.float32)
    low = lax.broadcasted_iota(jnp.int32, qg.shape, 1) < HD
    return jnp.concatenate(
        [jnp.where(low, qg, 0.0), jnp.where(low, 0.0, qg)], axis=0
    ).astype(jnp.bfloat16)


def products(keys, weights):
    return lax.dot_general(
        keys, weights, (((1,), (1,)), ((), ())), preferred_element_type=jnp.float32
    )


def exponentials(raw, gw):
    raw, gw = (x.reshape(-1, SUBLANES, TILE) for x in (raw, gw))
    top = jnp.max(raw, axis=0)
    expo = jnp.exp2((raw - top) * (SCALE * LOG2E))
    return expo, (top, jnp.sum(expo, axis=0), jnp.sum(expo * gw, axis=0))


def chunk_of(c):
    return slice(c * CHUNK, (c + 1) * CHUNK)


def begin_kernel(shares, mine_ref, valid_ref, views_ref, bias_ref, key_mark_ref,
                 query_mark_ref, weights_ref, flip_ref, expo_ref, gw_ref, stat_ref, keys_ref):
    homes, rows = mine_ref.shape[0], mine_ref.shape[1] // 2
    own = homes * rows
    per_home, per_tile, tiles = rows // FRAME, TILE // rows, own // TILE
    slot = lax.broadcasted_iota(jnp.int32, (FRAME, PAIR), 0)
    lane = lax.broadcasted_iota(jnp.int32, (1, PAIR), 1)

    me = lax.axis_index("heads")
    head = sum(jnp.where(me == owner, i, 0) for i, owner in enumerate(owners(homes)))
    bias = jnp.full((1, PAIR), bias_ref[head] / SCALE, jnp.float32)
    high = bias.astype(jnp.bfloat16).astype(jnp.float32)
    middle = (bias - high).astype(jnp.bfloat16).astype(jnp.float32)
    part = lax.rem(lane, 3)
    parts = jnp.where(part == 0, high, jnp.where(part == 1, middle, bias - high - middle))
    dead = jnp.where(lane == 6, DEAD / SCALE, 0.0)
    of_exo_query = jnp.where(lane < 3, parts, dead)
    of_ego_query = jnp.where((lane >= 3) & (lane < 6), parts, dead)

    for block in range(shares):
        for home in range(homes):
            for which in range(per_home):
                frame = frame_of(homes, shares, per_home, block, home, which)
                start = block * own + home * rows + which * FRAME
                here = slice(start, start + FRAME)
                exo = views_ref[frame] != 0
                first = jnp.where(exo, 3, 0)
                marks = jnp.where((lane >= first) & (lane < first + 3), 1.0, 0.0)
                gone = jnp.where(slot < valid_ref[frame], 0.0, 1.0)
                key_mark_ref[here, :] = jnp.where(lane == 6, gone, marks).astype(jnp.bfloat16)
                query_mark_ref[here, :] = jnp.broadcast_to(
                    jnp.where(exo, of_exo_query, of_ego_query), (FRAME, PAIR)
                ).astype(jnp.bfloat16)

    kv = mine_ref[:, :rows, :].reshape(own, PAIR)
    flip_ref[...] = kv.astype(jnp.float32).T[:HD].astype(jnp.bfloat16)
    keys_ref[:, :PAIR] = kv
    keys_ref[:, PAIR:] = key_mark_ref[:own, :]

    def score(index):
        qg = mine_ref[index * per_tile : (index + 1) * per_tile, rows:, :].reshape(TILE, PAIR)
        marks = query_mark_ref[index * TILE : (index + 1) * TILE, :]
        weights = side_by_side(
            query_weights(qg), jnp.concatenate([marks, jnp.zeros_like(marks)], axis=0)
        )
        weights_ref[index] = weights
        return products(keys_ref[...], weights)

    def leave(index, both):
        gw_ref[index] = both[:, TILE:]
        for c in range(own // CHUNK):
            at = chunk_of(c)
            expo, stats = exponentials(both[at, :TILE], both[at, TILE:])
            expo_ref[index, at, :] = expo.reshape(CHUNK, TILE)
            for which, stat in enumerate(stats):
                stat_ref[index, which, c] = stat

    scored = None
    for step in range(tiles + 1):
        last, scored = scored, score(step) if step < tiles else None
        if step:
            leave(step - 1, last)


def finish_kernel(shares, *refs):
    blocks, refs = refs[:shares], refs[shares:]
    key_mark_ref, query_mark_ref, weights_ref, own_flip_ref = refs[:4]
    expo_ref, gw_ref, stat_ref, out_ref, keys_ref, qg_ref, flip_ref, sum_ref, dq_ref = refs[4:]
    homes, rows = blocks[0].shape[0], blocks[0].shape[1] // 2
    own = homes * rows
    tokens = own * shares
    tiles, chunks, own_chunks = own // TILE, tokens // CHUNK, own // CHUNK

    keys_ref[:, PAIR:] = key_mark_ref[...]
    flip_ref[:, :own] = own_flip_ref[...]
    for block in range(shares):
        here = slice(block * own, (block + 1) * own)
        kv = blocks[block][:, :rows, :].reshape(own, PAIR)
        keys_ref[here, :PAIR] = kv
        if block:
            there = slice((block - 1) * own, block * own)
            flip_ref[:, here] = kv.astype(jnp.float32).T[:HD].astype(jnp.bfloat16)
            qg_ref[there, :] = blocks[block][:, rows:, :].reshape(own, PAIR)
    sum_ref[...] = jnp.zeros_like(sum_ref)

    def score(ours, index):
        if ours:
            weights = weights_ref[index]
            if chunks == own_chunks:
                return weights, None
            return weights, products(keys_ref[own:, :], weights)
        here = pl.ds(pl.multiple_of(index * TILE, TILE), TILE)
        there = pl.ds(pl.multiple_of(own + index * TILE, TILE), TILE)
        marks = query_mark_ref[there, :]
        weights = side_by_side(
            query_weights(qg_ref[here, :]),
            jnp.concatenate([marks, jnp.zeros_like(marks)], axis=0),
        )
        return weights, products(keys_ref[...], weights)

    def all_exponentials(ours, index, both):
        parts = []
        given = own_chunks if ours else 0
        for c in range(given):
            parts.append((None, None, *(stat_ref[index, which, c] for which in range(3))))
        for c in range(chunks - given):
            gw = both[chunk_of(c), TILE:]
            expo, stats = exponentials(both[chunk_of(c), :TILE], gw)
            parts.append((expo, gw.reshape(-1, SUBLANES, TILE), *stats))
        return parts

    def gradients(ours, index, parts):
        expos, gws, tops, totals, mixes = zip(*parts)
        highest = jnp.max(functools.reduce(jnp.maximum, tops), axis=0, keepdims=True)
        factors = [jnp.exp2((top - highest) * (SCALE * LOG2E)) for top in tops]
        total = jnp.sum(sum(f * t for f, t in zip(factors, totals)), axis=0, keepdims=True)
        mixed = jnp.sum(sum(f * m for f, m in zip(factors, mixes)), axis=0, keepdims=True)
        inverse = 1.0 / total
        delta = mixed * inverse
        lows, grads = [], []
        for c in range(chunks if ours else own_chunks):
            expo, gw = expos[c], gws[c]
            if expo is None:
                expo, gw = (
                    ref[index, chunk_of(c), :].reshape(-1, SUBLANES, TILE)
                    for ref in (expo_ref, gw_ref)
                )
            weight = expo * (factors[c] * inverse)
            grad = (weight * SCALE) * (gw - delta)
            grads.append(grad.reshape(CHUNK, TILE).astype(jnp.bfloat16))
            if c < own_chunks:
                lows.append(weight.reshape(CHUNK, TILE).astype(jnp.bfloat16))
        return jnp.concatenate(grads, axis=0), jnp.concatenate(lows, axis=0)

    def leave(ours, first, pair):
        weights, grads, lows = zip(*pair)
        factors = [x for both in zip(grads, lows) for x in (both[0][:own], both[1])]
        sum_ref[...] += jnp.dot(
            jnp.concatenate(factors, axis=1),
            jnp.concatenate([each[:, :PAIR] for each in weights], axis=0),
            preferred_element_type=jnp.float32,
        )
        if ours:
            turned = jnp.dot(
                flip_ref[...], side_by_side(*grads), preferred_element_type=jnp.float32
            )
            here = pl.ds(pl.multiple_of(first * TILE, 2 * TILE), 2 * TILE)
            dq_ref[here, :] = jnp.concatenate([turned, turned], axis=0).T

    def pipeline(work):
        scored, expos, done = {}, {}, {}
        for step in range(len(work) + 2):
            if step < len(work):
                scored[step] = score(*work[step])
            if 0 <= step - 1 < len(work):
                weights, both = scored.pop(step - 1)
                expos[step - 1] = weights, all_exponentials(*work[step - 1], both)
            if 0 <= step - 2:
                weights, parts = expos.pop(step - 2)
                done[step - 2] = (weights, *gradients(*work[step - 2], parts))
                if step % 2:
                    leave(*work[step - 3], (done.pop(step - 3), done.pop(step - 2)))

    others = tiles * (shares - 1)
    if shares <= 2:
        pipeline([(True, i) for i in range(tiles)] + [(False, i) for i in range(others)])
    else:
        pl.loop(0, tiles, step=2)(lambda i: pipeline([(True, i), (True, i + 1)]))
        pl.loop(0, others, step=2)(lambda i: pipeline([(False, i), (False, i + 1)]))
    out_ref[:, :rows, :] = sum_ref[...].astype(jnp.bfloat16).reshape(homes, rows, PAIR)
    for home in range(homes):
        start, half = home * rows, rows // 2
        out_ref[home, rows:, :] = side_by_side(
            dq_ref[start : start + half, :HD], dq_ref[start + half : start + rows, :HD]
        ).astype(jnp.bfloat16)


def attend(mine, others, valid, views, cross_bias):
    shares = len(others) + 1
    homes, both, _ = mine.shape
    rows = both // 2
    own = homes * rows
    tokens, tiles = own * shares, own // TILE
    begun = pl.pallas_call(
        functools.partial(begin_kernel, shares),
        out_shape=(
            pltpu.VMEM((tokens, PAIR), jnp.bfloat16),
            pltpu.VMEM((tokens, PAIR), jnp.bfloat16),
            pltpu.VMEM((tiles, 2 * TILE, 2 * PAIR), jnp.bfloat16),
            pltpu.VMEM((HD, own), jnp.bfloat16),
            pltpu.VMEM((tiles, own, TILE), jnp.float32),
            pltpu.VMEM((tiles, own, TILE), jnp.float32),
            pltpu.VMEM((tiles, 3, own // CHUNK, SUBLANES, TILE), jnp.float32),
        ),
        in_specs=[VMEM] + [SMEM] * 3,
        out_specs=(VMEM,) * 7,
        scratch_shapes=[pltpu.VMEM((own, 2 * PAIR), jnp.bfloat16)],
        compiler_params=pltpu.CompilerParams(vmem_limit_bytes=LIMIT),
        cost_estimate=pl.CostEstimate(
            flops=8 * own * own * PAIR, bytes_accessed=8 * own * own, transcendentals=own * own
        ),
        name="attend_begin",
    )(mine, valid, views, cross_bias)
    return pl.pallas_call(
        functools.partial(finish_kernel, shares),
        out_shape=pltpu.VMEM((homes, rows + rows // 2, PAIR), jnp.bfloat16),
        in_specs=[VMEM] * (shares + 7),
        out_specs=VMEM,
        scratch_shapes=[
            pltpu.VMEM((tokens, 2 * PAIR), jnp.bfloat16),
            pltpu.VMEM((max(tokens - own, TILE), PAIR), jnp.bfloat16),
            pltpu.VMEM((HD, tokens), jnp.bfloat16),
            pltpu.VMEM((own, PAIR), jnp.float32),
            pltpu.VMEM((own, PAIR), jnp.float32),
        ],
        compiler_params=pltpu.CompilerParams(vmem_limit_bytes=LIMIT),
        name="attend_finish",
    )(mine, *others, *begun)


def unpack_kernel(in_ref, dq_ref, dk_ref, dv_ref):
    rows = dq_ref.shape[0]
    half = rows // 2
    for head in range(0, in_ref.shape[0], 2):
        columns = slice(head * HD, (head + 2) * HD)
        one, two = (in_ref[head + which].astype(jnp.float32) for which in (0, 1))
        left = side_by_side(one[:, :HD], two[:, :HD])
        right = side_by_side(one[:, HD:], two[:, HD:])
        dk_ref[:, columns] = left[:rows]
        dv_ref[:, columns] = right[:rows]
        dq_ref[:half, columns] = left[rows:]
        dq_ref[half:, columns] = right[rows:]


def unpack(given, rows):
    shape = jax.ShapeDtypeStruct((rows, given.shape[0] * HD), jnp.float32)
    return pl.pallas_call(
        unpack_kernel,
        out_shape=(shape,) * 3,
        in_specs=[VMEM],
        out_specs=(VMEM,) * 3,
        name="unpack_heads",
    )(pltpu.with_memory_space_constraint(given, pltpu.VMEM))


def local(query, keys, values, grad_out, valid, views, cross_bias):
    swap = functools.partial(
        lax.all_to_all,
        axis_name="heads",
        split_axis=0,
        concat_axis=0,
        tiled=True,
        axis_index_groups=[owners(lax.axis_size("heads"))],
    )
    shares = lax.axis_size("share")
    mine = swap(pack(query, keys, values, grad_out))
    others = [
        lax.ppermute(mine, "share", [((i + k) % shares, i) for i in range(shares)])
        for k in range(1, shares)
    ]
    given = attend(mine, others, valid, views, cross_bias)
    return unpack(swap(given), query.shape[0])


def solution(mesh):
    groups = mesh.shape["grp"]
    members = mesh.shape["blk"] * mesh.shape["head"]

    def run(query, keys, values, grad_out, valid, views, cross_bias):
        heads = query.shape[1] // HD
        layout = Mesh(
            mesh.devices.reshape(groups, heads, members // heads), ("grp", "heads", "share")
        )
        tokens = P(("grp", "heads", "share"), None)
        return jax.shard_map(
            local,
            mesh=layout,
            in_specs=(tokens,) * 4 + (P("grp"), P("grp"), P()),
            out_specs=(tokens,) * 3,
            check_vma=False,
        )(query, keys, values, grad_out, valid, views, cross_bias)

    return run
```

```python
import functools
import math

import jax
import jax.numpy as jnp
from jax import lax
from jax.experimental import pallas as pl
from jax.experimental.pallas import tpu as pltpu
from jax.sharding import Mesh, PartitionSpec as P

HD = 64
FRAME = 32
PAIR = 2 * HD
TILE = 128
CHUNK = 128
SUBLANES = 8

SCALE = 0.125
DEAD = -1e30
LOG2E = math.log2(math.e)
LIMIT = 48 * 1024 * 1024

VMEM = pl.BlockSpec(memory_space=pltpu.VMEM)
SMEM = pl.BlockSpec(memory_space=pltpu.SMEM)


def side_by_side(left, right):
    return jnp.concatenate([left, right], axis=1)


def pack_kernel(q_ref, k_ref, v_ref, g_ref, out_ref):
    rows, width = q_ref.shape
    q, k, v, g = q_ref[...], k_ref[...], v_ref[...], g_ref[...]
    for head in range(width // HD):
        at = slice(head * HD, (head + 1) * HD)
        out_ref[head, :rows] = side_by_side(k[:, at], v[:, at])
        out_ref[head, rows:] = side_by_side(q[:, at], g[:, at])


def pack(query, keys, values, grad_out):
    rows, width = query.shape
    return pl.pallas_call(
        pack_kernel,
        out_shape=pltpu.VMEM((width // HD, 2 * rows, PAIR), query.dtype),
        in_specs=[VMEM] * 4,
        out_specs=VMEM,
        name="pack_heads",
    )(query, keys, values, grad_out)


def frame_of(homes, shares, per_home, block, home, which):
    share = lax.rem(lax.axis_index("share") + block, shares)
    return (home * shares + share) * per_home + which


def query_weights(qg):
    qg = qg.astype(jnp.float32)
    low = lax.broadcasted_iota(jnp.int32, qg.shape, 1) < HD
    return jnp.concatenate(
        [jnp.where(low, qg, 0.0), jnp.where(low, 0.0, qg * SCALE)], axis=0
    ).astype(jnp.bfloat16)


def products(keys, weights):
    return lax.dot_general(
        keys, weights, (((1,), (1,)), ((), ())), preferred_element_type=jnp.float32
    )


def exponentials(raw, gw):
    raw, gw = (x.reshape(-1, SUBLANES, TILE) for x in (raw, gw))
    top = jnp.max(raw, axis=0)
    expo = jnp.exp2((raw - top) * (SCALE * LOG2E))
    return expo, (top, jnp.sum(expo, axis=0), jnp.sum(expo * gw, axis=0))


def chunk_of(c):
    return slice(c * CHUNK, (c + 1) * CHUNK)


def begin_kernel(shares, mine_ref, valid_ref, views_ref, bias_ref, key_mark_ref,
                 query_mark_ref, weights_ref, flip_ref, expo_ref, gw_ref, stat_ref, keys_ref):
    homes, rows = mine_ref.shape[0], mine_ref.shape[1] // 2
    own = homes * rows
    per_home, per_tile, tiles = rows // FRAME, TILE // rows, own // TILE
    slot = lax.broadcasted_iota(jnp.int32, (FRAME, PAIR), 0)
    lane = lax.broadcasted_iota(jnp.int32, (1, PAIR), 1)

    bias = jnp.full((1, PAIR), bias_ref[lax.axis_index("heads")] / SCALE, jnp.float32)
    high = bias.astype(jnp.bfloat16).astype(jnp.float32)
    middle = (bias - high).astype(jnp.bfloat16).astype(jnp.float32)
    part = lax.rem(lane, 3)
    parts = jnp.where(part == 0, high, jnp.where(part == 1, middle, bias - high - middle))
    dead = jnp.where(lane == 6, DEAD / SCALE, 0.0)
    of_exo_query = jnp.where(lane < 3, parts, dead)
    of_ego_query = jnp.where((lane >= 3) & (lane < 6), parts, dead)

    for block in range(shares):
        for home in range(homes):
            for which in range(per_home):
                frame = frame_of(homes, shares, per_home, block, home, which)
                start = block * own + home * rows + which * FRAME
                here = slice(start, start + FRAME)
                exo = views_ref[frame] != 0
                first = jnp.where(exo, 3, 0)
                marks = jnp.where((lane >= first) & (lane < first + 3), 1.0, 0.0)
                gone = jnp.where(slot < valid_ref[frame], 0.0, 1.0)
                key_mark_ref[here, :] = jnp.where(lane == 6, gone, marks).astype(jnp.bfloat16)
                query_mark_ref[here, :] = jnp.broadcast_to(
                    jnp.where(exo, of_exo_query, of_ego_query), (FRAME, PAIR)
                ).astype(jnp.bfloat16)

    kv = mine_ref[:, :rows, :].reshape(own, PAIR)
    flip_ref[...] = kv.astype(jnp.float32).T[:HD].astype(jnp.bfloat16)
    keys_ref[:, :PAIR] = kv
    keys_ref[:, PAIR:] = key_mark_ref[:own, :]

    def score(index):
        qg = mine_ref[index * per_tile : (index + 1) * per_tile, rows:, :].reshape(TILE, PAIR)
        marks = query_mark_ref[index * TILE : (index + 1) * TILE, :]
        weights = side_by_side(
            query_weights(qg), jnp.concatenate([marks, jnp.zeros_like(marks)], axis=0)
        )
        weights_ref[index] = weights
        return products(keys_ref[...], weights)

    def leave(index, both):
        gw_ref[index] = both[:, TILE:]
        for c in range(own // CHUNK):
            at = chunk_of(c)
            expo, stats = exponentials(both[at, :TILE], both[at, TILE:])
            expo_ref[index, at, :] = expo.reshape(CHUNK, TILE)
            for which, stat in enumerate(stats):
                stat_ref[index, which, c] = stat

    scored = None
    for step in range(tiles + 1):
        last, scored = scored, score(step) if step < tiles else None
        if step:
            leave(step - 1, last)


def finish_kernel(shares, *refs):
    blocks, refs = refs[:shares], refs[shares:]
    key_mark_ref, query_mark_ref, weights_ref, own_flip_ref = refs[:4]
    expo_ref, gw_ref, stat_ref, out_ref, keys_ref, qg_ref, flip_ref, sum_ref, dq_ref = refs[4:]
    homes, rows = blocks[0].shape[0], blocks[0].shape[1] // 2
    own = homes * rows
    tokens = own * shares
    tiles, chunks, own_chunks = own // TILE, tokens // CHUNK, own // CHUNK

    keys_ref[:, PAIR:] = key_mark_ref[...]
    flip_ref[:, :own] = own_flip_ref[...]
    for block in range(shares):
        here = slice(block * own, (block + 1) * own)
        kv = blocks[block][:, :rows, :].reshape(own, PAIR)
        keys_ref[here, :PAIR] = kv
        if block:
            there = slice((block - 1) * own, block * own)
            flip_ref[:, here] = kv.astype(jnp.float32).T[:HD].astype(jnp.bfloat16)
            qg_ref[there, :] = blocks[block][:, rows:, :].reshape(own, PAIR)
    sum_ref[...] = jnp.zeros_like(sum_ref)

    def score(ours, index):
        if ours:
            weights = weights_ref[index]
            if chunks == own_chunks:
                return weights, None
            return weights, products(keys_ref[own:, :], weights)
        here = pl.ds(pl.multiple_of(index * TILE, TILE), TILE)
        there = pl.ds(pl.multiple_of(own + index * TILE, TILE), TILE)
        marks = query_mark_ref[there, :]
        weights = side_by_side(
            query_weights(qg_ref[here, :]),
            jnp.concatenate([marks, jnp.zeros_like(marks)], axis=0),
        )
        return weights, products(keys_ref[...], weights)

    def all_exponentials(ours, index, both):
        parts = []
        given = own_chunks if ours else 0
        for c in range(given):
            parts.append((None, None, *(stat_ref[index, which, c] for which in range(3))))
        for c in range(chunks - given):
            gw = both[chunk_of(c), TILE:]
            expo, stats = exponentials(both[chunk_of(c), :TILE], gw)
            parts.append((expo, gw.reshape(-1, SUBLANES, TILE), *stats))
        return parts

    def gradients(ours, index, parts):
        expos, gws, tops, totals, mixes = zip(*parts)
        highest = jnp.max(functools.reduce(jnp.maximum, tops), axis=0, keepdims=True)
        factors = [jnp.exp2((top - highest) * (SCALE * LOG2E)) for top in tops]
        total = jnp.sum(sum(f * t for f, t in zip(factors, totals)), axis=0, keepdims=True)
        mixed = jnp.sum(sum(f * m for f, m in zip(factors, mixes)), axis=0, keepdims=True)
        inverse = 1.0 / total
        delta = mixed * inverse
        lows, grads = [], []
        for c in range(chunks if ours else own_chunks):
            expo, gw = expos[c], gws[c]
            if expo is None:
                expo, gw = (
                    ref[index, chunk_of(c), :].reshape(-1, SUBLANES, TILE)
                    for ref in (expo_ref, gw_ref)
                )
            weight = expo * (factors[c] * inverse)
            grad = weight * (gw - delta)
            grads.append(grad.reshape(CHUNK, TILE).astype(jnp.bfloat16))
            if c < own_chunks:
                lows.append(weight.reshape(CHUNK, TILE).astype(jnp.bfloat16))
        return jnp.concatenate(grads, axis=0), jnp.concatenate(lows, axis=0)

    def leave(ours, first, pair):
        weights, grads, lows = zip(*pair)
        factors = [x for both in zip(grads, lows) for x in (both[0][:own], both[1])]
        sum_ref[...] += jnp.dot(
            jnp.concatenate(factors, axis=1),
            jnp.concatenate([each[:, :PAIR] for each in weights], axis=0),
            preferred_element_type=jnp.float32,
        )
        if ours:
            turned = jnp.dot(
                flip_ref[...], side_by_side(*grads), preferred_element_type=jnp.float32
            )
            here = pl.ds(pl.multiple_of(first * TILE, 2 * TILE), 2 * TILE)
            dq_ref[here, :] = jnp.concatenate([turned, turned], axis=0).T

    def pipeline(work):
        scored, expos, done = {}, {}, {}
        for step in range(len(work) + 2):
            if step < len(work):
                scored[step] = score(*work[step])
            if 0 <= step - 1 < len(work):
                weights, both = scored.pop(step - 1)
                expos[step - 1] = weights, all_exponentials(*work[step - 1], both)
            if 0 <= step - 2:
                weights, parts = expos.pop(step - 2)
                done[step - 2] = (weights, *gradients(*work[step - 2], parts))
                if step % 2:
                    leave(*work[step - 3], (done.pop(step - 3), done.pop(step - 2)))

    others = tiles * (shares - 1)
    if shares <= 2:
        pipeline([(False, i) for i in range(others)] + [(True, i) for i in range(tiles)])
    else:
        pl.loop(0, tiles, step=2)(lambda i: pipeline([(True, i), (True, i + 1)]))
        pl.loop(0, others, step=2)(lambda i: pipeline([(False, i), (False, i + 1)]))
    lane = lax.broadcasted_iota(jnp.int32, (1, PAIR), 1)
    sums = sum_ref[...] * jnp.where(lane < HD, 1.0, 1.0 / SCALE)
    out_ref[:, :rows, :] = sums.astype(jnp.bfloat16).reshape(homes, rows, PAIR)
    for home in range(homes):
        start, half = home * rows, rows // 2
        out_ref[home, rows:, :] = side_by_side(
            dq_ref[start : start + half, :HD], dq_ref[start + half : start + rows, :HD]
        ).astype(jnp.bfloat16)


def attend(mine, others, valid, views, cross_bias):
    shares = len(others) + 1
    homes, both, _ = mine.shape
    rows = both // 2
    own = homes * rows
    tokens, tiles = own * shares, own // TILE
    begun = pl.pallas_call(
        functools.partial(begin_kernel, shares),
        out_shape=(
            pltpu.VMEM((tokens, PAIR), jnp.bfloat16),
            pltpu.VMEM((tokens, PAIR), jnp.bfloat16),
            pltpu.VMEM((tiles, 2 * TILE, 2 * PAIR), jnp.bfloat16),
            pltpu.VMEM((HD, own), jnp.bfloat16),
            pltpu.VMEM((tiles, own, TILE), jnp.float32),
            pltpu.VMEM((tiles, own, TILE), jnp.float32),
            pltpu.VMEM((tiles, 3, own // CHUNK, SUBLANES, TILE), jnp.float32),
        ),
        in_specs=[VMEM] + [SMEM] * 3,
        out_specs=(VMEM,) * 7,
        scratch_shapes=[pltpu.VMEM((own, 2 * PAIR), jnp.bfloat16)],
        compiler_params=pltpu.CompilerParams(vmem_limit_bytes=LIMIT),
        cost_estimate=pl.CostEstimate(
            flops=8 * own * own * PAIR, bytes_accessed=8 * own * own, transcendentals=own * own
        ),
        name="attend_begin",
    )(mine, valid, views, cross_bias)
    return pl.pallas_call(
        functools.partial(finish_kernel, shares),
        out_shape=pltpu.VMEM((homes, rows + rows // 2, PAIR), jnp.bfloat16),
        in_specs=[VMEM] * (shares + 7),
        out_specs=VMEM,
        scratch_shapes=[
            pltpu.VMEM((tokens, 2 * PAIR), jnp.bfloat16),
            pltpu.VMEM((max(tokens - own, TILE), PAIR), jnp.bfloat16),
            pltpu.VMEM((HD, tokens), jnp.bfloat16),
            pltpu.VMEM((own, PAIR), jnp.float32),
            pltpu.VMEM((own, PAIR), jnp.float32),
        ],
        compiler_params=pltpu.CompilerParams(vmem_limit_bytes=LIMIT),
        name="attend_finish",
    )(mine, *others, *begun)


def unpack_kernel(in_ref, dq_ref, dk_ref, dv_ref):
    rows = dq_ref.shape[0]
    half = rows // 2
    for head in range(0, in_ref.shape[0], 2):
        columns = slice(head * HD, (head + 2) * HD)
        one, two = (in_ref[head + which].astype(jnp.float32) for which in (0, 1))
        left = side_by_side(one[:, :HD], two[:, :HD])
        right = side_by_side(one[:, HD:], two[:, HD:])
        dk_ref[:, columns] = left[:rows]
        dv_ref[:, columns] = right[:rows]
        dq_ref[:half, columns] = left[rows:]
        dq_ref[half:, columns] = right[rows:]


def unpack(given, rows):
    shape = jax.ShapeDtypeStruct((rows, given.shape[0] * HD), jnp.float32)
    return pl.pallas_call(
        unpack_kernel,
        out_shape=(shape,) * 3,
        in_specs=[VMEM],
        out_specs=(VMEM,) * 3,
        name="unpack_heads",
    )(pltpu.with_memory_space_constraint(given, pltpu.VMEM))


def local(query, keys, values, grad_out, valid, views, cross_bias):
    swap = functools.partial(
        lax.all_to_all, axis_name="heads", split_axis=0, concat_axis=0, tiled=True
    )
    shares = lax.axis_size("share")
    mine = swap(pack(query, keys, values, grad_out))
    others = [
        lax.ppermute(mine, "share", [((i + k) % shares, i) for i in range(shares)])
        for k in range(1, shares)
    ]
    given = attend(mine, others, valid, views, cross_bias)
    return unpack(swap(given), query.shape[0])


def solution(mesh):
    groups = mesh.shape["grp"]
    members = mesh.shape["blk"] * mesh.shape["head"]

    def run(query, keys, values, grad_out, valid, views, cross_bias):
        heads = query.shape[1] // HD
        layout = Mesh(
            mesh.devices.reshape(groups, heads, members // heads), ("grp", "heads", "share")
        )
        tokens = P(("grp", "heads", "share"), None)
        return jax.shard_map(
            local,
            mesh=layout,
            in_specs=(tokens,) * 4 + (P("grp"), P("grp"), P()),
            out_specs=(tokens,) * 3,
            check_vma=False,
        )(query, keys, values, grad_out, valid, views, cross_bias)

    return run
```

```python
import functools
import math

import jax
import jax.numpy as jnp
from jax import lax
from jax.experimental import pallas as pl
from jax.experimental.pallas import tpu as pltpu
from jax.sharding import Mesh, PartitionSpec as P

HD = 64
FRAME = 32
PAIR = 2 * HD
TILE = 128
CHUNK = 64
SUBLANES = 8

SCALE = 0.125
DEAD = -1e30
LOG2E = math.log2(math.e)
LIMIT = 48 * 1024 * 1024

VMEM = pl.BlockSpec(memory_space=pltpu.VMEM)
SMEM = pl.BlockSpec(memory_space=pltpu.SMEM)


def side_by_side(left, right):
    return jnp.concatenate([left, right], axis=1)


def pack_kernel(q_ref, k_ref, v_ref, g_ref, out_ref):
    rows, width = q_ref.shape
    q, k, v, g = q_ref[...], k_ref[...], v_ref[...], g_ref[...]
    for head in range(width // HD):
        at = slice(head * HD, (head + 1) * HD)
        out_ref[head, :rows] = side_by_side(k[:, at], v[:, at])
        out_ref[head, rows:] = side_by_side(q[:, at], g[:, at])


def pack(query, keys, values, grad_out):
    rows, width = query.shape
    return pl.pallas_call(
        pack_kernel,
        out_shape=pltpu.VMEM((width // HD, 2 * rows, PAIR), query.dtype),
        in_specs=[VMEM] * 4,
        out_specs=VMEM,
        name="pack_heads",
    )(query, keys, values, grad_out)


def frame_of(homes, shares, per_home, block, home, which):
    share = lax.rem(lax.axis_index("share") + block, shares)
    return (home * shares + share) * per_home + which


def query_weights(qg):
    qg = qg.astype(jnp.float32)
    low = lax.broadcasted_iota(jnp.int32, qg.shape, 1) < HD
    return jnp.concatenate(
        [jnp.where(low, qg, 0.0), jnp.where(low, 0.0, qg * SCALE)], axis=0
    ).astype(jnp.bfloat16)


def products(keys, weights):
    return lax.dot_general(
        keys, weights, (((1,), (1,)), ((), ())), preferred_element_type=jnp.float32
    )


def exponentials(raw, gw):
    raw, gw = (x.reshape(-1, SUBLANES, TILE) for x in (raw, gw))
    top = jnp.max(raw, axis=0)
    expo = jnp.exp2((raw - top) * (SCALE * LOG2E))
    return expo, (top, jnp.sum(expo, axis=0), jnp.sum(expo * gw, axis=0))


def chunk_of(c):
    return slice(c * CHUNK, (c + 1) * CHUNK)


def begin_kernel(shares, mine_ref, valid_ref, views_ref, bias_ref, key_mark_ref,
                 query_mark_ref, weights_ref, flip_ref, expo_ref, gw_ref, stat_ref, keys_ref):
    homes, rows = mine_ref.shape[0], mine_ref.shape[1] // 2
    own = homes * rows
    per_home, per_tile, tiles = rows // FRAME, TILE // rows, own // TILE
    slot = lax.broadcasted_iota(jnp.int32, (FRAME, PAIR), 0)
    lane = lax.broadcasted_iota(jnp.int32, (1, PAIR), 1)

    bias = jnp.full((1, PAIR), bias_ref[lax.axis_index("heads")] / SCALE, jnp.float32)
    high = bias.astype(jnp.bfloat16).astype(jnp.float32)
    middle = (bias - high).astype(jnp.bfloat16).astype(jnp.float32)
    part = lax.rem(lane, 3)
    parts = jnp.where(part == 0, high, jnp.where(part == 1, middle, bias - high - middle))
    dead = jnp.where(lane == 6, DEAD / SCALE, 0.0)
    of_exo_query = jnp.where(lane < 3, parts, dead)
    of_ego_query = jnp.where((lane >= 3) & (lane < 6), parts, dead)

    for block in range(shares):
        for home in range(homes):
            for which in range(per_home):
                frame = frame_of(homes, shares, per_home, block, home, which)
                start = block * own + home * rows + which * FRAME
                here = slice(start, start + FRAME)
                exo = views_ref[frame] != 0
                first = jnp.where(exo, 3, 0)
                marks = jnp.where((lane >= first) & (lane < first + 3), 1.0, 0.0)
                gone = jnp.where(slot < valid_ref[frame], 0.0, 1.0)
                key_mark_ref[here, :] = jnp.where(lane == 6, gone, marks).astype(jnp.bfloat16)
                query_mark_ref[here, :] = jnp.broadcast_to(
                    jnp.where(exo, of_exo_query, of_ego_query), (FRAME, PAIR)
                ).astype(jnp.bfloat16)

    kv = mine_ref[:, :rows, :].reshape(own, PAIR)
    flip_ref[...] = kv.astype(jnp.float32).T[:HD].astype(jnp.bfloat16)
    keys_ref[:, :PAIR] = kv
    keys_ref[:, PAIR:] = key_mark_ref[:own, :]

    def score(index):
        qg = mine_ref[index * per_tile : (index + 1) * per_tile, rows:, :].reshape(TILE, PAIR)
        marks = query_mark_ref[index * TILE : (index + 1) * TILE, :]
        weights = side_by_side(
            query_weights(qg), jnp.concatenate([marks, jnp.zeros_like(marks)], axis=0)
        )
        weights_ref[index] = weights
        return products(keys_ref[...], weights)

    def leave(index, both):
        gw_ref[index] = both[:, TILE:]
        for c in range(own // CHUNK):
            at = chunk_of(c)
            expo, stats = exponentials(both[at, :TILE], both[at, TILE:])
            expo_ref[index, at, :] = expo.reshape(CHUNK, TILE)
            for which, stat in enumerate(stats):
                stat_ref[index, which, c] = stat

    scored = None
    for step in range(tiles + 1):
        last, scored = scored, score(step) if step < tiles else None
        if step:
            leave(step - 1, last)


def finish_kernel(shares, *refs):
    blocks, refs = refs[:shares], refs[shares:]
    key_mark_ref, query_mark_ref, weights_ref, own_flip_ref = refs[:4]
    expo_ref, gw_ref, stat_ref, out_ref, keys_ref, qg_ref, flip_ref, sum_ref, dq_ref = refs[4:]
    homes, rows = blocks[0].shape[0], blocks[0].shape[1] // 2
    own = homes * rows
    tokens = own * shares
    tiles, chunks, own_chunks = own // TILE, tokens // CHUNK, own // CHUNK

    keys_ref[:, PAIR:] = key_mark_ref[...]
    flip_ref[:, :own] = own_flip_ref[...]
    for block in range(shares):
        here = slice(block * own, (block + 1) * own)
        kv = blocks[block][:, :rows, :].reshape(own, PAIR)
        keys_ref[here, :PAIR] = kv
        if block:
            there = slice((block - 1) * own, block * own)
            flip_ref[:, here] = kv.astype(jnp.float32).T[:HD].astype(jnp.bfloat16)
            qg_ref[there, :] = blocks[block][:, rows:, :].reshape(own, PAIR)
    sum_ref[...] = jnp.zeros_like(sum_ref)

    def score(ours, index):
        if ours:
            weights = weights_ref[index]
            if chunks == own_chunks:
                return weights, None
            return weights, products(keys_ref[own:, :], weights)
        here = pl.ds(pl.multiple_of(index * TILE, TILE), TILE)
        there = pl.ds(pl.multiple_of(own + index * TILE, TILE), TILE)
        marks = query_mark_ref[there, :]
        weights = side_by_side(
            query_weights(qg_ref[here, :]),
            jnp.concatenate([marks, jnp.zeros_like(marks)], axis=0),
        )
        return weights, products(keys_ref[...], weights)

    def all_exponentials(ours, index, both):
        parts = []
        given = own_chunks if ours else 0
        for c in range(given):
            parts.append((None, None, *(stat_ref[index, which, c] for which in range(3))))
        for c in range(chunks - given):
            gw = both[chunk_of(c), TILE:]
            expo, stats = exponentials(both[chunk_of(c), :TILE], gw)
            parts.append((expo, gw.reshape(-1, SUBLANES, TILE), *stats))
        return parts

    def gradients(ours, index, parts):
        expos, gws, tops, totals, mixes = zip(*parts)
        highest = jnp.max(functools.reduce(jnp.maximum, tops), axis=0, keepdims=True)
        factors = [jnp.exp2((top - highest) * (SCALE * LOG2E)) for top in tops]
        total = jnp.sum(sum(f * t for f, t in zip(factors, totals)), axis=0, keepdims=True)
        mixed = jnp.sum(sum(f * m for f, m in zip(factors, mixes)), axis=0, keepdims=True)
        inverse = 1.0 / total
        delta = mixed * inverse
        lows, grads = [], []
        for c in range(chunks if ours else own_chunks):
            expo, gw = expos[c], gws[c]
            if expo is None:
                expo, gw = (
                    ref[index, chunk_of(c), :].reshape(-1, SUBLANES, TILE)
                    for ref in (expo_ref, gw_ref)
                )
            weight = expo * (factors[c] * inverse)
            grad = weight * (gw - delta)
            grads.append(grad.reshape(CHUNK, TILE).astype(jnp.bfloat16))
            if c < own_chunks:
                lows.append(weight.reshape(CHUNK, TILE).astype(jnp.bfloat16))
        return jnp.concatenate(grads, axis=0), jnp.concatenate(lows, axis=0)

    def leave(ours, first, pair):
        weights, grads, lows = zip(*pair)
        factors = [x for both in zip(grads, lows) for x in (both[0][:own], both[1])]
        sum_ref[...] += jnp.dot(
            jnp.concatenate(factors, axis=1),
            jnp.concatenate([each[:, :PAIR] for each in weights], axis=0),
            preferred_element_type=jnp.float32,
        )
        if ours:
            turned = jnp.dot(
                flip_ref[...], side_by_side(*grads), preferred_element_type=jnp.float32
            )
            here = pl.ds(pl.multiple_of(first * TILE, 2 * TILE), 2 * TILE)
            dq_ref[here, :] = jnp.concatenate([turned, turned], axis=0).T

    def pipeline(work):
        scored, expos, done = {}, {}, {}
        for step in range(len(work) + 2):
            if step < len(work):
                scored[step] = score(*work[step])
            if 0 <= step - 1 < len(work):
                weights, both = scored.pop(step - 1)
                expos[step - 1] = weights, all_exponentials(*work[step - 1], both)
            if 0 <= step - 2:
                weights, parts = expos.pop(step - 2)
                done[step - 2] = (weights, *gradients(*work[step - 2], parts))
                if step % 2:
                    leave(*work[step - 3], (done.pop(step - 3), done.pop(step - 2)))

    others = tiles * (shares - 1)
    if shares <= 2:
        pipeline([(False, i) for i in range(others)] + [(True, i) for i in range(tiles)])
    else:
        pl.loop(0, tiles, step=2)(lambda i: pipeline([(True, i), (True, i + 1)]))
        pl.loop(0, others, step=2)(lambda i: pipeline([(False, i), (False, i + 1)]))
    lane = lax.broadcasted_iota(jnp.int32, (1, PAIR), 1)
    sums = sum_ref[...] * jnp.where(lane < HD, 1.0, 1.0 / SCALE)
    out_ref[:, :rows, :] = sums.astype(jnp.bfloat16).reshape(homes, rows, PAIR)
    for home in range(homes):
        start, half = home * rows, rows // 2
        out_ref[home, rows:, :] = side_by_side(
            dq_ref[start : start + half, :HD], dq_ref[start + half : start + rows, :HD]
        ).astype(jnp.bfloat16)


def attend(mine, others, valid, views, cross_bias):
    shares = len(others) + 1
    homes, both, _ = mine.shape
    rows = both // 2
    own = homes * rows
    tokens, tiles = own * shares, own // TILE
    begun = pl.pallas_call(
        functools.partial(begin_kernel, shares),
        out_shape=(
            pltpu.VMEM((tokens, PAIR), jnp.bfloat16),
            pltpu.VMEM((tokens, PAIR), jnp.bfloat16),
            pltpu.VMEM((tiles, 2 * TILE, 2 * PAIR), jnp.bfloat16),
            pltpu.VMEM((HD, own), jnp.bfloat16),
            pltpu.VMEM((tiles, own, TILE), jnp.float32),
            pltpu.VMEM((tiles, own, TILE), jnp.float32),
            pltpu.VMEM((tiles, 3, own // CHUNK, SUBLANES, TILE), jnp.float32),
        ),
        in_specs=[VMEM] + [SMEM] * 3,
        out_specs=(VMEM,) * 7,
        scratch_shapes=[pltpu.VMEM((own, 2 * PAIR), jnp.bfloat16)],
        compiler_params=pltpu.CompilerParams(vmem_limit_bytes=LIMIT),
        cost_estimate=pl.CostEstimate(
            flops=8 * own * own * PAIR, bytes_accessed=8 * own * own, transcendentals=own * own
        ),
        name="attend_begin",
    )(mine, valid, views, cross_bias)
    return pl.pallas_call(
        functools.partial(finish_kernel, shares),
        out_shape=pltpu.VMEM((homes, rows + rows // 2, PAIR), jnp.bfloat16),
        in_specs=[VMEM] * (shares + 7),
        out_specs=VMEM,
        scratch_shapes=[
            pltpu.VMEM((tokens, 2 * PAIR), jnp.bfloat16),
            pltpu.VMEM((max(tokens - own, TILE), PAIR), jnp.bfloat16),
            pltpu.VMEM((HD, tokens), jnp.bfloat16),
            pltpu.VMEM((own, PAIR), jnp.float32),
            pltpu.VMEM((own, PAIR), jnp.float32),
        ],
        compiler_params=pltpu.CompilerParams(vmem_limit_bytes=LIMIT),
        name="attend_finish",
    )(mine, *others, *begun)


def unpack_kernel(in_ref, dq_ref, dk_ref, dv_ref):
    rows = dq_ref.shape[0]
    half = rows // 2
    for head in range(0, in_ref.shape[0], 2):
        columns = slice(head * HD, (head + 2) * HD)
        one, two = (in_ref[head + which].astype(jnp.float32) for which in (0, 1))
        left = side_by_side(one[:, :HD], two[:, :HD])
        right = side_by_side(one[:, HD:], two[:, HD:])
        dk_ref[:, columns] = left[:rows]
        dv_ref[:, columns] = right[:rows]
        dq_ref[:half, columns] = left[rows:]
        dq_ref[half:, columns] = right[rows:]


def unpack(given, rows):
    shape = jax.ShapeDtypeStruct((rows, given.shape[0] * HD), jnp.float32)
    return pl.pallas_call(
        unpack_kernel,
        out_shape=(shape,) * 3,
        in_specs=[VMEM],
        out_specs=(VMEM,) * 3,
        name="unpack_heads",
    )(pltpu.with_memory_space_constraint(given, pltpu.VMEM))


def local(query, keys, values, grad_out, valid, views, cross_bias):
    swap = functools.partial(
        lax.all_to_all, axis_name="heads", split_axis=0, concat_axis=0, tiled=True
    )
    shares = lax.axis_size("share")
    mine = swap(pack(query, keys, values, grad_out))
    others = [
        lax.ppermute(mine, "share", [((i + k) % shares, i) for i in range(shares)])
        for k in range(1, shares)
    ]
    given = attend(mine, others, valid, views, cross_bias)
    return unpack(swap(given), query.shape[0])


def solution(mesh):
    groups = mesh.shape["grp"]
    members = mesh.shape["blk"] * mesh.shape["head"]

    def run(query, keys, values, grad_out, valid, views, cross_bias):
        heads = query.shape[1] // HD
        layout = Mesh(
            mesh.devices.reshape(groups, heads, members // heads), ("grp", "heads", "share")
        )
        tokens = P(("grp", "heads", "share"), None)
        return jax.shard_map(
            local,
            mesh=layout,
            in_specs=(tokens,) * 4 + (P("grp"), P("grp"), P()),
            out_specs=(tokens,) * 3,
            check_vma=False,
        )(query, keys, values, grad_out, valid, views, cross_bias)

    return run
```

```python
import functools
import math

import jax
import jax.numpy as jnp
from jax import lax
from jax.experimental import pallas as pl
from jax.experimental.pallas import tpu as pltpu
from jax.sharding import Mesh, PartitionSpec as P

HD = 64
FRAME = 32
PAIR = 2 * HD
TILE = 128
CHUNK = 128
SUBLANES = 8

SCALE = 0.125
DEAD = -1e30
LOG2E = math.log2(math.e)
LIMIT = 48 * 1024 * 1024

VMEM = pl.BlockSpec(memory_space=pltpu.VMEM)
SMEM = pl.BlockSpec(memory_space=pltpu.SMEM)


def side_by_side(left, right):
    return jnp.concatenate([left, right], axis=1)


def pack_kernel(q_ref, k_ref, v_ref, g_ref, out_ref):
    rows, width = q_ref.shape
    q, k, v, g = q_ref[...], k_ref[...], v_ref[...], g_ref[...]
    for head in range(width // HD):
        at = slice(head * HD, (head + 1) * HD)
        out_ref[head, :rows] = side_by_side(k[:, at], v[:, at])
        out_ref[head, rows:] = side_by_side(q[:, at], g[:, at])


def pack(query, keys, values, grad_out):
    rows, width = query.shape
    return pl.pallas_call(
        pack_kernel,
        out_shape=pltpu.VMEM((width // HD, 2 * rows, PAIR), query.dtype),
        in_specs=[VMEM] * 4,
        out_specs=VMEM,
        name="pack_heads",
    )(query, keys, values, grad_out)


def frame_of(homes, shares, per_home, block, home, which):
    share = lax.rem(lax.axis_index("share") + block, shares)
    return (home * shares + share) * per_home + which


def query_weights(qg):
    qg = qg.astype(jnp.float32)
    low = lax.broadcasted_iota(jnp.int32, qg.shape, 1) < HD
    return jnp.concatenate(
        [jnp.where(low, qg, 0.0), jnp.where(low, 0.0, qg * SCALE)], axis=0
    ).astype(jnp.bfloat16)


def products(keys, weights):
    return lax.dot_general(
        keys, weights, (((1,), (1,)), ((), ())), preferred_element_type=jnp.float32
    )


def exponentials(raw, gw):
    raw, gw = (x.reshape(-1, SUBLANES, TILE) for x in (raw, gw))
    top = jnp.max(raw, axis=0)
    expo = jnp.exp2((raw - top) * (SCALE * LOG2E))
    return expo, (top, jnp.sum(expo, axis=0), jnp.sum(expo * gw, axis=0))


def chunk_of(c):
    return slice(c * CHUNK, (c + 1) * CHUNK)


def begin_kernel(shares, mine_ref, valid_ref, views_ref, bias_ref, key_mark_ref,
                 query_mark_ref, weights_ref, flip_ref, expo_ref, gw_ref, stat_ref, keys_ref):
    homes, rows = mine_ref.shape[0], mine_ref.shape[1] // 2
    own = homes * rows
    per_home, per_tile, tiles = rows // FRAME, TILE // rows, own // TILE
    slot = lax.broadcasted_iota(jnp.int32, (FRAME, PAIR), 0)
    lane = lax.broadcasted_iota(jnp.int32, (1, PAIR), 1)

    bias = jnp.full((1, PAIR), bias_ref[lax.axis_index("heads")] / SCALE, jnp.float32)
    high = bias.astype(jnp.bfloat16).astype(jnp.float32)
    middle = (bias - high).astype(jnp.bfloat16).astype(jnp.float32)
    part = lax.rem(lane, 3)
    parts = jnp.where(part == 0, high, jnp.where(part == 1, middle, bias - high - middle))
    dead = jnp.where(lane == 6, DEAD / SCALE, 0.0)
    of_exo_query = jnp.where(lane < 3, parts, dead)
    of_ego_query = jnp.where((lane >= 3) & (lane < 6), parts, dead)

    for block in range(shares):
        for home in range(homes):
            for which in range(per_home):
                frame = frame_of(homes, shares, per_home, block, home, which)
                start = block * own + home * rows + which * FRAME
                here = slice(start, start + FRAME)
                exo = views_ref[frame] != 0
                first = jnp.where(exo, 3, 0)
                marks = jnp.where((lane >= first) & (lane < first + 3), 1.0, 0.0)
                gone = jnp.where(slot < valid_ref[frame], 0.0, 1.0)
                key_mark_ref[here, :] = jnp.where(lane == 6, gone, marks).astype(jnp.bfloat16)
                query_mark_ref[here, :] = jnp.broadcast_to(
                    jnp.where(exo, of_exo_query, of_ego_query), (FRAME, PAIR)
                ).astype(jnp.bfloat16)

    kv = mine_ref[:, :rows, :].reshape(own, PAIR)
    flip_ref[...] = kv.astype(jnp.float32).T[:HD].astype(jnp.bfloat16)
    keys_ref[:, :PAIR] = kv
    keys_ref[:, PAIR:] = key_mark_ref[:own, :]

    def score(index):
        qg = mine_ref[index * per_tile : (index + 1) * per_tile, rows:, :].reshape(TILE, PAIR)
        marks = query_mark_ref[index * TILE : (index + 1) * TILE, :]
        weights = side_by_side(
            query_weights(qg), jnp.concatenate([marks, jnp.zeros_like(marks)], axis=0)
        )
        weights_ref[index] = weights
        return products(keys_ref[...], weights)

    def leave(index, both):
        gw_ref[index] = both[:, TILE:]
        for c in range(own // CHUNK):
            at = chunk_of(c)
            expo, stats = exponentials(both[at, :TILE], both[at, TILE:])
            expo_ref[index, at, :] = expo.reshape(CHUNK, TILE)
            for which, stat in enumerate(stats):
                stat_ref[index, which, c] = stat

    scored = None
    for step in range(tiles + 1):
        last, scored = scored, score(step) if step < tiles else None
        if step:
            leave(step - 1, last)


def finish_kernel(shares, *refs):
    blocks, refs = refs[:shares], refs[shares:]
    key_mark_ref, query_mark_ref, weights_ref, own_flip_ref = refs[:4]
    expo_ref, gw_ref, stat_ref, out_ref, keys_ref, qg_ref, flip_ref, sum_ref, dq_ref = refs[4:]
    homes, rows = blocks[0].shape[0], blocks[0].shape[1] // 2
    own = homes * rows
    tokens = own * shares
    tiles, chunks, own_chunks = own // TILE, tokens // CHUNK, own // CHUNK

    keys_ref[:, PAIR:] = key_mark_ref[...]
    flip_ref[:, :own] = own_flip_ref[...]
    for block in range(shares):
        here = slice(block * own, (block + 1) * own)
        kv = blocks[block][:, :rows, :].reshape(own, PAIR)
        keys_ref[here, :PAIR] = kv
        if block:
            there = slice((block - 1) * own, block * own)
            flip_ref[:, here] = kv.astype(jnp.float32).T[:HD].astype(jnp.bfloat16)
            qg_ref[there, :] = blocks[block][:, rows:, :].reshape(own, PAIR)
    sum_ref[...] = jnp.zeros_like(sum_ref)

    def score(ours, index):
        if ours:
            weights = weights_ref[index]
            if chunks == own_chunks:
                return weights, None
            return weights, products(keys_ref[own:, :], weights)
        here = pl.ds(pl.multiple_of(index * TILE, TILE), TILE)
        there = pl.ds(pl.multiple_of(own + index * TILE, TILE), TILE)
        marks = query_mark_ref[there, :]
        weights = side_by_side(
            query_weights(qg_ref[here, :]),
            jnp.concatenate([marks, jnp.zeros_like(marks)], axis=0),
        )
        return weights, products(keys_ref[...], weights)

    def all_exponentials(ours, index, both):
        parts = []
        given = own_chunks if ours else 0
        for c in range(given):
            parts.append((None, None, *(stat_ref[index, which, c] for which in range(3))))
        for c in range(chunks - given):
            gw = both[chunk_of(c), TILE:]
            expo, stats = exponentials(both[chunk_of(c), :TILE], gw)
            parts.append((expo, gw.reshape(-1, SUBLANES, TILE), *stats))
        return parts

    def gradients(ours, index, parts):
        expos, gws, tops, totals, mixes = zip(*parts)
        highest = jnp.max(functools.reduce(jnp.maximum, tops), axis=0, keepdims=True)
        factors = [jnp.exp2((top - highest) * (SCALE * LOG2E)) for top in tops]
        total = jnp.sum(sum(f * t for f, t in zip(factors, totals)), axis=0, keepdims=True)
        mixed = jnp.sum(sum(f * m for f, m in zip(factors, mixes)), axis=0, keepdims=True)
        inverse = 1.0 / total
        delta = mixed * inverse
        lows, grads = [], []
        for c in range(chunks if ours else own_chunks):
            expo, gw = expos[c], gws[c]
            if expo is None:
                expo, gw = (
                    ref[index, chunk_of(c), :].reshape(-1, SUBLANES, TILE)
                    for ref in (expo_ref, gw_ref)
                )
            weight = expo * (factors[c] * inverse)
            grad = weight * (gw - delta)
            grads.append(grad.reshape(CHUNK, TILE).astype(jnp.bfloat16))
            if c < own_chunks:
                lows.append(weight.reshape(CHUNK, TILE).astype(jnp.bfloat16))
        return jnp.concatenate(grads, axis=0), jnp.concatenate(lows, axis=0)

    def leave(ours, first, pair):
        weights, grads, lows = zip(*pair)
        factors = [x for both in zip(grads, lows) for x in (both[0][:own], both[1])]
        sum_ref[...] += jnp.dot(
            jnp.concatenate(factors, axis=1),
            jnp.concatenate([each[:, :PAIR] for each in weights], axis=0),
            preferred_element_type=jnp.float32,
        )
        if ours:
            turned = jnp.dot(
                flip_ref[...], side_by_side(*grads), preferred_element_type=jnp.float32
            )
            here = pl.ds(pl.multiple_of(first * TILE, 2 * TILE), 2 * TILE)
            dq_ref[here, :] = jnp.concatenate([turned, turned], axis=0).T

    def pipeline(work):
        scored, expos, done = {}, {}, {}
        for step in range(len(work) + 3):
            if step < len(work):
                scored[step] = score(*work[step])
            if 4 <= step and step % 2 == 0:
                leave(*work[step - 4], (done.pop(step - 4), done.pop(step - 3)))
            if 0 <= step - 1 < len(work):
                weights, both = scored.pop(step - 1)
                expos[step - 1] = weights, all_exponentials(*work[step - 1], both)
            if 0 <= step - 2 < len(work):
                weights, parts = expos.pop(step - 2)
                done[step - 2] = (weights, *gradients(*work[step - 2], parts))

    others = tiles * (shares - 1)
    if shares <= 2:
        pipeline([(False, i) for i in range(others)] + [(True, i) for i in range(tiles)])
    else:
        pl.loop(0, tiles, step=2)(lambda i: pipeline([(True, i), (True, i + 1)]))
        pl.loop(0, others, step=2)(lambda i: pipeline([(False, i), (False, i + 1)]))
    lane = lax.broadcasted_iota(jnp.int32, (1, PAIR), 1)
    sums = sum_ref[...] * jnp.where(lane < HD, 1.0, 1.0 / SCALE)
    out_ref[:, :rows, :] = sums.astype(jnp.bfloat16).reshape(homes, rows, PAIR)
    for home in range(homes):
        start, half = home * rows, rows // 2
        out_ref[home, rows:, :] = side_by_side(
            dq_ref[start : start + half, :HD], dq_ref[start + half : start + rows, :HD]
        ).astype(jnp.bfloat16)


def attend(mine, others, valid, views, cross_bias):
    shares = len(others) + 1
    homes, both, _ = mine.shape
    rows = both // 2
    own = homes * rows
    tokens, tiles = own * shares, own // TILE
    begun = pl.pallas_call(
        functools.partial(begin_kernel, shares),
        out_shape=(
            pltpu.VMEM((tokens, PAIR), jnp.bfloat16),
            pltpu.VMEM((tokens, PAIR), jnp.bfloat16),
            pltpu.VMEM((tiles, 2 * TILE, 2 * PAIR), jnp.bfloat16),
            pltpu.VMEM((HD, own), jnp.bfloat16),
            pltpu.VMEM((tiles, own, TILE), jnp.float32),
            pltpu.VMEM((tiles, own, TILE), jnp.float32),
            pltpu.VMEM((tiles, 3, own // CHUNK, SUBLANES, TILE), jnp.float32),
        ),
        in_specs=[VMEM] + [SMEM] * 3,
        out_specs=(VMEM,) * 7,
        scratch_shapes=[pltpu.VMEM((own, 2 * PAIR), jnp.bfloat16)],
        compiler_params=pltpu.CompilerParams(vmem_limit_bytes=LIMIT),
        cost_estimate=pl.CostEstimate(
            flops=8 * own * own * PAIR, bytes_accessed=8 * own * own, transcendentals=own * own
        ),
        name="attend_begin",
    )(mine, valid, views, cross_bias)
    return pl.pallas_call(
        functools.partial(finish_kernel, shares),
        out_shape=pltpu.VMEM((homes, rows + rows // 2, PAIR), jnp.bfloat16),
        in_specs=[VMEM] * (shares + 7),
        out_specs=VMEM,
        scratch_shapes=[
            pltpu.VMEM((tokens, 2 * PAIR), jnp.bfloat16),
            pltpu.VMEM((max(tokens - own, TILE), PAIR), jnp.bfloat16),
            pltpu.VMEM((HD, tokens), jnp.bfloat16),
            pltpu.VMEM((own, PAIR), jnp.float32),
            pltpu.VMEM((own, PAIR), jnp.float32),
        ],
        compiler_params=pltpu.CompilerParams(vmem_limit_bytes=LIMIT),
        name="attend_finish",
    )(mine, *others, *begun)


def unpack_kernel(in_ref, dq_ref, dk_ref, dv_ref):
    rows = dq_ref.shape[0]
    half = rows // 2
    for head in range(0, in_ref.shape[0], 2):
        columns = slice(head * HD, (head + 2) * HD)
        one, two = (in_ref[head + which].astype(jnp.float32) for which in (0, 1))
        left = side_by_side(one[:, :HD], two[:, :HD])
        right = side_by_side(one[:, HD:], two[:, HD:])
        dk_ref[:, columns] = left[:rows]
        dv_ref[:, columns] = right[:rows]
        dq_ref[:half, columns] = left[rows:]
        dq_ref[half:, columns] = right[rows:]


def unpack(given, rows):
    shape = jax.ShapeDtypeStruct((rows, given.shape[0] * HD), jnp.float32)
    return pl.pallas_call(
        unpack_kernel,
        out_shape=(shape,) * 3,
        in_specs=[VMEM],
        out_specs=(VMEM,) * 3,
        name="unpack_heads",
    )(pltpu.with_memory_space_constraint(given, pltpu.VMEM))


def local(query, keys, values, grad_out, valid, views, cross_bias):
    swap = functools.partial(
        lax.all_to_all, axis_name="heads", split_axis=0, concat_axis=0, tiled=True
    )
    shares = lax.axis_size("share")
    mine = swap(pack(query, keys, values, grad_out))
    others = [
        lax.ppermute(mine, "share", [((i + k) % shares, i) for i in range(shares)])
        for k in range(1, shares)
    ]
    given = attend(mine, others, valid, views, cross_bias)
    return unpack(swap(given), query.shape[0])


def solution(mesh):
    groups = mesh.shape["grp"]
    members = mesh.shape["blk"] * mesh.shape["head"]

    def run(query, keys, values, grad_out, valid, views, cross_bias):
        heads = query.shape[1] // HD
        layout = Mesh(
            mesh.devices.reshape(groups, heads, members // heads), ("grp", "heads", "share")
        )
        tokens = P(("grp", "heads", "share"), None)
        return jax.shard_map(
            local,
            mesh=layout,
            in_specs=(tokens,) * 4 + (P("grp"), P("grp"), P()),
            out_specs=(tokens,) * 3,
            check_vma=False,
        )(query, keys, values, grad_out, valid, views, cross_bias)

    return run
```

```python
import functools
import math

import jax
import jax.numpy as jnp
from jax import lax
from jax.experimental import pallas as pl
from jax.experimental.pallas import tpu as pltpu
from jax.sharding import Mesh, PartitionSpec as P

HD = 64
FRAME = 32
PAIR = 2 * HD
TILE = 128
CHUNK = 128
SUBLANES = 8

SCALE = 0.125
DEAD = -1e30
LOG2E = math.log2(math.e)
LIMIT = 48 * 1024 * 1024

VMEM = pl.BlockSpec(memory_space=pltpu.VMEM)
SMEM = pl.BlockSpec(memory_space=pltpu.SMEM)


def side_by_side(left, right):
    return jnp.concatenate([left, right], axis=1)


def pack_kernel(q_ref, k_ref, v_ref, g_ref, out_ref):
    rows, width = q_ref.shape
    q, k, v, g = q_ref[...], k_ref[...], v_ref[...], g_ref[...]
    for head in range(width // HD):
        at = slice(head * HD, (head + 1) * HD)
        out_ref[head, :rows] = side_by_side(k[:, at], v[:, at])
        out_ref[head, rows:] = side_by_side(q[:, at], g[:, at])


def pack(query, keys, values, grad_out):
    rows, width = query.shape
    return pl.pallas_call(
        pack_kernel,
        out_shape=pltpu.VMEM((width // HD, 2 * rows, PAIR), query.dtype),
        in_specs=[VMEM] * 4,
        out_specs=VMEM,
        name="pack_heads",
    )(query, keys, values, grad_out)


def frame_of(homes, shares, per_home, block, home, which):
    share = lax.rem(lax.axis_index("share") + block, shares)
    return (home * shares + share) * per_home + which


def query_weights(qg):
    qg = qg.astype(jnp.float32)
    low = lax.broadcasted_iota(jnp.int32, qg.shape, 1) < HD
    return jnp.concatenate(
        [jnp.where(low, qg, 0.0), jnp.where(low, 0.0, qg * SCALE)], axis=0
    ).astype(jnp.bfloat16)


def products(keys, weights):
    return lax.dot_general(
        keys, weights, (((1,), (1,)), ((), ())), preferred_element_type=jnp.float32
    )


def exponentials(raw, gw):
    raw, gw = (x.reshape(-1, SUBLANES, TILE) for x in (raw, gw))
    top = jnp.max(raw, axis=0)
    expo = jnp.exp2((raw - top) * (SCALE * LOG2E))
    return expo, (top, jnp.sum(expo, axis=0), jnp.sum(expo * gw, axis=0))


def chunk_of(c):
    return slice(c * CHUNK, (c + 1) * CHUNK)


def begin_kernel(shares, mine_ref, valid_ref, views_ref, bias_ref, key_mark_ref,
                 query_mark_ref, weights_ref, flip_ref, expo_ref, gw_ref, stat_ref, keys_ref):
    homes, rows = mine_ref.shape[0], mine_ref.shape[1] // 2
    own = homes * rows
    per_home, per_tile, tiles = rows // FRAME, TILE // rows, own // TILE
    slot = lax.broadcasted_iota(jnp.int32, (FRAME, PAIR), 0)
    lane = lax.broadcasted_iota(jnp.int32, (1, PAIR), 1)

    bias = jnp.full((1, PAIR), bias_ref[lax.axis_index("heads")] / SCALE, jnp.float32)
    high = bias.astype(jnp.bfloat16).astype(jnp.float32)
    middle = (bias - high).astype(jnp.bfloat16).astype(jnp.float32)
    part = lax.rem(lane, 3)
    parts = jnp.where(part == 0, high, jnp.where(part == 1, middle, bias - high - middle))
    dead = jnp.where(lane == 6, DEAD / SCALE, 0.0)
    of_exo_query = jnp.where(lane < 3, parts, dead)
    of_ego_query = jnp.where((lane >= 3) & (lane < 6), parts, dead)

    for block in range(shares):
        for home in range(homes):
            for which in range(per_home):
                frame = frame_of(homes, shares, per_home, block, home, which)
                start = block * own + home * rows + which * FRAME
                here = slice(start, start + FRAME)
                exo = views_ref[frame] != 0
                first = jnp.where(exo, 3, 0)
                marks = jnp.where((lane >= first) & (lane < first + 3), 1.0, 0.0)
                gone = jnp.where(slot < valid_ref[frame], 0.0, 1.0)
                key_mark_ref[here, :] = jnp.where(lane == 6, gone, marks).astype(jnp.bfloat16)
                query_mark_ref[here, :] = jnp.broadcast_to(
                    jnp.where(exo, of_exo_query, of_ego_query), (FRAME, PAIR)
                ).astype(jnp.bfloat16)

    kv = mine_ref[:, :rows, :].reshape(own, PAIR)
    flip_ref[...] = kv.astype(jnp.float32).T[:HD].astype(jnp.bfloat16)
    keys_ref[:, :PAIR] = kv
    keys_ref[:, PAIR:] = key_mark_ref[:own, :]

    def score(index):
        qg = mine_ref[index * per_tile : (index + 1) * per_tile, rows:, :].reshape(TILE, PAIR)
        marks = query_mark_ref[index * TILE : (index + 1) * TILE, :]
        weights = side_by_side(
            query_weights(qg), jnp.concatenate([marks, jnp.zeros_like(marks)], axis=0)
        )
        weights_ref[index] = weights
        return products(keys_ref[...], weights)

    def leave(index, both):
        gw_ref[index] = both[:, TILE:]
        for c in range(own // CHUNK):
            at = chunk_of(c)
            expo, stats = exponentials(both[at, :TILE], both[at, TILE:])
            expo_ref[index, at, :] = expo.reshape(CHUNK, TILE)
            for which, stat in enumerate(stats):
                stat_ref[index, which, c] = stat

    scored = None
    for step in range(tiles + 1):
        last, scored = scored, score(step) if step < tiles else None
        if step:
            leave(step - 1, last)


def finish_kernel(shares, *refs):
    blocks, refs = refs[:shares], refs[shares:]
    key_mark_ref, query_mark_ref, weights_ref, own_flip_ref = refs[:4]
    expo_ref, gw_ref, stat_ref, out_ref, keys_ref, qg_ref, flip_ref, sum_ref, dq_ref = refs[4:]
    homes, rows = blocks[0].shape[0], blocks[0].shape[1] // 2
    own = homes * rows
    tokens = own * shares
    tiles, chunks, own_chunks = own // TILE, tokens // CHUNK, own // CHUNK

    keys_ref[:, PAIR:] = key_mark_ref[...]
    flip_ref[:, :own] = own_flip_ref[...]
    for block in range(shares):
        here = slice(block * own, (block + 1) * own)
        kv = blocks[block][:, :rows, :].reshape(own, PAIR)
        keys_ref[here, :PAIR] = kv
        if block:
            there = slice((block - 1) * own, block * own)
            flip_ref[:, here] = kv.astype(jnp.float32).T[:HD].astype(jnp.bfloat16)
            qg_ref[there, :] = blocks[block][:, rows:, :].reshape(own, PAIR)
    sum_ref[...] = jnp.zeros_like(sum_ref)

    def score(ours, index):
        if ours:
            weights = weights_ref[index]
            if chunks == own_chunks:
                return weights, None
            return weights, products(keys_ref[own:, :], weights)
        here = pl.ds(pl.multiple_of(index * TILE, TILE), TILE)
        there = pl.ds(pl.multiple_of(own + index * TILE, TILE), TILE)
        marks = query_mark_ref[there, :]
        weights = side_by_side(
            query_weights(qg_ref[here, :]),
            jnp.concatenate([marks, jnp.zeros_like(marks)], axis=0),
        )
        return weights, products(keys_ref[...], weights)

    def all_exponentials(ours, index, both):
        parts = []
        given = own_chunks if ours else 0
        for c in range(given):
            parts.append((None, None, *(stat_ref[index, which, c] for which in range(3))))
        for c in range(chunks - given):
            gw = both[chunk_of(c), TILE:]
            expo, stats = exponentials(both[chunk_of(c), :TILE], gw)
            parts.append((expo, gw.reshape(-1, SUBLANES, TILE), *stats))
        return parts

    def gradients(ours, index, parts):
        expos, gws, tops, totals, mixes = zip(*parts)
        highest = jnp.max(functools.reduce(jnp.maximum, tops), axis=0, keepdims=True)
        factors = [jnp.exp2((top - highest) * (SCALE * LOG2E)) for top in tops]
        total = jnp.sum(sum(f * t for f, t in zip(factors, totals)), axis=0, keepdims=True)
        mixed = jnp.sum(sum(f * m for f, m in zip(factors, mixes)), axis=0, keepdims=True)
        inverse = 1.0 / total
        delta = mixed * inverse
        lows, grads = [], []
        for c in range(chunks if ours else own_chunks):
            expo, gw = expos[c], gws[c]
            if expo is None:
                expo, gw = (
                    ref[index, chunk_of(c), :].reshape(-1, SUBLANES, TILE)
                    for ref in (expo_ref, gw_ref)
                )
            weight = expo * (factors[c] * inverse)
            grad = weight * (gw - delta)
            grads.append(grad.reshape(CHUNK, TILE).astype(jnp.bfloat16))
            if c < own_chunks:
                lows.append(weight.reshape(CHUNK, TILE).astype(jnp.bfloat16))
        return jnp.concatenate(grads, axis=0), jnp.concatenate(lows, axis=0)

    def leave(ours, first, pair):
        weights, grads, lows = zip(*pair)
        factors = [x for both in zip(grads, lows) for x in (both[0][:own], both[1])]
        sum_ref[...] += jnp.dot(
            jnp.concatenate(factors, axis=1),
            jnp.concatenate([each[:, :PAIR] for each in weights], axis=0),
            preferred_element_type=jnp.float32,
        )
        if ours:
            turned = jnp.dot(
                flip_ref[...], side_by_side(*grads), preferred_element_type=jnp.float32
            )
            here = pl.ds(pl.multiple_of(first * TILE, 2 * TILE), 2 * TILE)
            dq_ref[here, :] = jnp.concatenate([turned, turned], axis=0).T

    def pipeline(work):
        scored, expos, done = {}, {}, {}
        for step in range(len(work) + 2):
            if step < len(work):
                scored[step] = score(*work[step])
            if 0 <= step - 1 < len(work):
                weights, both = scored.pop(step - 1)
                expos[step - 1] = weights, all_exponentials(*work[step - 1], both)
            if 0 <= step - 2:
                weights, parts = expos.pop(step - 2)
                done[step - 2] = (weights, *gradients(*work[step - 2], parts))
                if step % 2:
                    leave(*work[step - 3], (done.pop(step - 3), done.pop(step - 2)))

    others = tiles * (shares - 1)
    if shares <= 2:
        work = [[(False, i), (False, i + 1)] for i in range(0, others, 2)]
        mine = [[(True, i), (True, i + 1)] for i in range(0, tiles, 2)]
        turns = [pair for both in zip(work, mine) for pair in both] if work else mine
        pipeline([tile for pair in turns for tile in pair])
    else:
        pl.loop(0, tiles, step=2)(lambda i: pipeline([(True, i), (True, i + 1)]))
        pl.loop(0, others, step=2)(lambda i: pipeline([(False, i), (False, i + 1)]))
    lane = lax.broadcasted_iota(jnp.int32, (1, PAIR), 1)
    sums = sum_ref[...] * jnp.where(lane < HD, 1.0, 1.0 / SCALE)
    out_ref[:, :rows, :] = sums.astype(jnp.bfloat16).reshape(homes, rows, PAIR)
    for home in range(homes):
        start, half = home * rows, rows // 2
        out_ref[home, rows:, :] = side_by_side(
            dq_ref[start : start + half, :HD], dq_ref[start + half : start + rows, :HD]
        ).astype(jnp.bfloat16)


def attend(mine, others, valid, views, cross_bias):
    shares = len(others) + 1
    homes, both, _ = mine.shape
    rows = both // 2
    own = homes * rows
    tokens, tiles = own * shares, own // TILE
    begun = pl.pallas_call(
        functools.partial(begin_kernel, shares),
        out_shape=(
            pltpu.VMEM((tokens, PAIR), jnp.bfloat16),
            pltpu.VMEM((tokens, PAIR), jnp.bfloat16),
            pltpu.VMEM((tiles, 2 * TILE, 2 * PAIR), jnp.bfloat16),
            pltpu.VMEM((HD, own), jnp.bfloat16),
            pltpu.VMEM((tiles, own, TILE), jnp.float32),
            pltpu.VMEM((tiles, own, TILE), jnp.float32),
            pltpu.VMEM((tiles, 3, own // CHUNK, SUBLANES, TILE), jnp.float32),
        ),
        in_specs=[VMEM] + [SMEM] * 3,
        out_specs=(VMEM,) * 7,
        scratch_shapes=[pltpu.VMEM((own, 2 * PAIR), jnp.bfloat16)],
        compiler_params=pltpu.CompilerParams(vmem_limit_bytes=LIMIT),
        cost_estimate=pl.CostEstimate(
            flops=8 * own * own * PAIR, bytes_accessed=8 * own * own, transcendentals=own * own
        ),
        name="attend_begin",
    )(mine, valid, views, cross_bias)
    return pl.pallas_call(
        functools.partial(finish_kernel, shares),
        out_shape=pltpu.VMEM((homes, rows + rows // 2, PAIR), jnp.bfloat16),
        in_specs=[VMEM] * (shares + 7),
        out_specs=VMEM,
        scratch_shapes=[
            pltpu.VMEM((tokens, 2 * PAIR), jnp.bfloat16),
            pltpu.VMEM((max(tokens - own, TILE), PAIR), jnp.bfloat16),
            pltpu.VMEM((HD, tokens), jnp.bfloat16),
            pltpu.VMEM((own, PAIR), jnp.float32),
            pltpu.VMEM((own, PAIR), jnp.float32),
        ],
        compiler_params=pltpu.CompilerParams(vmem_limit_bytes=LIMIT),
        name="attend_finish",
    )(mine, *others, *begun)


def unpack_kernel(in_ref, dq_ref, dk_ref, dv_ref):
    rows = dq_ref.shape[0]
    half = rows // 2
    for head in range(0, in_ref.shape[0], 2):
        columns = slice(head * HD, (head + 2) * HD)
        one, two = (in_ref[head + which].astype(jnp.float32) for which in (0, 1))
        left = side_by_side(one[:, :HD], two[:, :HD])
        right = side_by_side(one[:, HD:], two[:, HD:])
        dk_ref[:, columns] = left[:rows]
        dv_ref[:, columns] = right[:rows]
        dq_ref[:half, columns] = left[rows:]
        dq_ref[half:, columns] = right[rows:]


def unpack(given, rows):
    shape = jax.ShapeDtypeStruct((rows, given.shape[0] * HD), jnp.float32)
    return pl.pallas_call(
        unpack_kernel,
        out_shape=(shape,) * 3,
        in_specs=[VMEM],
        out_specs=(VMEM,) * 3,
        name="unpack_heads",
    )(pltpu.with_memory_space_constraint(given, pltpu.VMEM))


def local(query, keys, values, grad_out, valid, views, cross_bias):
    swap = functools.partial(
        lax.all_to_all, axis_name="heads", split_axis=0, concat_axis=0, tiled=True
    )
    shares = lax.axis_size("share")
    mine = swap(pack(query, keys, values, grad_out))
    others = [
        lax.ppermute(mine, "share", [((i + k) % shares, i) for i in range(shares)])
        for k in range(1, shares)
    ]
    given = attend(mine, others, valid, views, cross_bias)
    return unpack(swap(given), query.shape[0])


def solution(mesh):
    groups = mesh.shape["grp"]
    members = mesh.shape["blk"] * mesh.shape["head"]

    def run(query, keys, values, grad_out, valid, views, cross_bias):
        heads = query.shape[1] // HD
        layout = Mesh(
            mesh.devices.reshape(groups, heads, members // heads), ("grp", "heads", "share")
        )
        tokens = P(("grp", "heads", "share"), None)
        return jax.shard_map(
            local,
            mesh=layout,
            in_specs=(tokens,) * 4 + (P("grp"), P("grp"), P()),
            out_specs=(tokens,) * 3,
            check_vma=False,
        )(query, keys, values, grad_out, valid, views, cross_bias)

    return run
```

```python
import functools
import math

import jax
import jax.numpy as jnp
from jax import lax
from jax.experimental import pallas as pl
from jax.experimental.pallas import tpu as pltpu
from jax.sharding import Mesh, PartitionSpec as P

HD = 64
FRAME = 32
PAIR = 2 * HD
TILE = 128
CHUNK = 128
SUBLANES = 8

SCALE = 0.125
DEAD = -1e30
LOG2E = math.log2(math.e)
LIMIT = 48 * 1024 * 1024

VMEM = pl.BlockSpec(memory_space=pltpu.VMEM)
SMEM = pl.BlockSpec(memory_space=pltpu.SMEM)


def side_by_side(left, right):
    return jnp.concatenate([left, right], axis=1)


def pack_kernel(q_ref, k_ref, v_ref, g_ref, out_ref):
    rows, width = q_ref.shape
    q, k, v, g = q_ref[...], k_ref[...], v_ref[...], g_ref[...]
    for head in range(width // HD):
        at = slice(head * HD, (head + 1) * HD)
        out_ref[head, :rows] = side_by_side(k[:, at], v[:, at])
        out_ref[head, rows:] = side_by_side(q[:, at], g[:, at])


def pack(query, keys, values, grad_out):
    rows, width = query.shape
    return pl.pallas_call(
        pack_kernel,
        out_shape=pltpu.VMEM((width // HD, 2 * rows, PAIR), query.dtype),
        in_specs=[VMEM] * 4,
        out_specs=VMEM,
        name="pack_heads",
    )(query, keys, values, grad_out)


def frame_of(homes, shares, per_home, block, home, which):
    share = lax.rem(lax.axis_index("share") + block, shares)
    return (home * shares + share) * per_home + which


def query_weights(qg):
    qg = qg.astype(jnp.float32)
    low = lax.broadcasted_iota(jnp.int32, qg.shape, 1) < HD
    return jnp.concatenate(
        [jnp.where(low, qg, 0.0), jnp.where(low, 0.0, qg * SCALE)], axis=0
    ).astype(jnp.bfloat16)


def products(keys, weights):
    return lax.dot_general(
        keys, weights, (((1,), (1,)), ((), ())), preferred_element_type=jnp.float32
    )


def exponentials(raw, gw):
    raw, gw = (x.reshape(-1, SUBLANES, TILE) for x in (raw, gw))
    top = jnp.max(raw, axis=0)
    expo = jnp.exp2((raw - top) * (SCALE * LOG2E))
    return expo, (top, jnp.sum(expo, axis=0), jnp.sum(expo * gw, axis=0))


def chunk_of(c):
    return slice(c * CHUNK, (c + 1) * CHUNK)


def begin_kernel(shares, mine_ref, valid_ref, views_ref, bias_ref, key_mark_ref,
                 query_mark_ref, weights_ref, flip_ref, expo_ref, gw_ref, stat_ref, keys_ref):
    homes, rows = mine_ref.shape[0], mine_ref.shape[1] // 2
    own = homes * rows
    per_home, per_tile, tiles = rows // FRAME, TILE // rows, own // TILE
    slot = lax.broadcasted_iota(jnp.int32, (FRAME, PAIR), 0)
    lane = lax.broadcasted_iota(jnp.int32, (1, PAIR), 1)

    bias = jnp.full((1, PAIR), bias_ref[lax.axis_index("heads")] / SCALE, jnp.float32)
    high = bias.astype(jnp.bfloat16).astype(jnp.float32)
    middle = (bias - high).astype(jnp.bfloat16).astype(jnp.float32)
    part = lax.rem(lane, 3)
    parts = jnp.where(part == 0, high, jnp.where(part == 1, middle, bias - high - middle))
    dead = jnp.where(lane == 6, DEAD / SCALE, 0.0)
    of_exo_query = jnp.where(lane < 3, parts, dead)
    of_ego_query = jnp.where((lane >= 3) & (lane < 6), parts, dead)

    for block in range(shares):
        for home in range(homes):
            for which in range(per_home):
                frame = frame_of(homes, shares, per_home, block, home, which)
                start = block * own + home * rows + which * FRAME
                here = slice(start, start + FRAME)
                exo = views_ref[frame] != 0
                first = jnp.where(exo, 3, 0)
                marks = jnp.where((lane >= first) & (lane < first + 3), 1.0, 0.0)
                gone = jnp.where(slot < valid_ref[frame], 0.0, 1.0)
                key_mark_ref[here, :] = jnp.where(lane == 6, gone, marks).astype(jnp.bfloat16)
                query_mark_ref[here, :] = jnp.broadcast_to(
                    jnp.where(exo, of_exo_query, of_ego_query), (FRAME, PAIR)
                ).astype(jnp.bfloat16)

    kv = mine_ref[:, :rows, :].reshape(own, PAIR)
    flip_ref[...] = kv.astype(jnp.float32).T[:HD].astype(jnp.bfloat16)
    keys_ref[:, :PAIR] = kv
    keys_ref[:, PAIR:] = key_mark_ref[:own, :]

    def score(index):
        qg = mine_ref[index * per_tile : (index + 1) * per_tile, rows:, :].reshape(TILE, PAIR)
        marks = query_mark_ref[index * TILE : (index + 1) * TILE, :]
        weights = side_by_side(
            query_weights(qg), jnp.concatenate([marks, jnp.zeros_like(marks)], axis=0)
        )
        weights_ref[index] = weights
        return products(keys_ref[...], weights)

    def leave(index, both):
        gw_ref[index] = both[:, TILE:]
        for c in range(own // CHUNK):
            at = chunk_of(c)
            expo, stats = exponentials(both[at, :TILE], both[at, TILE:])
            expo_ref[index, at, :] = expo.reshape(CHUNK, TILE)
            for which, stat in enumerate(stats):
                stat_ref[index, which, c] = stat

    scored = None
    for step in range(tiles + 1):
        last, scored = scored, score(step) if step < tiles else None
        if step:
            leave(step - 1, last)


def finish_kernel(shares, *refs):
    blocks, refs = refs[:shares], refs[shares:]
    key_mark_ref, query_mark_ref, weights_ref, own_flip_ref = refs[:4]
    expo_ref, gw_ref, stat_ref, out_ref, keys_ref, qg_ref, flip_ref, sum_ref, dq_ref = refs[4:]
    homes, rows = blocks[0].shape[0], blocks[0].shape[1] // 2
    own = homes * rows
    tokens = own * shares
    tiles, chunks, own_chunks = own // TILE, tokens // CHUNK, own // CHUNK

    keys_ref[:, PAIR:] = key_mark_ref[...]
    flip_ref[:, :own] = own_flip_ref[...]
    for block in range(shares):
        here = slice(block * own, (block + 1) * own)
        kv = blocks[block][:, :rows, :].reshape(own, PAIR)
        keys_ref[here, :PAIR] = kv
        if block:
            there = slice((block - 1) * own, block * own)
            flip_ref[:, here] = kv.astype(jnp.float32).T[:HD].astype(jnp.bfloat16)
            qg_ref[there, :] = blocks[block][:, rows:, :].reshape(own, PAIR)
    sum_ref[...] = jnp.zeros_like(sum_ref)

    def score(ours, index):
        if ours:
            weights = weights_ref[index]
            if chunks == own_chunks:
                return weights, None
            return weights, products(keys_ref[own:, :], weights)
        here = pl.ds(pl.multiple_of(index * TILE, TILE), TILE)
        there = pl.ds(pl.multiple_of(own + index * TILE, TILE), TILE)
        marks = query_mark_ref[there, :]
        weights = side_by_side(
            query_weights(qg_ref[here, :]),
            jnp.concatenate([marks, jnp.zeros_like(marks)], axis=0),
        )
        return weights, products(keys_ref[...], weights)

    def all_exponentials(ours, index, both):
        parts = []
        given = own_chunks if ours else 0
        for c in range(given):
            parts.append((None, None, *(stat_ref[index, which, c] for which in range(3))))
        for c in range(chunks - given):
            gw = both[chunk_of(c), TILE:]
            expo, stats = exponentials(both[chunk_of(c), :TILE], gw)
            parts.append((expo, gw.reshape(-1, SUBLANES, TILE), *stats))
        return parts

    def gradients(ours, index, parts):
        expos, gws, tops, totals, mixes = zip(*parts)
        highest = jnp.max(functools.reduce(jnp.maximum, tops), axis=0, keepdims=True)
        factors = [jnp.exp2((top - highest) * (SCALE * LOG2E)) for top in tops]
        total = jnp.sum(sum(f * t for f, t in zip(factors, totals)), axis=0, keepdims=True)
        mixed = jnp.sum(sum(f * m for f, m in zip(factors, mixes)), axis=0, keepdims=True)
        inverse = 1.0 / total
        delta = mixed * inverse
        lows, grads = [], []
        for c in range(chunks if ours else own_chunks):
            expo, gw = expos[c], gws[c]
            if expo is None:
                expo, gw = (
                    ref[index, chunk_of(c), :].reshape(-1, SUBLANES, TILE)
                    for ref in (expo_ref, gw_ref)
                )
            weight = expo * (factors[c] * inverse)
            grad = weight * (gw - delta)
            grads.append(grad.reshape(CHUNK, TILE).astype(jnp.bfloat16))
            if c < own_chunks:
                lows.append(weight.reshape(CHUNK, TILE).astype(jnp.bfloat16))
        return jnp.concatenate(grads, axis=0), jnp.concatenate(lows, axis=0)

    def leave(ours, first, group):
        weights, grads, lows = zip(*group)
        factors = [x for both in zip(grads, lows) for x in (both[0][:own], both[1])]
        sum_ref[...] += jnp.dot(
            jnp.concatenate(factors, axis=1),
            jnp.concatenate([each[:, :PAIR] for each in weights], axis=0),
            preferred_element_type=jnp.float32,
        )
        if ours:
            turned = jnp.dot(
                flip_ref[...], side_by_side(*grads), preferred_element_type=jnp.float32
            )
            here = pl.ds(pl.multiple_of(first * TILE, 2 * TILE), 2 * TILE)
            dq_ref[here, :] = jnp.concatenate([turned, turned], axis=0).T

    def pipeline(groups):
        work = [tile for group in groups for tile in group]
        scored, expos, done, groups = {}, {}, [], list(groups)
        for step in range(len(work) + 2):
            if step < len(work):
                scored[step] = score(*work[step])
            if 0 <= step - 1 < len(work):
                weights, both = scored.pop(step - 1)
                expos[step - 1] = weights, all_exponentials(*work[step - 1], both)
            if 0 <= step - 2:
                weights, parts = expos.pop(step - 2)
                done.append((weights, *gradients(*work[step - 2], parts)))
                if len(done) == len(groups[0]):
                    leave(*groups.pop(0)[0], done)
                    done = []

    others = tiles * (shares - 1)
    if shares <= 2:
        theirs = [[(False, i) for i in range(others)]] if others else []
        pipeline(theirs + [[(True, i), (True, i + 1)] for i in range(0, tiles, 2)])
    else:
        pl.loop(0, tiles, step=2)(lambda i: pipeline([[(True, i), (True, i + 1)]]))
        pl.loop(0, others, step=2)(lambda i: pipeline([[(False, i), (False, i + 1)]]))
    lane = lax.broadcasted_iota(jnp.int32, (1, PAIR), 1)
    sums = sum_ref[...] * jnp.where(lane < HD, 1.0, 1.0 / SCALE)
    out_ref[:, :rows, :] = sums.astype(jnp.bfloat16).reshape(homes, rows, PAIR)
    for home in range(homes):
        start, half = home * rows, rows // 2
        out_ref[home, rows:, :] = side_by_side(
            dq_ref[start : start + half, :HD], dq_ref[start + half : start + rows, :HD]
        ).astype(jnp.bfloat16)


def attend(mine, others, valid, views, cross_bias):
    shares = len(others) + 1
    homes, both, _ = mine.shape
    rows = both // 2
    own = homes * rows
    tokens, tiles = own * shares, own // TILE
    begun = pl.pallas_call(
        functools.partial(begin_kernel, shares),
        out_shape=(
            pltpu.VMEM((tokens, PAIR), jnp.bfloat16),
            pltpu.VMEM((tokens, PAIR), jnp.bfloat16),
            pltpu.VMEM((tiles, 2 * TILE, 2 * PAIR), jnp.bfloat16),
            pltpu.VMEM((HD, own), jnp.bfloat16),
            pltpu.VMEM((tiles, own, TILE), jnp.float32),
            pltpu.VMEM((tiles, own, TILE), jnp.float32),
            pltpu.VMEM((tiles, 3, own // CHUNK, SUBLANES, TILE), jnp.float32),
        ),
        in_specs=[VMEM] + [SMEM] * 3,
        out_specs=(VMEM,) * 7,
        scratch_shapes=[pltpu.VMEM((own, 2 * PAIR), jnp.bfloat16)],
        compiler_params=pltpu.CompilerParams(vmem_limit_bytes=LIMIT),
        cost_estimate=pl.CostEstimate(
            flops=8 * own * own * PAIR, bytes_accessed=8 * own * own, transcendentals=own * own
        ),
        name="attend_begin",
    )(mine, valid, views, cross_bias)
    return pl.pallas_call(
        functools.partial(finish_kernel, shares),
        out_shape=pltpu.VMEM((homes, rows + rows // 2, PAIR), jnp.bfloat16),
        in_specs=[VMEM] * (shares + 7),
        out_specs=VMEM,
        scratch_shapes=[
            pltpu.VMEM((tokens, 2 * PAIR), jnp.bfloat16),
            pltpu.VMEM((max(tokens - own, TILE), PAIR), jnp.bfloat16),
            pltpu.VMEM((HD, tokens), jnp.bfloat16),
            pltpu.VMEM((own, PAIR), jnp.float32),
            pltpu.VMEM((own, PAIR), jnp.float32),
        ],
        compiler_params=pltpu.CompilerParams(vmem_limit_bytes=LIMIT),
        name="attend_finish",
    )(mine, *others, *begun)


def unpack_kernel(in_ref, dq_ref, dk_ref, dv_ref):
    rows = dq_ref.shape[0]
    half = rows // 2
    for head in range(0, in_ref.shape[0], 2):
        columns = slice(head * HD, (head + 2) * HD)
        one, two = (in_ref[head + which].astype(jnp.float32) for which in (0, 1))
        left = side_by_side(one[:, :HD], two[:, :HD])
        right = side_by_side(one[:, HD:], two[:, HD:])
        dk_ref[:, columns] = left[:rows]
        dv_ref[:, columns] = right[:rows]
        dq_ref[:half, columns] = left[rows:]
        dq_ref[half:, columns] = right[rows:]


def unpack(given, rows):
    shape = jax.ShapeDtypeStruct((rows, given.shape[0] * HD), jnp.float32)
    return pl.pallas_call(
        unpack_kernel,
        out_shape=(shape,) * 3,
        in_specs=[VMEM],
        out_specs=(VMEM,) * 3,
        name="unpack_heads",
    )(pltpu.with_memory_space_constraint(given, pltpu.VMEM))


def local(query, keys, values, grad_out, valid, views, cross_bias):
    swap = functools.partial(
        lax.all_to_all, axis_name="heads", split_axis=0, concat_axis=0, tiled=True
    )
    shares = lax.axis_size("share")
    mine = swap(pack(query, keys, values, grad_out))
    others = [
        lax.ppermute(mine, "share", [((i + k) % shares, i) for i in range(shares)])
        for k in range(1, shares)
    ]
    given = attend(mine, others, valid, views, cross_bias)
    return unpack(swap(given), query.shape[0])


def solution(mesh):
    groups = mesh.shape["grp"]
    members = mesh.shape["blk"] * mesh.shape["head"]

    def run(query, keys, values, grad_out, valid, views, cross_bias):
        heads = query.shape[1] // HD
        layout = Mesh(
            mesh.devices.reshape(groups, heads, members // heads), ("grp", "heads", "share")
        )
        tokens = P(("grp", "heads", "share"), None)
        return jax.shard_map(
            local,
            mesh=layout,
            in_specs=(tokens,) * 4 + (P("grp"), P("grp"), P()),
            out_specs=(tokens,) * 3,
            check_vma=False,
        )(query, keys, values, grad_out, valid, views, cross_bias)

    return run
```

```python
import functools
import math

import jax
import jax.numpy as jnp
from jax import lax
from jax.experimental import pallas as pl
from jax.experimental.pallas import tpu as pltpu
from jax.sharding import Mesh, PartitionSpec as P

HD = 64
FRAME = 32
PAIR = 2 * HD
TILE = 128
CHUNK = 256
SUBLANES = 8

SCALE = 0.125
DEAD = -1e30
LOG2E = math.log2(math.e)
LIMIT = 48 * 1024 * 1024

VMEM = pl.BlockSpec(memory_space=pltpu.VMEM)
SMEM = pl.BlockSpec(memory_space=pltpu.SMEM)


def side_by_side(left, right):
    return jnp.concatenate([left, right], axis=1)


def pack_kernel(q_ref, k_ref, v_ref, g_ref, out_ref):
    rows, width = q_ref.shape
    q, k, v, g = q_ref[...], k_ref[...], v_ref[...], g_ref[...]
    for head in range(width // HD):
        at = slice(head * HD, (head + 1) * HD)
        out_ref[head, :rows] = side_by_side(k[:, at], v[:, at])
        out_ref[head, rows:] = side_by_side(q[:, at], g[:, at])


def pack(query, keys, values, grad_out):
    rows, width = query.shape
    return pl.pallas_call(
        pack_kernel,
        out_shape=pltpu.VMEM((width // HD, 2 * rows, PAIR), query.dtype),
        in_specs=[VMEM] * 4,
        out_specs=VMEM,
        name="pack_heads",
    )(query, keys, values, grad_out)


def frame_of(homes, shares, per_home, block, home, which):
    share = lax.rem(lax.axis_index("share") + block, shares)
    return (home * shares + share) * per_home + which


def query_weights(qg):
    qg = qg.astype(jnp.float32)
    low = lax.broadcasted_iota(jnp.int32, qg.shape, 1) < HD
    return jnp.concatenate(
        [jnp.where(low, qg, 0.0), jnp.where(low, 0.0, qg * SCALE)], axis=0
    ).astype(jnp.bfloat16)


def products(keys, weights):
    return lax.dot_general(
        keys, weights, (((1,), (1,)), ((), ())), preferred_element_type=jnp.float32
    )


def exponentials(raw, gw):
    raw, gw = (x.reshape(-1, SUBLANES, TILE) for x in (raw, gw))
    top = jnp.max(raw, axis=0)
    expo = jnp.exp2((raw - top) * (SCALE * LOG2E))
    return expo, (top, jnp.sum(expo, axis=0), jnp.sum(expo * gw, axis=0))


def chunk_of(c):
    return slice(c * CHUNK, (c + 1) * CHUNK)


def begin_kernel(shares, mine_ref, valid_ref, views_ref, bias_ref, key_mark_ref,
                 query_mark_ref, weights_ref, flip_ref, expo_ref, gw_ref, stat_ref, keys_ref):
    homes, rows = mine_ref.shape[0], mine_ref.shape[1] // 2
    own = homes * rows
    per_home, per_tile, tiles = rows // FRAME, TILE // rows, own // TILE
    slot = lax.broadcasted_iota(jnp.int32, (FRAME, PAIR), 0)
    lane = lax.broadcasted_iota(jnp.int32, (1, PAIR), 1)

    bias = jnp.full((1, PAIR), bias_ref[lax.axis_index("heads")] / SCALE, jnp.float32)
    high = bias.astype(jnp.bfloat16).astype(jnp.float32)
    middle = (bias - high).astype(jnp.bfloat16).astype(jnp.float32)
    part = lax.rem(lane, 3)
    parts = jnp.where(part == 0, high, jnp.where(part == 1, middle, bias - high - middle))
    dead = jnp.where(lane == 6, DEAD / SCALE, 0.0)
    of_exo_query = jnp.where(lane < 3, parts, dead)
    of_ego_query = jnp.where((lane >= 3) & (lane < 6), parts, dead)

    for block in range(shares):
        for home in range(homes):
            for which in range(per_home):
                frame = frame_of(homes, shares, per_home, block, home, which)
                start = block * own + home * rows + which * FRAME
                here = slice(start, start + FRAME)
                exo = views_ref[frame] != 0
                first = jnp.where(exo, 3, 0)
                marks = jnp.where((lane >= first) & (lane < first + 3), 1.0, 0.0)
                gone = jnp.where(slot < valid_ref[frame], 0.0, 1.0)
                key_mark_ref[here, :] = jnp.where(lane == 6, gone, marks).astype(jnp.bfloat16)
                query_mark_ref[here, :] = jnp.broadcast_to(
                    jnp.where(exo, of_exo_query, of_ego_query), (FRAME, PAIR)
                ).astype(jnp.bfloat16)

    kv = mine_ref[:, :rows, :].reshape(own, PAIR)
    flip_ref[...] = kv.astype(jnp.float32).T[:HD].astype(jnp.bfloat16)
    keys_ref[:, :PAIR] = kv
    keys_ref[:, PAIR:] = key_mark_ref[:own, :]

    def score(index):
        qg = mine_ref[index * per_tile : (index + 1) * per_tile, rows:, :].reshape(TILE, PAIR)
        marks = query_mark_ref[index * TILE : (index + 1) * TILE, :]
        weights = side_by_side(
            query_weights(qg), jnp.concatenate([marks, jnp.zeros_like(marks)], axis=0)
        )
        weights_ref[index] = weights
        return products(keys_ref[...], weights)

    def leave(index, both):
        gw_ref[index] = both[:, TILE:]
        for c in range(own // CHUNK):
            at = chunk_of(c)
            expo, stats = exponentials(both[at, :TILE], both[at, TILE:])
            expo_ref[index, at, :] = expo.reshape(CHUNK, TILE)
            for which, stat in enumerate(stats):
                stat_ref[index, which, c] = stat

    scored = None
    for step in range(tiles + 1):
        last, scored = scored, score(step) if step < tiles else None
        if step:
            leave(step - 1, last)


def finish_kernel(shares, *refs):
    blocks, refs = refs[:shares], refs[shares:]
    key_mark_ref, query_mark_ref, weights_ref, own_flip_ref = refs[:4]
    expo_ref, gw_ref, stat_ref, out_ref, keys_ref, qg_ref, flip_ref, sum_ref, dq_ref = refs[4:]
    homes, rows = blocks[0].shape[0], blocks[0].shape[1] // 2
    own = homes * rows
    tokens = own * shares
    tiles, chunks, own_chunks = own // TILE, tokens // CHUNK, own // CHUNK

    keys_ref[:, PAIR:] = key_mark_ref[...]
    flip_ref[:, :own] = own_flip_ref[...]
    for block in range(shares):
        here = slice(block * own, (block + 1) * own)
        kv = blocks[block][:, :rows, :].reshape(own, PAIR)
        keys_ref[here, :PAIR] = kv
        if block:
            there = slice((block - 1) * own, block * own)
            flip_ref[:, here] = kv.astype(jnp.float32).T[:HD].astype(jnp.bfloat16)
            qg_ref[there, :] = blocks[block][:, rows:, :].reshape(own, PAIR)
    sum_ref[...] = jnp.zeros_like(sum_ref)

    def score(ours, index):
        if ours:
            weights = weights_ref[index]
            if chunks == own_chunks:
                return weights, None
            return weights, products(keys_ref[own:, :], weights)
        here = pl.ds(pl.multiple_of(index * TILE, TILE), TILE)
        there = pl.ds(pl.multiple_of(own + index * TILE, TILE), TILE)
        marks = query_mark_ref[there, :]
        weights = side_by_side(
            query_weights(qg_ref[here, :]),
            jnp.concatenate([marks, jnp.zeros_like(marks)], axis=0),
        )
        return weights, products(keys_ref[...], weights)

    def all_exponentials(ours, index, both):
        parts = []
        given = own_chunks if ours else 0
        for c in range(given):
            parts.append((None, None, *(stat_ref[index, which, c] for which in range(3))))
        for c in range(chunks - given):
            gw = both[chunk_of(c), TILE:]
            expo, stats = exponentials(both[chunk_of(c), :TILE], gw)
            parts.append((expo, gw.reshape(-1, SUBLANES, TILE), *stats))
        return parts

    def gradients(ours, index, parts):
        expos, gws, tops, totals, mixes = zip(*parts)
        highest = jnp.max(functools.reduce(jnp.maximum, tops), axis=0, keepdims=True)
        factors = [jnp.exp2((top - highest) * (SCALE * LOG2E)) for top in tops]
        total = jnp.sum(sum(f * t for f, t in zip(factors, totals)), axis=0, keepdims=True)
        mixed = jnp.sum(sum(f * m for f, m in zip(factors, mixes)), axis=0, keepdims=True)
        inverse = 1.0 / total
        delta = mixed * inverse
        lows, grads = [], []
        for c in range(chunks if ours else own_chunks):
            expo, gw = expos[c], gws[c]
            if expo is None:
                expo, gw = (
                    ref[index, chunk_of(c), :].reshape(-1, SUBLANES, TILE)
                    for ref in (expo_ref, gw_ref)
                )
            weight = expo * (factors[c] * inverse)
            grad = weight * (gw - delta)
            grads.append(grad.reshape(CHUNK, TILE).astype(jnp.bfloat16))
            if c < own_chunks:
                lows.append(weight.reshape(CHUNK, TILE).astype(jnp.bfloat16))
        return jnp.concatenate(grads, axis=0), jnp.concatenate(lows, axis=0)

    def leave(ours, first, pair):
        weights, grads, lows = zip(*pair)
        factors = [x for both in zip(grads, lows) for x in (both[0][:own], both[1])]
        sum_ref[...] += jnp.dot(
            jnp.concatenate(factors, axis=1),
            jnp.concatenate([each[:, :PAIR] for each in weights], axis=0),
            preferred_element_type=jnp.float32,
        )
        if ours:
            turned = jnp.dot(
                flip_ref[...], side_by_side(*grads), preferred_element_type=jnp.float32
            )
            here = pl.ds(pl.multiple_of(first * TILE, 2 * TILE), 2 * TILE)
            dq_ref[here, :] = jnp.concatenate([turned, turned], axis=0).T

    def pipeline(work):
        scored, expos, done = {}, {}, {}
        for step in range(len(work) + 2):
            if step < len(work):
                scored[step] = score(*work[step])
            if 0 <= step - 1 < len(work):
                weights, both = scored.pop(step - 1)
                expos[step - 1] = weights, all_exponentials(*work[step - 1], both)
            if 0 <= step - 2:
                weights, parts = expos.pop(step - 2)
                done[step - 2] = (weights, *gradients(*work[step - 2], parts))
                if step % 2:
                    leave(*work[step - 3], (done.pop(step - 3), done.pop(step - 2)))

    others = tiles * (shares - 1)
    if shares <= 2:
        pipeline([(False, i) for i in range(others)] + [(True, i) for i in range(tiles)])
    else:
        pl.loop(0, tiles, step=2)(lambda i: pipeline([(True, i), (True, i + 1)]))
        pl.loop(0, others, step=2)(lambda i: pipeline([(False, i), (False, i + 1)]))
    lane = lax.broadcasted_iota(jnp.int32, (1, PAIR), 1)
    sums = sum_ref[...] * jnp.where(lane < HD, 1.0, 1.0 / SCALE)
    out_ref[:, :rows, :] = sums.astype(jnp.bfloat16).reshape(homes, rows, PAIR)
    for home in range(homes):
        start, half = home * rows, rows // 2
        out_ref[home, rows:, :] = side_by_side(
            dq_ref[start : start + half, :HD], dq_ref[start + half : start + rows, :HD]
        ).astype(jnp.bfloat16)


def attend(mine, others, valid, views, cross_bias):
    shares = len(others) + 1
    homes, both, _ = mine.shape
    rows = both // 2
    own = homes * rows
    tokens, tiles = own * shares, own // TILE
    begun = pl.pallas_call(
        functools.partial(begin_kernel, shares),
        out_shape=(
            pltpu.VMEM((tokens, PAIR), jnp.bfloat16),
            pltpu.VMEM((tokens, PAIR), jnp.bfloat16),
            pltpu.VMEM((tiles, 2 * TILE, 2 * PAIR), jnp.bfloat16),
            pltpu.VMEM((HD, own), jnp.bfloat16),
            pltpu.VMEM((tiles, own, TILE), jnp.float32),
            pltpu.VMEM((tiles, own, TILE), jnp.float32),
            pltpu.VMEM((tiles, 3, own // CHUNK, SUBLANES, TILE), jnp.float32),
        ),
        in_specs=[VMEM] + [SMEM] * 3,
        out_specs=(VMEM,) * 7,
        scratch_shapes=[pltpu.VMEM((own, 2 * PAIR), jnp.bfloat16)],
        compiler_params=pltpu.CompilerParams(vmem_limit_bytes=LIMIT),
        cost_estimate=pl.CostEstimate(
            flops=8 * own * own * PAIR, bytes_accessed=8 * own * own, transcendentals=own * own
        ),
        name="attend_begin",
    )(mine, valid, views, cross_bias)
    return pl.pallas_call(
        functools.partial(finish_kernel, shares),
        out_shape=pltpu.VMEM((homes, rows + rows // 2, PAIR), jnp.bfloat16),
        in_specs=[VMEM] * (shares + 7),
        out_specs=VMEM,
        scratch_shapes=[
            pltpu.VMEM((tokens, 2 * PAIR), jnp.bfloat16),
            pltpu.VMEM((max(tokens - own, TILE), PAIR), jnp.bfloat16),
            pltpu.VMEM((HD, tokens), jnp.bfloat16),
            pltpu.VMEM((own, PAIR), jnp.float32),
            pltpu.VMEM((own, PAIR), jnp.float32),
        ],
        compiler_params=pltpu.CompilerParams(vmem_limit_bytes=LIMIT),
        name="attend_finish",
    )(mine, *others, *begun)


def unpack_kernel(in_ref, dq_ref, dk_ref, dv_ref):
    rows = dq_ref.shape[0]
    half = rows // 2
    for head in range(0, in_ref.shape[0], 2):
        columns = slice(head * HD, (head + 2) * HD)
        one, two = (in_ref[head + which].astype(jnp.float32) for which in (0, 1))
        left = side_by_side(one[:, :HD], two[:, :HD])
        right = side_by_side(one[:, HD:], two[:, HD:])
        dk_ref[:, columns] = left[:rows]
        dv_ref[:, columns] = right[:rows]
        dq_ref[:half, columns] = left[rows:]
        dq_ref[half:, columns] = right[rows:]


def unpack(given, rows):
    shape = jax.ShapeDtypeStruct((rows, given.shape[0] * HD), jnp.float32)
    return pl.pallas_call(
        unpack_kernel,
        out_shape=(shape,) * 3,
        in_specs=[VMEM],
        out_specs=(VMEM,) * 3,
        name="unpack_heads",
    )(pltpu.with_memory_space_constraint(given, pltpu.VMEM))


def local(query, keys, values, grad_out, valid, views, cross_bias):
    swap = functools.partial(
        lax.all_to_all, axis_name="heads", split_axis=0, concat_axis=0, tiled=True
    )
    shares = lax.axis_size("share")
    mine = swap(pack(query, keys, values, grad_out))
    others = [
        lax.ppermute(mine, "share", [((i + k) % shares, i) for i in range(shares)])
        for k in range(1, shares)
    ]
    given = attend(mine, others, valid, views, cross_bias)
    return unpack(swap(given), query.shape[0])


def solution(mesh):
    groups = mesh.shape["grp"]
    members = mesh.shape["blk"] * mesh.shape["head"]

    def run(query, keys, values, grad_out, valid, views, cross_bias):
        heads = query.shape[1] // HD
        layout = Mesh(
            mesh.devices.reshape(groups, heads, members // heads), ("grp", "heads", "share")
        )
        tokens = P(("grp", "heads", "share"), None)
        return jax.shard_map(
            local,
            mesh=layout,
            in_specs=(tokens,) * 4 + (P("grp"), P("grp"), P()),
            out_specs=(tokens,) * 3,
            check_vma=False,
        )(query, keys, values, grad_out, valid, views, cross_bias)

    return run
```

```python
import functools
import math

import jax
import jax.numpy as jnp
from jax import lax
from jax.experimental import pallas as pl
from jax.experimental.pallas import tpu as pltpu
from jax.sharding import Mesh, PartitionSpec as P

HD = 64
FRAME = 32
PAIR = 2 * HD
TILE = 128
CHUNK = 128
SUBLANES = 8

SCALE = 0.125
DEAD = -1e30
LOG2E = math.log2(math.e)
LIMIT = 48 * 1024 * 1024

VMEM = pl.BlockSpec(memory_space=pltpu.VMEM)
SMEM = pl.BlockSpec(memory_space=pltpu.SMEM)


def side_by_side(left, right):
    return jnp.concatenate([left, right], axis=1)


def pack_kernel(q_ref, k_ref, v_ref, g_ref, out_ref):
    rows, width = q_ref.shape
    q, k, v, g = q_ref[...], k_ref[...], v_ref[...], g_ref[...]
    for head in range(width // HD):
        at = slice(head * HD, (head + 1) * HD)
        out_ref[head, :rows] = side_by_side(k[:, at], v[:, at])
        out_ref[head, rows:] = side_by_side(q[:, at], g[:, at])


def pack(query, keys, values, grad_out):
    rows, width = query.shape
    return pl.pallas_call(
        pack_kernel,
        out_shape=pltpu.VMEM((width // HD, 2 * rows, PAIR), query.dtype),
        in_specs=[VMEM] * 4,
        out_specs=VMEM,
        name="pack_heads",
    )(query, keys, values, grad_out)


def frame_of(homes, shares, per_home, block, home, which):
    share = lax.rem(lax.axis_index("share") + block, shares)
    return (home * shares + share) * per_home + which


def query_weights(qg):
    qg = qg.astype(jnp.float32)
    low = lax.broadcasted_iota(jnp.int32, qg.shape, 1) < HD
    return jnp.concatenate(
        [jnp.where(low, qg, 0.0), jnp.where(low, 0.0, qg * SCALE)], axis=0
    ).astype(jnp.bfloat16)


def products(keys, weights):
    return lax.dot_general(
        keys, weights, (((1,), (1,)), ((), ())), preferred_element_type=jnp.float32
    )


def exponentials(raw, gw):
    raw, gw = (x.reshape(-1, SUBLANES, TILE) for x in (raw, gw))
    top = jnp.max(raw, axis=0)
    expo = jnp.exp2((raw - top) * (SCALE * LOG2E))
    return expo, (top, jnp.sum(expo, axis=0), jnp.sum(expo * gw, axis=0))


def chunk_of(c):
    return slice(c * CHUNK, (c + 1) * CHUNK)


def begin_kernel(shares, mine_ref, valid_ref, views_ref, bias_ref, key_mark_ref,
                 query_mark_ref, weights_ref, flip_ref, expo_ref, gw_ref, stat_ref, keys_ref):
    homes, rows = mine_ref.shape[0], mine_ref.shape[1] // 2
    own = homes * rows
    per_home, per_tile, tiles = rows // FRAME, TILE // rows, own // TILE
    slot = lax.broadcasted_iota(jnp.int32, (FRAME, PAIR), 0)
    lane = lax.broadcasted_iota(jnp.int32, (1, PAIR), 1)

    bias = jnp.full((1, PAIR), bias_ref[lax.axis_index("heads")] / SCALE, jnp.float32)
    high = bias.astype(jnp.bfloat16).astype(jnp.float32)
    middle = (bias - high).astype(jnp.bfloat16).astype(jnp.float32)
    part = lax.rem(lane, 3)
    parts = jnp.where(part == 0, high, jnp.where(part == 1, middle, bias - high - middle))
    dead = jnp.where(lane == 6, DEAD / SCALE, 0.0)
    of_exo_query = jnp.where(lane < 3, parts, dead)
    of_ego_query = jnp.where((lane >= 3) & (lane < 6), parts, dead)

    for block in range(shares):
        for home in range(homes):
            for which in range(per_home):
                frame = frame_of(homes, shares, per_home, block, home, which)
                start = block * own + home * rows + which * FRAME
                here = slice(start, start + FRAME)
                exo = views_ref[frame] != 0
                first = jnp.where(exo, 3, 0)
                marks = jnp.where((lane >= first) & (lane < first + 3), 1.0, 0.0)
                gone = jnp.where(slot < valid_ref[frame], 0.0, 1.0)
                key_mark_ref[here, :] = jnp.where(lane == 6, gone, marks).astype(jnp.bfloat16)
                query_mark_ref[here, :] = jnp.broadcast_to(
                    jnp.where(exo, of_exo_query, of_ego_query), (FRAME, PAIR)
                ).astype(jnp.bfloat16)

    kv = mine_ref[:, :rows, :].reshape(own, PAIR)
    flip_ref[...] = kv.astype(jnp.float32).T[:HD].astype(jnp.bfloat16)
    keys_ref[:, :PAIR] = kv
    keys_ref[:, PAIR:] = key_mark_ref[:own, :]

    def score(index):
        qg = mine_ref[index * per_tile : (index + 1) * per_tile, rows:, :].reshape(TILE, PAIR)
        marks = query_mark_ref[index * TILE : (index + 1) * TILE, :]
        weights = side_by_side(
            query_weights(qg), jnp.concatenate([marks, jnp.zeros_like(marks)], axis=0)
        )
        weights_ref[index] = weights
        return products(keys_ref[...], weights)

    def leave(index, both):
        gw_ref[index] = both[:, TILE:]
        for c in range(own // CHUNK):
            at = chunk_of(c)
            expo, stats = exponentials(both[at, :TILE], both[at, TILE:])
            expo_ref[index, at, :] = expo.reshape(CHUNK, TILE)
            for which, stat in enumerate(stats):
                stat_ref[index, which, c] = stat

    scored = None
    for step in range(tiles + 1):
        last, scored = scored, score(step) if step < tiles else None
        if step:
            leave(step - 1, last)


def finish_kernel(shares, *refs):
    blocks, refs = refs[:shares], refs[shares:]
    key_mark_ref, query_mark_ref, weights_ref, own_flip_ref = refs[:4]
    expo_ref, gw_ref, stat_ref, out_ref, keys_ref, qg_ref, flip_ref, sum_ref, dq_ref = refs[4:]
    homes, rows = blocks[0].shape[0], blocks[0].shape[1] // 2
    own = homes * rows
    tokens = own * shares
    tiles, chunks, own_chunks = own // TILE, tokens // CHUNK, own // CHUNK

    keys_ref[:, PAIR:] = key_mark_ref[...]
    flip_ref[:, :own] = own_flip_ref[...]
    for block in range(shares):
        here = slice(block * own, (block + 1) * own)
        kv = blocks[block][:, :rows, :].reshape(own, PAIR)
        keys_ref[here, :PAIR] = kv
        if block:
            there = slice((block - 1) * own, block * own)
            flip_ref[:, here] = kv.astype(jnp.float32).T[:HD].astype(jnp.bfloat16)
            qg_ref[there, :] = blocks[block][:, rows:, :].reshape(own, PAIR)
    if shares > 2:
        sum_ref[...] = jnp.zeros_like(sum_ref)

    def score(ours, index):
        if ours:
            weights = weights_ref[index]
            if chunks == own_chunks:
                return weights, None
            return weights, products(keys_ref[own:, :], weights)
        here = pl.ds(pl.multiple_of(index * TILE, TILE), TILE)
        there = pl.ds(pl.multiple_of(own + index * TILE, TILE), TILE)
        marks = query_mark_ref[there, :]
        weights = side_by_side(
            query_weights(qg_ref[here, :]),
            jnp.concatenate([marks, jnp.zeros_like(marks)], axis=0),
        )
        return weights, products(keys_ref[...], weights)

    def all_exponentials(ours, index, both):
        parts = []
        given = own_chunks if ours else 0
        for c in range(given):
            parts.append((None, None, *(stat_ref[index, which, c] for which in range(3))))
        for c in range(chunks - given):
            gw = both[chunk_of(c), TILE:]
            expo, stats = exponentials(both[chunk_of(c), :TILE], gw)
            parts.append((expo, gw.reshape(-1, SUBLANES, TILE), *stats))
        return parts

    def gradients(ours, index, parts):
        expos, gws, tops, totals, mixes = zip(*parts)
        highest = jnp.max(functools.reduce(jnp.maximum, tops), axis=0, keepdims=True)
        factors = [jnp.exp2((top - highest) * (SCALE * LOG2E)) for top in tops]
        total = jnp.sum(sum(f * t for f, t in zip(factors, totals)), axis=0, keepdims=True)
        mixed = jnp.sum(sum(f * m for f, m in zip(factors, mixes)), axis=0, keepdims=True)
        inverse = 1.0 / total
        delta = mixed * inverse
        lows, grads = [], []
        for c in range(chunks if ours else own_chunks):
            expo, gw = expos[c], gws[c]
            if expo is None:
                expo, gw = (
                    ref[index, chunk_of(c), :].reshape(-1, SUBLANES, TILE)
                    for ref in (expo_ref, gw_ref)
                )
            weight = expo * (factors[c] * inverse)
            grad = weight * (gw - delta)
            grads.append(grad.reshape(CHUNK, TILE).astype(jnp.bfloat16))
            if c < own_chunks:
                lows.append(weight.reshape(CHUNK, TILE).astype(jnp.bfloat16))
        return jnp.concatenate(grads, axis=0), jnp.concatenate(lows, axis=0)

    def leave(ours, first, pair, fresh):
        weights, grads, lows = zip(*pair)
        factors = [x for both in zip(grads, lows) for x in (both[0][:own], both[1])]
        added = jnp.dot(
            jnp.concatenate(factors, axis=1),
            jnp.concatenate([each[:, :PAIR] for each in weights], axis=0),
            preferred_element_type=jnp.float32,
        )
        sum_ref[...] = added if fresh else sum_ref[...] + added
        if ours:
            turned = jnp.dot(
                flip_ref[...], side_by_side(*grads), preferred_element_type=jnp.float32
            )
            here = pl.ds(pl.multiple_of(first * TILE, 2 * TILE), 2 * TILE)
            dq_ref[here, :] = jnp.concatenate([turned, turned], axis=0).T

    def pipeline(work):
        scored, expos, done = {}, {}, {}
        for step in range(len(work) + 2):
            if step < len(work):
                scored[step] = score(*work[step])
            if 0 <= step - 1 < len(work):
                weights, both = scored.pop(step - 1)
                expos[step - 1] = weights, all_exponentials(*work[step - 1], both)
            if 0 <= step - 2:
                weights, parts = expos.pop(step - 2)
                done[step - 2] = (weights, *gradients(*work[step - 2], parts))
                if step % 2:
                    pair = (done.pop(step - 3), done.pop(step - 2))
                    leave(*work[step - 3], pair, step == 3 and shares <= 2)

    others = tiles * (shares - 1)
    if shares <= 2:
        pipeline([(False, i) for i in range(others)] + [(True, i) for i in range(tiles)])
    else:
        pl.loop(0, tiles, step=2)(lambda i: pipeline([(True, i), (True, i + 1)]))
        pl.loop(0, others, step=2)(lambda i: pipeline([(False, i), (False, i + 1)]))
    lane = lax.broadcasted_iota(jnp.int32, (1, PAIR), 1)
    sums = sum_ref[...] * jnp.where(lane < HD, 1.0, 1.0 / SCALE)
    out_ref[:, :rows, :] = sums.astype(jnp.bfloat16).reshape(homes, rows, PAIR)
    for home in range(homes):
        start, half = home * rows, rows // 2
        out_ref[home, rows:, :] = side_by_side(
            dq_ref[start : start + half, :HD], dq_ref[start + half : start + rows, :HD]
        ).astype(jnp.bfloat16)


def attend(mine, others, valid, views, cross_bias):
    shares = len(others) + 1
    homes, both, _ = mine.shape
    rows = both // 2
    own = homes * rows
    tokens, tiles = own * shares, own // TILE
    begun = pl.pallas_call(
        functools.partial(begin_kernel, shares),
        out_shape=(
            pltpu.VMEM((tokens, PAIR), jnp.bfloat16),
            pltpu.VMEM((tokens, PAIR), jnp.bfloat16),
            pltpu.VMEM((tiles, 2 * TILE, 2 * PAIR), jnp.bfloat16),
            pltpu.VMEM((HD, own), jnp.bfloat16),
            pltpu.VMEM((tiles, own, TILE), jnp.float32),
            pltpu.VMEM((tiles, own, TILE), jnp.float32),
            pltpu.VMEM((tiles, 3, own // CHUNK, SUBLANES, TILE), jnp.float32),
        ),
        in_specs=[VMEM] + [SMEM] * 3,
        out_specs=(VMEM,) * 7,
        scratch_shapes=[pltpu.VMEM((own, 2 * PAIR), jnp.bfloat16)],
        compiler_params=pltpu.CompilerParams(vmem_limit_bytes=LIMIT),
        cost_estimate=pl.CostEstimate(
            flops=8 * own * own * PAIR, bytes_accessed=8 * own * own, transcendentals=own * own
        ),
        name="attend_begin",
    )(mine, valid, views, cross_bias)
    return pl.pallas_call(
        functools.partial(finish_kernel, shares),
        out_shape=pltpu.VMEM((homes, rows + rows // 2, PAIR), jnp.bfloat16),
        in_specs=[VMEM] * (shares + 7),
        out_specs=VMEM,
        scratch_shapes=[
            pltpu.VMEM((tokens, 2 * PAIR), jnp.bfloat16),
            pltpu.VMEM((max(tokens - own, TILE), PAIR), jnp.bfloat16),
            pltpu.VMEM((HD, tokens), jnp.bfloat16),
            pltpu.VMEM((own, PAIR), jnp.float32),
            pltpu.VMEM((own, PAIR), jnp.float32),
        ],
        compiler_params=pltpu.CompilerParams(vmem_limit_bytes=LIMIT),
        name="attend_finish",
    )(mine, *others, *begun)


def unpack_kernel(in_ref, dq_ref, dk_ref, dv_ref):
    rows = dq_ref.shape[0]
    half = rows // 2
    for head in range(0, in_ref.shape[0], 2):
        columns = slice(head * HD, (head + 2) * HD)
        one, two = (in_ref[head + which].astype(jnp.float32) for which in (0, 1))
        left = side_by_side(one[:, :HD], two[:, :HD])
        right = side_by_side(one[:, HD:], two[:, HD:])
        dk_ref[:, columns] = left[:rows]
        dv_ref[:, columns] = right[:rows]
        dq_ref[:half, columns] = left[rows:]
        dq_ref[half:, columns] = right[rows:]


def unpack(given, rows):
    shape = jax.ShapeDtypeStruct((rows, given.shape[0] * HD), jnp.float32)
    return pl.pallas_call(
        unpack_kernel,
        out_shape=(shape,) * 3,
        in_specs=[VMEM],
        out_specs=(VMEM,) * 3,
        name="unpack_heads",
    )(pltpu.with_memory_space_constraint(given, pltpu.VMEM))


def local(query, keys, values, grad_out, valid, views, cross_bias):
    swap = functools.partial(
        lax.all_to_all, axis_name="heads", split_axis=0, concat_axis=0, tiled=True
    )
    shares = lax.axis_size("share")
    mine = swap(pack(query, keys, values, grad_out))
    others = [
        lax.ppermute(mine, "share", [((i + k) % shares, i) for i in range(shares)])
        for k in range(1, shares)
    ]
    given = attend(mine, others, valid, views, cross_bias)
    return unpack(swap(given), query.shape[0])


def solution(mesh):
    groups = mesh.shape["grp"]
    members = mesh.shape["blk"] * mesh.shape["head"]

    def run(query, keys, values, grad_out, valid, views, cross_bias):
        heads = query.shape[1] // HD
        layout = Mesh(
            mesh.devices.reshape(groups, heads, members // heads), ("grp", "heads", "share")
        )
        tokens = P(("grp", "heads", "share"), None)
        return jax.shard_map(
            local,
            mesh=layout,
            in_specs=(tokens,) * 4 + (P("grp"), P("grp"), P()),
            out_specs=(tokens,) * 3,
            check_vma=False,
        )(query, keys, values, grad_out, valid, views, cross_bias)

    return run
```
